256 devices in a mesh: gx: 16 (over x, y), gz: 8 (over z), gy: 2 (over core).
Axes of the slice: x: 4, y: 4, z: 8, core: 2. Of those that a mesh axis runs over, the one named last changes fastest.
Arguments:
- source: float32 [2, 384, 192, 256], P(None, 'gx', 'gz', 'gy'), may hold values from -12 to 20
- iterate: float32 [2, 384, 192, 256], P(None, 'gx', 'gz', 'gy'), may hold values from -3 to 5
- wave_sq: float32 [384, 192, 256], P('gx', 'gz', 'gy'), may hold values from 0.3 to 1.2
- front: int32 [1], replicated, may hold values from 8 to 14
- pml_flags: int32 [16, 8], P('gx', 'gz'), may hold values from 0 to 3
Outputs:
- solution: float32 [2, 384, 192, 256], P(None, 'gx', 'gz', 'gy')
- residual: float32 [2, 384, 192, 256], P(None, 'gx', 'gz', 'gy')
- norm: float32 [1], replicated
The draws below stay inside these ranges and needn't reach their ends.
Inputs may be any that keep to these rules, and one draw needn't show every extreme that they name: Subdomains whose column and row indices sum to front[0] plus a multiple of 8 relax. `pml_flags`: bit 0 puts an absorbing layer on the subdomain's upper x side, bit 1 on its upper z side.
All inputs are finite; a program needn't handle non-finite values.
Results may differ from the reference program's by a relative error of at most 0.0001.
Values sent between devices are 32-bit elements; how exact they have to be, the bound alone decides.
No kernel may reach another device: no remote copies, remote signals or barrier semaphores. Data moves between devices by JAX's collectives and lax.ppermute only.
A program may use at most 64 MiB of HBM per device.

```python
import math
import jax
import jax.numpy as jnp
from jax import lax

CX = 24
CZ = 24
P_SIZE = 3
PML = 8
SWEEPS = 10
SUB_X = 16
SUB_Z = 8
NX = 384
NZ = 192
NY = 256


def envelope(strength):
    along_x = jnp.arange(NX, dtype=jnp.float32) / NX
    along_z = jnp.arange(NZ, dtype=jnp.float32) / NZ
    return jnp.exp(strength * (along_x[:, None, None] + along_z[None, :, None]))


def rough_field(key, strength):
    rough = jnp.clip(jax.random.normal(key, (2, NX, NZ, NY), jnp.float32), -4.0, 4.0)
    return rough * envelope(strength)


def draw_source(key, part):
    key = jax.random.fold_in(key, 11)
    return rough_field(key, 0.55)


def draw_iterate(key, part):
    key = jax.random.fold_in(key, 23)
    return 0.25 * rough_field(key, 0.55)


def set_ends(drawn, stream_key, least, high):
    spot = [jax.random.randint(jax.random.fold_in(stream_key, axis), (), 0, length) for axis, length in enumerate(drawn.shape)]
    longest = drawn.shape.index(max(drawn.shape))
    beside = spot[:longest] + [(spot[longest] + 1) % drawn.shape[longest]] + spot[longest + 1:]
    return drawn.at[tuple(spot)].set(least).at[tuple(beside)].set(high)


def levels(key, shape, shards, least, largest):
    def one(position, parts):
        heights = jax.random.uniform(jax.random.fold_in(jax.random.fold_in(key, 6), position), (parts,), jnp.float32, least / len(shards), largest / len(shards))
        return jnp.repeat(jnp.exp(heights), shape[position] // parts).reshape((-1,) + (1,) * (len(shape) - position - 1))

    factor_of = one(*shards[0])
    for cut in shards[1:]:
        factor_of = factor_of * one(*cut)
    return factor_of


def setup_inputs(seed: int = 0) -> dict:
    arg_keys = jax.random.split(jax.random.key(seed), 6)
    return {
        "source": draw_source(jax.random.fold_in(arg_keys[5], 71), 0),
        "iterate": draw_iterate(jax.random.fold_in(arg_keys[5], 71), 0),
        "wave_sq": jnp.clip(jnp.exp(math.log(1.2) - 1.3862944 * jax.random.uniform(arg_keys[2], (NX, NZ, NY), jnp.float32) ** levels(arg_keys[2], (NX, NZ, NY), ((0, 16), (1, 8), (2, 2)), -0.2, 0.2)), 0.3, 1.2),
        "front": jax.random.randint(arg_keys[3], (1,), SUB_X // 2, SUB_X // 2 + SUB_Z - 1).astype(jnp.int32),
        "pml_flags": set_ends(jax.random.randint(arg_keys[4], (SUB_X, SUB_Z), 0, 4), jax.random.fold_in(arg_keys[4], 1), 0, 3).astype(jnp.int32),
    }


OMEGA = 0.6
SIGMA = 6.0

def off_sum(padded):
    along_y = padded[..., 2:] + padded[..., :-2]
    inner_y = padded[..., 1:-1]
    along_z = inner_y[..., 2:, :] + inner_y[..., :-2, :]
    along_yz = along_y[..., 2:, :] + along_y[..., :-2, :]
    centre_y = along_y[..., 1:-1, :]
    centre = inner_y[..., 1:-1, :]
    pair_sum = centre_y + along_z
    faces = centre[..., 2:, :, :] + centre[..., :-2, :, :] + centre_y[..., 1:-1, :, :] + along_z[..., 1:-1, :, :]
    edges = pair_sum[..., 2:, :, :] + pair_sum[..., :-2, :, :] + along_yz[..., 1:-1, :, :]
    corners = along_yz[..., 2:, :, :] + along_yz[..., :-2, :, :]
    return 0.5 * faces + 0.125 * edges + 0.0625 * corners

def pad_all(values):
    return jnp.pad(values, ((0, 0), (1, 1), (1, 1), (1, 1)))

def profile(count, layers, band_depth, flag):
    places = jnp.arange(count, dtype=jnp.float32)
    ramp = jnp.maximum(places - (count - layers) + 1.0, 0.0) / layers
    own = SIGMA * ramp * ramp * flag
    return jnp.concatenate([jnp.zeros((band_depth,), jnp.float32), own])

def relax_once(current, padded, forcing, diag_real, diag_imag, active):
    stencil = off_sum(padded)
    apply_re = diag_real * current[0] - diag_imag * current[1] - stencil[0]
    apply_im = diag_real * current[1] + diag_imag * current[0] - stencil[1]
    gap_re = forcing[0] - apply_re
    gap_im = forcing[1] - apply_im
    modulus = diag_real * diag_real + diag_imag * diag_imag
    step_re = OMEGA * (gap_re * diag_real + gap_im * diag_imag) / modulus
    step_im = OMEGA * (gap_im * diag_real - gap_re * diag_imag) / modulus
    update = jnp.stack([step_re, step_im])
    return current + jnp.where(active, update, jnp.zeros_like(update))

def shift_terms(flag_bits, width_x, width_z):
    band_depth = P_SIZE + 1
    flag_x = (flag_bits % 2).astype(jnp.float32)
    flag_z = (flag_bits // 2 % 2).astype(jnp.float32)
    sigma_x = profile(width_x, PML, band_depth, flag_x)
    sigma_z = profile(width_z, PML, band_depth, flag_z)
    diag_imag = sigma_x[:, None, None] + sigma_z[None, :, None]
    keep_x = jnp.arange(width_x + band_depth) >= 1
    keep_z = jnp.arange(width_z + band_depth) >= 1
    active = keep_x[:, None, None] & keep_z[None, :, None]
    return (diag_imag, active)

def relax_block(extended, flag_bits):
    current = extended[0:2]
    forcing = extended[2:4]
    diag_real = 5.0 - extended[4]
    diag_imag, active = shift_terms(flag_bits, CX, CZ)
    for sweep_turn in range(SWEEPS):
        current = relax_once(current, pad_all(current), forcing, diag_real, diag_imag, active)
    return current[:, P_SIZE + 1:, P_SIZE + 1:, :]

def reference(source, iterate, wave_sq, front, pml_flags):
    stacked = jnp.concatenate([iterate, source, wave_sq[None]], 0)
    padded = jnp.pad(stacked, ((0, 0), (P_SIZE + 1, 0), (P_SIZE + 1, 0), (0, 0)))
    result = iterate
    zero_index = jnp.int32(0)
    for column_index in range(SUB_X):
        row = jnp.mod(front[0] - column_index, SUB_Z).astype(jnp.int32)
        start_x = jnp.int32(column_index * CX)
        start_z = (row * CZ).astype(jnp.int32)
        extended = lax.dynamic_slice(padded, (zero_index, start_x, start_z, zero_index), (5, CX + P_SIZE + 1, CZ + P_SIZE + 1, NY))
        relaxed = relax_block(extended, pml_flags[column_index, row])
        result = lax.dynamic_update_slice(result, relaxed, (zero_index, start_x, start_z, zero_index))
    padded_new = pad_all(result)
    pieces = []
    total = jnp.float32(0.0)
    for slab_index in range(SUB_X):
        low = slab_index * CX
        window = padded_new[:, low:low + CX + 2]
        own = result[:, low:low + CX]
        applied = (5.0 - wave_sq[low:low + CX]) * own - off_sum(window)
        gap = source[:, low:low + CX] - applied
        total = total + jnp.sum(gap * gap)
        pieces.append(gap)
    residual = jnp.concatenate(pieces, 1)
    norm = jnp.sqrt(total / (2 * NX * NZ * NY)).reshape(1)
    return (result, residual, norm)
```

```python
import functools

import jax
import jax.numpy as jnp
from jax import lax
from jax.experimental import pallas as pl
from jax.experimental.pallas import tpu as pltpu
from jax.sharding import PartitionSpec as P

BAND = 4
PML = 8
SWEEPS = 10
OMEGA = 0.6
SIGMA = 6.0

CX = 24
CZ = 24
LANES = 128
EXT = CX + BAND
GROUP = 16
HALO = 10
STRIDE = 4
BATCH = 4
PER = EXT // STRIDE

VMEM_LIMIT = 40 * 1024 * 1024

SMEM = pl.BlockSpec(memory_space=pltpu.SMEM)
VMEM = pl.BlockSpec(memory_space=pltpu.VMEM)


def lane_ids():
    return lax.broadcasted_iota(jnp.int32, (8, LANES), 1)


def row_ids():
    return lax.broadcasted_iota(jnp.int32, (8, LANES), 0)


def roll(value, shift):
    if isinstance(shift, int):
        shift = shift % LANES
        if shift == 0:
            return value
    return pltpu.roll(value, shift, 1)


def pair_sum(value):
    return roll(value, 1) + roll(value, -1)


def stencil_parts(centre, across, z_centre, z_across):
    both = across + z_centre
    part = 0.25 * z_across
    near = both + part
    return centre + 0.25 * (near + part), near


def tile_of(fields, bands, corner_tiles, field, plane, tile):
    if tile == 0:
        return corner_tiles[field, plane]
    rows = pl.ds(8 * (tile - 1), 8)
    if plane < BAND:
        return bands[field, plane, rows, :]
    ref, index = fields[field]
    x = plane - BAND
    return ref[x, rows, :] if index is None else ref[index, x, rows, :]


def fill_low_tiles(low, z_band, corner, keep_x, keep_z):
    keep_both = keep_x * keep_z
    low[...] = jnp.zeros_like(low)
    for field in range(5):
        for plane in range(EXT):
            if plane < BAND:
                low[field, plane, pl.ds(4, 4), :] = corner[field, plane] * keep_both
            else:
                low[field, plane, pl.ds(4, 4), :] = z_band[field, plane - BAND] * keep_z


def halo_kernel(info, keep, iterate, source, wave, x_band, z_band, corner, out, low):
    half = info[0]
    active = info[1]

    @pl.when(active == 1)
    def _():
        keep_x = keep[0]
        fill_low_tiles(low, z_band, corner, keep_x, keep[1])
        fields = [(iterate, 0), (iterate, 1), (source, 0), (source, 1), (wave, None)]
        lanes = lane_ids()
        place = lanes % GROUP
        least = (GROUP - HALO) * (1 - half)
        wanted = (place >= least) & (place < least + HALO)
        masks = [wanted & (lanes // GROUP == j) for j in range(PER)]
        for field in range(5):
            for start in range(STRIDE):
                for tile in range(4):
                    packed = jnp.zeros((8, LANES), jnp.float32)
                    for j in range(PER):
                        plane = STRIDE * j + start
                        value = tile_of(fields, x_band, low, field, plane, tile)
                        if plane < BAND and tile > 0:
                            value = value * keep_x
                        turned = pltpu.roll(value, GROUP * (j + 1 - half), 1)
                        packed = jnp.where(masks[j], turned, packed)
                    out[field, start, pl.ds(8 * tile, 8), :] = packed

    @pl.when(active == 0)
    def _():
        out[...] = jnp.zeros_like(out)


def relax_kernel(
    info, keep, iterate, source, wave, x_band, z_band, corner, halo, out,
    low, w, w_next, e_re, e_im, f_re, f_im, h, h_next, he_re, he_im, hf_re, hf_im, hq, hr, hs, mq, mr,
):
    half = info[0]
    active = info[1]

    @pl.when(active == 0)
    def _():
        out[...] = iterate[...]

    @pl.when(active == 1)
    def _():
        keep_x = keep[0]
        flag_x = keep[2]
        flag_z = keep[3]
        fill_low_tiles(low, z_band, corner, keep_x, keep[1])
        fields = [(iterate, 0), (iterate, 1), (source, 0), (source, 1), (wave, None)]
        lanes = lane_ids()
        rows = row_ids()
        place = lanes % GROUP
        group = lanes // GROUP
        least = (GROUP - HALO) * half
        zeros = jnp.zeros((8, LANES), jnp.float32)

        for scratch in (w, w_next, h, h_next):
            scratch[...] = jnp.zeros_like(scratch)

        def coefficients(wave_sq, s_re, s_im, sigma):
            diag = 5.0 - wave_sq
            scale = (0.5 * OMEGA) / (diag * diag + sigma * sigma)
            er = diag * scale
            ei = -sigma * scale
            return er, ei, 2.0 * (er * s_re - ei * s_im), 2.0 * (er * s_im + ei * s_re)

        def sigma_z(tile):
            if tile == 0:
                return zeros
            z = (rows + 8 * (tile - 1)).astype(jnp.float32)
            ramp = jnp.maximum(z - (CZ - PML) + 1.0, 0.0) / PML
            return SIGMA * ramp * ramp * flag_z

        for tile in range(4):
            along_z = sigma_z(tile)
            kept_rows = rows < 5
            for plane in range(EXT):
                values = [tile_of(fields, x_band, low, f, plane, tile) for f in range(5)]
                if plane < BAND and tile > 0:
                    values = [value * keep_x for value in values]
                w_re, w_im, s_re, s_im, wave_sq = values
                at = pl.ds(8 * tile, 8)
                w[0, plane + 1, pl.ds(8 + 8 * tile, 8), :] = w_re
                w[1, plane + 1, pl.ds(8 + 8 * tile, 8), :] = w_im
                if plane == 0:
                    er, ei, fr, fi = zeros, zeros, OMEGA * w_re, OMEGA * w_im
                else:
                    ramp = max(plane - BAND - (CX - PML) + 1.0, 0.0) / PML
                    sigma = along_z + SIGMA * ramp * ramp * flag_x
                    er, ei, fr, fi = coefficients(wave_sq, s_re, s_im, sigma)
                    if tile == 0:
                        er = jnp.where(kept_rows, 0.0, er)
                        ei = jnp.where(kept_rows, 0.0, ei)
                        fr = jnp.where(kept_rows, OMEGA * w_re, fr)
                        fi = jnp.where(kept_rows, OMEGA * w_im, fi)
                e_re[plane, at, :] = er
                e_im[plane, at, :] = ei
                f_re[plane, at, :] = fr
                f_im[plane, at, :] = fi

            for start in range(STRIDE):
                at = pl.ds(8 * tile, 8)
                w_re, w_im, s_re, s_im, wave_sq = [halo[f, start, at, :] for f in range(5)]
                h[0, start, pl.ds(8 + 8 * tile, 8), :] = w_re
                h[1, start, pl.ds(8 + 8 * tile, 8), :] = w_im
                x = (STRIDE * group + start - BAND).astype(jnp.float32)
                ramp = jnp.maximum(x - (CX - PML) + 1.0, 0.0) / PML
                sigma = along_z + SIGMA * ramp * ramp * flag_x
                er, ei, fr, fi = coefficients(wave_sq, s_re, s_im, sigma)
                kept = (place < least) | (place >= least + HALO) | (group == PER)
                if start == 0:
                    kept = kept | (group == 0)
                if tile == 0:
                    kept = kept | kept_rows
                he_re[start, at, :] = jnp.where(kept, 0.0, er)
                he_im[start, at, :] = jnp.where(kept, 0.0, ei)
                hf_re[start, at, :] = jnp.where(kept, OMEGA * w_re, fr)
                hf_im[start, at, :] = jnp.where(kept, OMEGA * w_im, fi)

        first_lane = lanes == 0
        last_lane = lanes == LANES - 1
        turns = [GROUP * (j + half) for j in range(PER)]
        joined = place == (GROUP - 1) * half
        to_edge = jnp.where(half == 0, LANES - 1, 1)
        back_turns = [lax.rem(LANES - turn + to_edge, LANES) for turn in turns]
        taken = [
            lanes == lax.rem(turn + jnp.where(half == 0, LANES - 1, 0), LANES) for turn in turns
        ]

        def updated(w_re, w_im, t_re, t_im, er, ei, fr, fi):
            new_re = (1.0 - OMEGA) * w_re + fr + (er * t_re - ei * t_im)
            new_im = (1.0 - OMEGA) * w_im + fi + (er * t_im + ei * t_re)
            return new_re, new_im

        def sweep(w, h, w_out, h_out):
            def centre_and_z(ref, part, plane, tile):
                base = 8 + 8 * tile
                return ref[part, plane, pl.ds(base, 8), :], (
                    ref[part, plane, pl.ds(base - 1, 8), :]
                    + ref[part, plane, pl.ds(base + 1, 8), :]
                )

            for tile in range(4):
                at = pl.ds(8 * tile, 8)
                for part in range(2):
                    both = [centre_and_z(h, part, s, tile) for s in range(STRIDE)]
                    below = [roll(value, GROUP) for value in both[-1]]
                    above = [roll(value, -GROUP) for value in both[0]]
                    both = [below] + both + [above]
                    for s in range(STRIDE):
                        q, near = stencil_parts(
                            both[s + 1][0], both[s][0] + both[s + 2][0],
                            both[s + 1][1], both[s][1] + both[s + 2][1],
                        )
                        hq[part, s, at, :] = q
                        hs[part, s, at, :] = jnp.where(joined, q, 0.0)
                        hr[part, s, at, :] = near

            for tile in range(4):
                at = pl.ds(8 * tile, 8)
                for part in range(2):
                    before, here = (zeros, zeros), centre_and_z(w, part, 1, tile)
                    for plane in range(EXT):
                        after = (zeros, zeros)
                        if plane + 1 < EXT:
                            after = centre_and_z(w, part, plane + 2, tile)
                        q, near = stencil_parts(
                            here[0], before[0] + after[0], here[1], before[1] + after[1]
                        )
                        mq[part, plane, at, :] = q
                        mr[part, plane, at, :] = near
                        before, here = here, after

            for tile in range(4):
                at = pl.ds(8 * tile, 8)
                base = 8 + 8 * tile
                for first in range(0, EXT, BATCH):
                    planes = range(first, first + BATCH)
                    q = [[mq[part, plane, at, :] for part in range(2)] for plane in planes]
                    up = [[roll(value, -1) for value in pair] for pair in q]
                    down = [[roll(value, 1) for value in pair] for pair in q]
                    side = [
                        [
                            pltpu.roll(hs[part, plane % STRIDE, at, :], back_turns[plane // STRIDE], 1)
                            for part in range(2)
                        ]
                        for plane in planes
                    ]
                    for n, plane in enumerate(planes):
                        total = [
                            jnp.where(last_lane, side[n][part], up[n][part])
                            + jnp.where(first_lane, side[n][part], down[n][part])
                            + mr[part, plane, at, :]
                            for part in range(2)
                        ]
                        new_re, new_im = updated(
                            w[0, plane + 1, pl.ds(base, 8), :], w[1, plane + 1, pl.ds(base, 8), :],
                            total[0], total[1],
                            e_re[plane, at, :], e_im[plane, at, :],
                            f_re[plane, at, :], f_im[plane, at, :],
                        )
                        w_out[0, plane + 1, pl.ds(base, 8), :] = new_re
                        w_out[1, plane + 1, pl.ds(base, 8), :] = new_im

            for tile in range(4):
                at = pl.ds(8 * tile, 8)
                base = 8 + 8 * tile
                for start in range(STRIDE):
                    total = []
                    for part in range(2):
                        turned = [
                            pltpu.roll(mq[part, STRIDE * j + start, at, :], turns[j], 1)
                            for j in range(PER)
                        ]
                        q = hq[part, start, at, :]
                        for j in range(PER):
                            q = jnp.where(taken[j], turned[j], q)
                        total.append(pair_sum(q) + hr[part, start, at, :])
                    new_re, new_im = updated(
                        h[0, start, pl.ds(base, 8), :], h[1, start, pl.ds(base, 8), :],
                        total[0], total[1],
                        he_re[start, at, :], he_im[start, at, :],
                        hf_re[start, at, :], hf_im[start, at, :],
                    )
                    h_out[0, start, pl.ds(base, 8), :] = new_re
                    h_out[1, start, pl.ds(base, 8), :] = new_im

        def two_sweeps(turn, carry):
            sweep(w, h, w_next, h_next)
            sweep(w_next, h_next, w, h)
            return carry

        lax.fori_loop(0, SWEEPS // 2, two_sweeps, 0)
        for part in range(2):
            for x in range(CX):
                out[part, x] = w[part, x + BAND + 1, pl.ds(16, CZ), :]


def fill_box(box, field, x_low, x_high, z_low, z_high, keep):
    for part in range(2):
        box[part, 0, pl.ds(8, CZ), :] = x_low[part] * keep[0]
        box[part, CX + 1, pl.ds(8, CZ), :] = x_high[part] * keep[1]
        for x in range(CX):
            box[part, x + 1, pl.ds(8, CZ), :] = field[part, x]
        for x in range(CX + 2):
            box[part, x, pl.ds(0, 8), :] = jnp.zeros((8, LANES), jnp.float32)
            box[part, x, pl.ds(8 + CZ, 8), :] = jnp.zeros((8, LANES), jnp.float32)
            side = 1.0 if 0 < x <= CX else keep[0 if x == 0 else 1]
            low_scale, high_scale = keep[2] * side, keep[3] * side
            box[part, x, pl.ds(7, 1), :] = z_low[part, pl.ds(x, 1), :] * low_scale
            box[part, x, pl.ds(8 + CZ, 1), :] = z_high[part, pl.ds(x, 1), :] * high_scale


def side_kernel(info, keep, field, x_low, x_high, z_low, z_high, out, box):
    half = info[0]
    fill_box(box, field, x_low, x_high, z_low, z_high, keep)
    lanes = lane_ids()
    edge = jnp.where(half == 0, LANES - 1, 0)
    for part in range(2):
        for tile in range(5):
            packed = jnp.zeros((8, LANES), jnp.float32)
            for x in range(CX + 2):
                value = box[part, x, pl.ds(8 * tile, 8), :]
                turned = pltpu.roll(value, lax.rem(x + LANES - edge, LANES), 1)
                packed = jnp.where(lanes == x, turned, packed)
            out[part, pl.ds(8 * tile, 8), :] = packed


def residual_kernel(
    info, keep, field, source, wave, x_low, x_high, z_low, z_high, side, out, total, box, sides
):
    half = info[0]
    fill_box(box, field, x_low, x_high, z_low, z_high, keep)
    lanes = lane_ids()
    zeros = jnp.zeros((8, LANES), jnp.float32)
    first_lane = lanes == 0
    last_lane = lanes == LANES - 1
    open_lane = lanes == jnp.where(half == 0, 0, LANES - 1)
    squares = zeros
    for part in range(2):
        for tile in range(1, 4):
            base = 8 * tile
            c = side[part, pl.ds(base, 8), :]
            zc = side[part, pl.ds(base - 1, 8), :] + side[part, pl.ds(base + 1, 8), :]
            side_q, _ = stencil_parts(c, pair_sum(c), zc, pair_sum(zc))

            def load(plane):
                c = box[part, plane, pl.ds(base, 8), :]
                zc = (
                    box[part, plane, pl.ds(base - 1, 8), :]
                    + box[part, plane, pl.ds(base + 1, 8), :]
                )
                return c, zc

            before, here = load(0), load(1)
            at = pl.ds(base - 8, 8)
            for x in range(CX):
                after = load(x + 2)
                q, near = stencil_parts(
                    here[0], before[0] + after[0], here[1], before[1] + after[1]
                )
                shift = lax.rem(2 * LANES - (x + 1) - half, LANES)
                beyond = jnp.where(open_lane, pltpu.roll(side_q, shift, 1), 0.0)
                up = roll(jnp.where(first_lane, beyond, q), -1)
                down = roll(jnp.where(last_lane, beyond, q), 1)
                gap = (
                    source[part, x, at, :]
                    - (5.0 - wave[x, at, :]) * here[0]
                    + 0.5 * (up + down + near)
                )
                out[part, x, at, :] = gap
                squares = squares + gap * gap
                before, here = here, after
    total[...] = jnp.broadcast_to(jnp.sum(squares), total.shape)


def params():
    return pltpu.CompilerParams(vmem_limit_bytes=VMEM_LIMIT)


def f32(*shape):
    return jax.ShapeDtypeStruct(shape, jnp.float32)


def ring(value, axis, by):
    size = lax.axis_size(axis)
    return lax.ppermute(value, axis, [(i, (i + by) % size) for i in range(size)])


def diagonal(value, by_x, by_z):
    size_x, size_z = lax.axis_size("gx"), lax.axis_size("gz")
    pairs = [
        (x * size_z + z, ((x + by_x) % size_x) * size_z + (z + by_z) % size_z)
        for x in range(size_x)
        for z in range(size_z)
    ]
    return lax.ppermute(value, ("gx", "gz"), pairs)


def swap(value):
    return lax.ppermute(value, "gy", [(0, 1), (1, 0)])


def on_device(source, iterate, wave_sq, front, pml_flags):
    size_x, size_z, size_y = lax.axis_size("gx"), lax.axis_size("gz"), lax.axis_size("gy")
    at_x, at_z, half = lax.axis_index("gx"), lax.axis_index("gz"), lax.axis_index("gy")
    active = (jnp.mod(at_x + at_z - front[0], size_z) == 0).astype(jnp.int32)
    info = jnp.stack([half.astype(jnp.int32), active])
    flag_bits = pml_flags[0, 0]
    as_float = lambda test: test.astype(jnp.float32)
    band_keep = jnp.stack(
        [
            as_float(at_x > 0),
            as_float(at_z > 0),
            as_float(flag_bits % 2),
            as_float(flag_bits // 2 % 2),
        ]
    )
    box_keep = jnp.stack(
        [
            as_float(at_x > 0),
            as_float(at_x < size_x - 1),
            as_float(at_z > 0),
            as_float(at_z < size_z - 1),
        ]
    )

    def bands(index):
        return jnp.concatenate([iterate[index], source[index], wave_sq[index[1:]][None]], 0)

    every, last = slice(None), slice(CX - BAND, CX)
    corner = diagonal(bands((every, last, last)), 1, 1)
    x_band = ring(bands((every, last, every)), "gx", 1)
    z_band = ring(bands((every, every, last)), "gz", 1)

    halo = pl.pallas_call(
        halo_kernel,
        out_shape=f32(5, STRIDE, 32, LANES),
        in_specs=[SMEM] * 2 + [VMEM] * 6,
        out_specs=VMEM,
        scratch_shapes=[pltpu.VMEM((5, EXT, 8, LANES), jnp.float32)],
        compiler_params=params(),
        name="pack_halo",
    )(info, band_keep, iterate, source, wave_sq, x_band, z_band, corner)
    halo = swap(halo)
    box_like = pltpu.VMEM((EXT, 32, LANES), jnp.float32)
    halo_like = pltpu.VMEM((STRIDE, 32, LANES), jnp.float32)
    pair_like = pltpu.VMEM((2, STRIDE, 32, LANES), jnp.float32)
    plane_pair = pltpu.VMEM((2, EXT, 32, LANES), jnp.float32)
    new = pl.pallas_call(
        relax_kernel,
        out_shape=f32(2, CX, CZ, LANES),
        in_specs=[SMEM] * 2 + [VMEM] * 7,
        out_specs=VMEM,
        scratch_shapes=[
            pltpu.VMEM((5, EXT, 8, LANES), jnp.float32),
            pltpu.VMEM((2, EXT + 2, 48, LANES), jnp.float32),
            pltpu.VMEM((2, EXT + 2, 48, LANES), jnp.float32),
            box_like, box_like, box_like, box_like,
            pltpu.VMEM((2, STRIDE, 48, LANES), jnp.float32),
            pltpu.VMEM((2, STRIDE, 48, LANES), jnp.float32),
            halo_like, halo_like, halo_like, halo_like,
            pair_like, pair_like, pair_like, plane_pair, plane_pair,
        ],
        compiler_params=params(),
        name="relax",
    )(info, band_keep, iterate, source, wave_sq, x_band, z_band, corner, halo)

    x_low = ring(new[:, CX - 1], "gx", 1)
    x_high = ring(new[:, 0], "gx", -1)

    def face(z):
        return jnp.concatenate([x_low[:, z][:, None], new[:, :, z], x_high[:, z][:, None]], 1)

    z_low = ring(face(CZ - 1), "gz", 1)
    z_high = ring(face(0), "gz", -1)
    box_scratch = pltpu.VMEM((2, CX + 2, 48, LANES), jnp.float32)
    side = pl.pallas_call(
        side_kernel,
        out_shape=f32(2, 40, LANES),
        in_specs=[SMEM] * 2 + [VMEM] * 5,
        out_specs=VMEM,
        scratch_shapes=[box_scratch],
        compiler_params=params(),
        name="y_side",
    )(info, box_keep, new, x_low, x_high, z_low, z_high)
    side = swap(side)
    count = size_x * size_z * size_y
    residual, total = pl.pallas_call(
        residual_kernel,
        out_shape=(f32(2, CX, CZ, LANES), f32(count, LANES)),
        in_specs=[SMEM] * 2 + [VMEM] * 8,
        out_specs=(VMEM, VMEM),
        scratch_shapes=[box_scratch, pltpu.VMEM((2, 40, LANES), jnp.float32)],
        compiler_params=params(),
        name="residual",
    )(info, box_keep, new, source, wave_sq, x_low, x_high, z_low, z_high, side)
    parts = lax.all_to_all(total, ("gx", "gz", "gy"), 0, 0, tiled=True)
    cells = 2 * CX * CZ * LANES * count
    norm = jnp.sqrt(jnp.sum(parts, axis=0)[:1] / cells)
    return new, residual, norm


def solution(mesh):
    in_specs = (
        P(None, "gx", "gz", "gy"),
        P(None, "gx", "gz", "gy"),
        P("gx", "gz", "gy"),
        P(),
        P("gx", "gz"),
    )
    out_specs = (P(None, "gx", "gz", "gy"), P(None, "gx", "gz", "gy"), P())
    return jax.shard_map(
        on_device, mesh=mesh, in_specs=in_specs, out_specs=out_specs, check_vma=False
    )
```

```python
import jax
import jax.numpy as jnp
from jax import lax
from jax.experimental import pallas as pl
from jax.experimental.pallas import tpu as pltpu
from jax.sharding import PartitionSpec as P

BAND = 4
PML = 8
SWEEPS = 10
OMEGA = 0.6
SIGMA = 6.0

CX = 24
CZ = 24
LANES = 128
EXT = CX + BAND
GROUP = 16
HALO = 11
STRIDE = 4
LAYERS = 2 * BAND + 3 * (BAND - 1)
PER = EXT // STRIDE

SIDE_ROW = 26

MIB = 1024 * 1024

SMEM = pl.BlockSpec(memory_space=pltpu.SMEM)
VMEM = pl.BlockSpec(memory_space=pltpu.VMEM)
HBM = pl.BlockSpec(memory_space=pltpu.HBM)


def lane_ids():
    return lax.broadcasted_iota(jnp.int32, (8, LANES), 1)


def row_ids():
    return lax.broadcasted_iota(jnp.int32, (8, LANES), 0)


def roll(value, shift):
    if isinstance(shift, int):
        shift = shift % LANES
        if shift == 0:
            return value
    return pltpu.roll(value, shift, 1)


def pair_sum(value):
    return roll(value, 1) + roll(value, -1)


def stencil_parts(centre, across, z_centre, z_across):
    both = across + z_centre
    part = 0.25 * z_across
    near = both + part
    return centre + 0.25 * (near + part), near


def layers(field):
    return 0 if field < 2 else 1


def layer_row(field, layer):
    return 4 * field + layer if field < 2 else 8 + 3 * (field - 2) + layer - 1


def bands_kernel(iterate, source, wave, x_out, z_out, corner_out, x_part, z_part, sems):
    fields = [iterate.at[0], iterate.at[1], source.at[0], source.at[1], wave]
    copies = [
        pltpu.make_async_copy(ref.at[pl.ds(CX - BAND, BAND)], x_part.at[f], sems.at[f])
        for f, ref in enumerate(fields)
    ]
    for f, ref in enumerate(fields):
        for piece in range(2):
            some = pl.ds(CX // 2 * piece, CX // 2)
            copies.append(
                pltpu.make_async_copy(
                    ref.at[some, pl.ds(CZ - 8, 8)], z_part.at[f, some], sems.at[5 + 2 * f + piece]
                )
            )
    for copy in copies:
        copy.start()
    for copy in copies:
        copy.wait()
    corner_out[...] = jnp.zeros_like(corner_out)
    for field in range(5):
        first = layers(field)
        depth = BAND - first
        for layer in range(first, BAND):
            row = layer_row(field, layer)
            x_out[row] = x_part[field, layer]
            corner_out[pl.ds(BAND * row, BAND), :] = x_part[field, layer, pl.ds(CZ - BAND, BAND), :]
        for x in range(CX):
            rows = pl.ds(LAYERS * x + layer_row(field, first), depth)
            z_out[rows, :] = z_part[field, x, pl.ds(8 - depth, depth), :]


def tile_of(fields, bands, corner_tiles, field, plane, tile, keep_x):
    if tile == 0:
        return corner_tiles[field, plane]
    rows = pl.ds(8 * (tile - 1), 8)
    if plane < BAND:
        if plane < layers(field):
            return jnp.zeros((8, LANES), jnp.float32)
        return bands[layer_row(field, plane), rows, :] * keep_x
    ref, index = fields[field]
    x = plane - BAND
    return ref[x, rows, :] if index is None else ref[index, x, rows, :]


def fill_low_tiles(low, z_band, corner, keep_x, keep_z):
    keep_both = keep_x * keep_z
    low[...] = jnp.zeros_like(low)
    for field in range(5):
        first = layers(field)
        depth = BAND - first
        for plane in range(EXT):
            to = pl.ds(8 - depth, depth)
            if plane >= BAND:
                rows = pl.ds(LAYERS * (plane - BAND) + layer_row(field, first), depth)
                low[field, plane, to, :] = z_band[rows, :] * keep_z
            elif plane >= first:
                rows = pl.ds(BAND * layer_row(field, plane) + first, depth)
                low[field, plane, to, :] = corner[rows, :] * keep_both


def halo_kernel(info, keep, iterate, source, wave, x_band, z_band, corner, out, low):
    half = info[0]
    keep_x = keep[0]
    fill_low_tiles(low, z_band, corner, keep_x, keep[1])
    fields = [(iterate, 0), (iterate, 1), (source, 0), (source, 1), (wave, None)]
    lanes = lane_ids()
    place = lanes % GROUP
    least = (GROUP - HALO) * (1 - half)
    wanted = (place >= least) & (place < least + HALO)
    masks = [wanted & (lanes // GROUP == j) for j in range(PER)]
    for field in range(5):
        for start in range(STRIDE):
            for tile in range(4):
                packed = jnp.zeros((8, LANES), jnp.float32)
                for j in range(PER):
                    value = tile_of(fields, x_band, low, field, STRIDE * j + start, tile, keep_x)
                    turned = pltpu.roll(value, GROUP * (j + 1 - half), 1)
                    packed = jnp.where(masks[j], turned, packed)
                out[field, start, pl.ds(8 * tile, 8), :] = packed


def relax_kernel(
    info, keep, iterate, source, wave, x_band, z_band, corner, halo,
    out, own, beside, x_first, x_last, z_first, z_last,
    low, w, w_next, e_re, e_im, f_re, f_im, h, h_next, he_re, he_im, hf_re, hf_im, hq, hr, hs, mq, mr,
):
    half = info[0]
    active = info[1]

    @pl.when(active == 0)
    def _():
        own[...] = iterate[...]
        beside[...] = halo[pl.ds(0, 2)]

    @pl.when(active == 1)
    def _():
        keep_x = keep[0]
        flag_x = keep[2]
        flag_z = keep[3]
        fill_low_tiles(low, z_band, corner, keep_x, keep[1])
        fields = [(iterate, 0), (iterate, 1), (source, 0), (source, 1), (wave, None)]
        lanes = lane_ids()
        rows = row_ids()
        place = lanes % GROUP
        group = lanes // GROUP
        least = (GROUP - HALO) * half
        zeros = jnp.zeros((8, LANES), jnp.float32)

        for scratch in (w, w_next, h, h_next):
            scratch[...] = jnp.zeros_like(scratch)

        def coefficients(wave_sq, s_re, s_im, sigma):
            diag = 5.0 - wave_sq
            scale = (0.5 * OMEGA) / (diag * diag + sigma * sigma)
            er = diag * scale
            ei = -sigma * scale
            return er, ei, 2.0 * (er * s_re - ei * s_im), 2.0 * (er * s_im + ei * s_re)

        def sigma_z(tile):
            if tile == 0:
                return zeros
            z = (rows + 8 * (tile - 1)).astype(jnp.float32)
            ramp = jnp.maximum(z - (CZ - PML) + 1.0, 0.0) / PML
            return SIGMA * ramp * ramp * flag_z

        for tile in range(4):
            along_z = sigma_z(tile)
            kept_rows = rows < 5
            for plane in range(EXT):
                values = [tile_of(fields, x_band, low, f, plane, tile, keep_x) for f in range(5)]
                w_re, w_im, s_re, s_im, wave_sq = values
                at = pl.ds(8 * tile, 8)
                w[0, plane + 1, pl.ds(8 + 8 * tile, 8), :] = w_re
                w[1, plane + 1, pl.ds(8 + 8 * tile, 8), :] = w_im
                if plane == 0:
                    er, ei, fr, fi = zeros, zeros, OMEGA * w_re, OMEGA * w_im
                else:
                    ramp = max(plane - BAND - (CX - PML) + 1.0, 0.0) / PML
                    sigma = along_z + SIGMA * ramp * ramp * flag_x
                    er, ei, fr, fi = coefficients(wave_sq, s_re, s_im, sigma)
                    if tile == 0:
                        er = jnp.where(kept_rows, 0.0, er)
                        ei = jnp.where(kept_rows, 0.0, ei)
                        fr = jnp.where(kept_rows, OMEGA * w_re, fr)
                        fi = jnp.where(kept_rows, OMEGA * w_im, fi)
                e_re[plane, at, :] = er
                e_im[plane, at, :] = ei
                f_re[plane, at, :] = fr
                f_im[plane, at, :] = fi

            for start in range(STRIDE):
                at = pl.ds(8 * tile, 8)
                w_re, w_im, s_re, s_im, wave_sq = [halo[f, start, at, :] for f in range(5)]
                h[0, start, pl.ds(8 + 8 * tile, 8), :] = w_re
                h[1, start, pl.ds(8 + 8 * tile, 8), :] = w_im
                x = (STRIDE * group + start - BAND).astype(jnp.float32)
                ramp = jnp.maximum(x - (CX - PML) + 1.0, 0.0) / PML
                sigma = along_z + SIGMA * ramp * ramp * flag_x
                er, ei, fr, fi = coefficients(wave_sq, s_re, s_im, sigma)
                kept = (place < least) | (place >= least + HALO) | (group == PER)
                if start == 0:
                    kept = kept | (group == 0)
                if tile == 0:
                    kept = kept | kept_rows
                he_re[start, at, :] = jnp.where(kept, 0.0, er)
                he_im[start, at, :] = jnp.where(kept, 0.0, ei)
                hf_re[start, at, :] = jnp.where(kept, OMEGA * w_re, fr)
                hf_im[start, at, :] = jnp.where(kept, OMEGA * w_im, fi)

        first_lane = lanes == 0
        last_lane = lanes == LANES - 1
        turns = [GROUP * (j + half) for j in range(PER)]
        joined = place == (GROUP - 1) * half
        to_edge = jnp.where(half == 0, LANES - 1, 1)
        back_turns = [lax.rem(LANES - turn + to_edge, LANES) for turn in turns]
        taken = [
            lanes == lax.rem(turn + jnp.where(half == 0, LANES - 1, 0), LANES) for turn in turns
        ]

        def undamped(plane, tile):
            return plane < BAND + CX - PML and tile < 3

        def updated(w_re, w_im, t_re, t_im, er, ei, fr, fi):
            new_re = (1.0 - OMEGA) * w_re + fr
            new_im = (1.0 - OMEGA) * w_im + fi
            if ei is None:
                return new_re + er * t_re, new_im + er * t_im
            return new_re + (er * t_re - ei * t_im), new_im + (er * t_im + ei * t_re)

        def sweep(w, h, w_out, h_out):
            def centre_and_z(ref, part, plane, tile):
                base = 8 + 8 * tile
                return ref[part, plane, pl.ds(base, 8), :], (
                    ref[part, plane, pl.ds(base - 1, 8), :]
                    + ref[part, plane, pl.ds(base + 1, 8), :]
                )

            for tile in range(4):
                at = pl.ds(8 * tile, 8)
                for part in range(2):
                    both = [centre_and_z(h, part, s, tile) for s in range(STRIDE)]
                    below = [roll(value, GROUP) for value in both[-1]]
                    above = [roll(value, -GROUP) for value in both[0]]
                    both = [below] + both + [above]
                    for s in range(STRIDE):
                        q, near = stencil_parts(
                            both[s + 1][0], both[s][0] + both[s + 2][0],
                            both[s + 1][1], both[s][1] + both[s + 2][1],
                        )
                        hq[part, s, at, :] = q
                        hs[part, s, at, :] = jnp.where(joined, q, 0.0)
                        hr[part, s, at, :] = near

            for tile in range(4):
                at = pl.ds(8 * tile, 8)
                for part in range(2):
                    before, here = (zeros, zeros), centre_and_z(w, part, 1, tile)
                    for plane in range(EXT):
                        after = (zeros, zeros)
                        if plane + 1 < EXT:
                            after = centre_and_z(w, part, plane + 2, tile)
                        q, near = stencil_parts(
                            here[0], before[0] + after[0], here[1], before[1] + after[1]
                        )
                        mq[part, plane, at, :] = q
                        mr[part, plane, at, :] = near
                        before, here = here, after

            for tile in range(4):
                at = pl.ds(8 * tile, 8)
                base = 8 + 8 * tile
                joint = [[hq[part, s, at, :] for s in range(STRIDE)] for part in range(2)]
                for j in range(PER):
                    planes = range(STRIDE * j, STRIDE * (j + 1))
                    q = [[mq[part, plane, at, :] for part in range(2)] for plane in planes]
                    up = [[roll(value, -1) for value in pair] for pair in q]
                    down = [[roll(value, 1) for value in pair] for pair in q]
                    side = [
                        [
                            pltpu.roll(hs[part, s, at, :], back_turns[j], 1)
                            for part in range(2)
                        ]
                        for s in range(STRIDE)
                    ]
                    turned = [[pltpu.roll(value, turns[j], 1) for value in pair] for pair in q]
                    for n, plane in enumerate(planes):
                        total = [
                            jnp.where(last_lane, side[n][part], up[n][part])
                            + jnp.where(first_lane, side[n][part], down[n][part])
                            + mr[part, plane, at, :]
                            for part in range(2)
                        ]
                        for part in range(2):
                            joint[part][n] = jnp.where(taken[j], turned[n][part], joint[part][n])
                        new_re, new_im = updated(
                            w[0, plane + 1, pl.ds(base, 8), :], w[1, plane + 1, pl.ds(base, 8), :],
                            total[0], total[1],
                            e_re[plane, at, :], None if undamped(plane, tile) else e_im[plane, at, :],
                            f_re[plane, at, :], f_im[plane, at, :],
                        )
                        w_out[0, plane + 1, pl.ds(base, 8), :] = new_re
                        w_out[1, plane + 1, pl.ds(base, 8), :] = new_im

                for part in range(2):
                    for s in range(STRIDE):
                        hq[part, s, at, :] = joint[part][s]

            for tile in range(4):
                at = pl.ds(8 * tile, 8)
                base = 8 + 8 * tile
                total = [
                    [pair_sum(hq[part, s, at, :]) + hr[part, s, at, :] for part in range(2)]
                    for s in range(STRIDE)
                ]
                for s in range(STRIDE):
                    new_re, new_im = updated(
                        h[0, s, pl.ds(base, 8), :], h[1, s, pl.ds(base, 8), :],
                        total[s][0], total[s][1],
                        he_re[s, at, :], he_im[s, at, :],
                        hf_re[s, at, :], hf_im[s, at, :],
                    )
                    h_out[0, s, pl.ds(base, 8), :] = new_re
                    h_out[1, s, pl.ds(base, 8), :] = new_im

        def two_sweeps(turn, carry):
            sweep(w, h, w_next, h_next)
            sweep(w_next, h_next, w, h)
            return carry

        lax.fori_loop(0, SWEEPS // 2, two_sweeps, 0)
        for part in range(2):
            for x in range(CX):
                own[part, x] = w[part, x + BAND + 1, pl.ds(16, CZ), :]
            for s in range(STRIDE):
                beside[part, s] = h[part, s, pl.ds(8, 32), :]

    out[...] = own[...]
    for part in range(2):
        x_first[part, 0] = own[part, 0]
        x_first[part, 1] = beside[part, 0, pl.ds(8, CZ), :]
        x_last[part, 0] = own[part, CX - 1]
        x_last[part, 1] = beside[part, (CX - 1) % STRIDE, pl.ds(8, CZ), :]
        for face, z in ((z_first, 0), (z_last, CZ - 1)):
            face[part, pl.ds(24, 8), :] = jnp.zeros((8, LANES), jnp.float32)
            for x in range(CX):
                face[part, pl.ds(x + 1, 1), :] = own[part, x, pl.ds(z, 1), :]
            for s in range(STRIDE):
                face[part, pl.ds(SIDE_ROW + s, 1), :] = beside[part, s, pl.ds(8 + z, 1), :]


def face_kernel(keep, z_first, z_last, x_low, x_high, first_out, last_out):
    group = lax.broadcasted_iota(jnp.int32, (1, LANES), 1) // GROUP
    for face, out, z in ((z_first, first_out, 0), (z_last, last_out, CZ - 1)):
        out[...] = face[...]
        for part in range(2):
            row = pl.ds(z, 1)
            out[part, pl.ds(0, 1), :] = x_low[part, 0, row, :] * keep[0]
            out[part, pl.ds(CX + 1, 1), :] = x_high[part, 0, row, :] * keep[1]
            for s, ref, scale in ((STRIDE - 1, x_low, keep[0]), (0, x_high, keep[1])):
                at = pl.ds(SIDE_ROW + s, 1)
                to, turn = (0, -6 * GROUP) if s else (7, 6 * GROUP)
                out[part, at, :] = jnp.where(
                    group == to, roll(ref[part, 1, row, :] * scale, turn), face[part, at, :]
                )


def residual_kernel(
    info, keep, field, source, wave, beside, x_low, x_high, z_low, z_high,
    out, total, box, sides, mq, mr, hs,
):
    half = info[0]
    lanes = lane_ids()
    group = lanes // GROUP
    zeros = jnp.zeros((8, LANES), jnp.float32)
    for part in range(2):
        box[part, 0, pl.ds(8, CZ), :] = x_low[part, 0] * keep[0]
        box[part, CX + 1, pl.ds(8, CZ), :] = x_high[part, 0] * keep[1]
        for x in range(CX):
            box[part, x + 1, pl.ds(8, CZ), :] = field[part, x]
        for x in range(CX + 2):
            box[part, x, pl.ds(7, 1), :] = z_low[part, pl.ds(x, 1), :] * keep[2]
            box[part, x, pl.ds(8 + CZ, 1), :] = z_high[part, pl.ds(x, 1), :] * keep[3]
        for s in range(STRIDE):
            row = pl.ds(SIDE_ROW + s, 1)
            sides[part, s, pl.ds(7, 1), :] = z_low[part, row, :] * keep[2]
            sides[part, s, pl.ds(8 + CZ, 1), :] = z_high[part, row, :] * keep[3]
            for tile in range(3):
                value = beside[part, s, pl.ds(8 + 8 * tile, 8), :]
                rows = pl.ds(8 * tile, 8)
                if s == STRIDE - 1:
                    value = jnp.where(
                        group == 0, roll(x_low[part, 1, rows, :] * keep[0], -6 * GROUP), value
                    )
                if s == 0:
                    value = jnp.where(
                        group == 7, roll(x_high[part, 1, rows, :] * keep[1], 6 * GROUP), value
                    )
                sides[part, s, pl.ds(8 + 8 * tile, 8), :] = value

    def centre_and_z(ref, part, plane, tile):
        base = 8 + 8 * tile
        return ref[part, plane, pl.ds(base, 8), :], (
            ref[part, plane, pl.ds(base - 1, 8), :] + ref[part, plane, pl.ds(base + 1, 8), :]
        )

    joined = lanes % GROUP == (GROUP - 1) * half
    for part in range(2):
        for tile in range(3):
            at = pl.ds(8 * tile, 8)
            both = [centre_and_z(sides, part, s, tile) for s in range(STRIDE)]
            below = [roll(value, GROUP) for value in both[-1]]
            above = [roll(value, -GROUP) for value in both[0]]
            both = [below] + both + [above]
            for s in range(STRIDE):
                q, _ = stencil_parts(
                    both[s + 1][0], both[s][0] + both[s + 2][0],
                    both[s + 1][1], both[s][1] + both[s + 2][1],
                )
                hs[part, s, at, :] = jnp.where(joined, q, 0.0)

    for part in range(2):
        for tile in range(3):
            at = pl.ds(8 * tile, 8)
            before, here = centre_and_z(box, part, 0, tile), centre_and_z(box, part, 1, tile)
            for x in range(CX):
                after = centre_and_z(box, part, x + 2, tile)
                q, near = stencil_parts(
                    here[0], before[0] + after[0], here[1], before[1] + after[1]
                )
                mq[part, x, at, :] = q
                mr[part, x, at, :] = near
                before, here = here, after

    first_lane = lanes == 0
    last_lane = lanes == LANES - 1
    to_edge = jnp.where(half == 0, LANES - 1, 1)
    squares = [zeros] * 4
    for part in range(2):
        for tile in range(3):
            at = pl.ds(8 * tile, 8)
            for j in range(1, PER):
                turn = lax.rem(LANES - GROUP * (j + half) + to_edge, LANES)
                planes = range(STRIDE * (j - 1), STRIDE * j)
                q = [mq[part, x, at, :] for x in planes]
                up = [roll(value, -1) for value in q]
                down = [roll(value, 1) for value in q]
                side = [pltpu.roll(hs[part, s, at, :], turn, 1) for s in range(STRIDE)]
                for n, x in enumerate(planes):
                    y = jnp.where(last_lane, side[n], up[n]) + jnp.where(
                        first_lane, side[n], down[n]
                    )
                    gap = (
                        source[part, x, at, :]
                        - (5.0 - wave[x, at, :]) * field[part, x, at, :]
                        + 0.5 * (y + mr[part, x, at, :])
                    )
                    out[part, x, at, :] = gap
                    squares[n] = squares[n] + gap * gap
    total[...] = jnp.broadcast_to(jnp.sum(sum(squares[1:], squares[0])), total.shape)


def f32(*shape):
    return jax.ShapeDtypeStruct(shape, jnp.float32)


def ring(value, axis, by):
    size = lax.axis_size(axis)
    return lax.ppermute(value, axis, [(i, (i + by) % size) for i in range(size)])


def diagonal(value, by_x, by_z):
    size_x, size_z = lax.axis_size("gx"), lax.axis_size("gz")
    pairs = [
        (x * size_z + z, ((x + by_x) % size_x) * size_z + (z + by_z) % size_z)
        for x in range(size_x)
        for z in range(size_z)
    ]
    return lax.ppermute(value, ("gx", "gz"), pairs)


def swap(value):
    return lax.ppermute(value, "gy", [(0, 1), (1, 0)])


def on_device(source, iterate, wave_sq, front, pml_flags):
    size_x, size_z, size_y = lax.axis_size("gx"), lax.axis_size("gz"), lax.axis_size("gy")
    at_x, at_z, half = lax.axis_index("gx"), lax.axis_index("gz"), lax.axis_index("gy")
    active = (jnp.mod(at_x + at_z - front[0], size_z) == 0).astype(jnp.int32)
    info = jnp.stack([half.astype(jnp.int32), active])
    flag_bits = pml_flags[0, 0]
    as_float = lambda test: test.astype(jnp.float32)
    band_keep = jnp.stack(
        [
            as_float(at_x > 0),
            as_float(at_z > 0),
            as_float(flag_bits % 2),
            as_float(flag_bits // 2 % 2),
        ]
    )
    box_keep = jnp.stack(
        [
            as_float(at_x > 0),
            as_float(at_x < size_x - 1),
            as_float(at_z > 0),
            as_float(at_z < size_z - 1),
        ]
    )

    def call(kernel, outs, ins, name, scratch=(), place=VMEM, sems=0, limit=20 * MIB):
        scalars = sum(value.ndim == 1 for value in ins)
        return pl.pallas_call(
            kernel,
            out_shape=outs,
            in_specs=[SMEM] * scalars + [place] * (len(ins) - scalars),
            out_specs=jax.tree.map(lambda _: VMEM, outs),
            scratch_shapes=[pltpu.VMEM(shape, jnp.float32) for shape in scratch]
            + [pltpu.SemaphoreType.DMA((sems,))] * (sems > 0),
            compiler_params=pltpu.CompilerParams(vmem_limit_bytes=limit),
            name=name,
        )(*ins)

    x_band, z_band, corner = call(
        bands_kernel,
        (f32(LAYERS, CZ, LANES), f32(LAYERS * CX, LANES), f32(72, LANES)),
        (iterate, source, wave_sq),
        "bands",
        [(5, BAND, CZ, LANES), (5, CX, 8, LANES)],
        place=HBM,
        sems=15,
        limit=60 * MIB,
    )
    corner = diagonal(corner, 1, 1)
    x_band = ring(x_band, "gx", 1)
    z_band = ring(z_band, "gz", 1)
    low_tiles = (5, EXT, 8, LANES)
    halo = call(
        halo_kernel,
        f32(5, STRIDE, 32, LANES),
        (info, band_keep, iterate, source, wave_sq, x_band, z_band, corner),
        "pack_halo",
        [low_tiles],
    )
    halo = swap(halo)
    planes, packs = (EXT, 32, LANES), (STRIDE, 32, LANES)
    own = (2, CX, CZ, LANES)
    box_like, pack_like = (2, EXT + 2, 48, LANES), (2, STRIDE, 48, LANES)
    x_face, z_face = f32(2, 2, CZ, LANES), f32(2, 32, LANES)
    new, field, beside, x_first, x_last, z_first, z_last = call(
        relax_kernel,
        (f32(*own), f32(*own), f32(2, STRIDE, 32, LANES), x_face, x_face, z_face, z_face),
        (info, band_keep, iterate, source, wave_sq, x_band, z_band, corner, halo),
        "relax",
        [low_tiles, box_like, box_like]
        + [planes] * 4
        + [pack_like] * 2
        + [packs] * 4
        + [(2,) + packs] * 3
        + [(2,) + planes] * 2,
    )
    x_low = ring(x_last, "gx", 1)
    x_high = ring(x_first, "gx", -1)
    z_first, z_last = call(
        face_kernel, (z_face, z_face), (box_keep, z_first, z_last, x_low, x_high), "faces"
    )
    z_low = ring(z_last, "gz", 1)
    z_high = ring(z_first, "gz", -1)
    count = size_x * size_z * size_y
    residual, total = call(
        residual_kernel,
        (f32(*own), f32(count, LANES)),
        (info, box_keep, field, source, wave_sq, beside, x_low, x_high, z_low, z_high),
        "residual",
        [(2, CX + 2, 48, LANES), (2, STRIDE, 48, LANES), own, own, (2, STRIDE, CZ, LANES)],
    )
    parts = lax.all_to_all(total, ("gx", "gz", "gy"), 0, 0, tiled=True)
    cells = 2 * CX * CZ * LANES * count
    norm = jnp.sqrt(jnp.sum(parts, axis=0)[:1] / cells)
    return new, residual, norm


def solution(mesh):
    in_specs = (
        P(None, "gx", "gz", "gy"),
        P(None, "gx", "gz", "gy"),
        P("gx", "gz", "gy"),
        P(),
        P("gx", "gz"),
    )
    out_specs = (P(None, "gx", "gz", "gy"), P(None, "gx", "gz", "gy"), P())
    return jax.shard_map(
        on_device, mesh=mesh, in_specs=in_specs, out_specs=out_specs, check_vma=False
    )
```

```python
import jax
import jax.numpy as jnp
from jax import lax
from jax.experimental import pallas as pl
from jax.experimental.pallas import tpu as pltpu
from jax.sharding import PartitionSpec as P

BAND = 4
PML = 8
SWEEPS = 10
OMEGA = 0.6
SIGMA = 6.0

CX = 24
CZ = 24
LANES = 128
EXT = CX + BAND
GROUP = 16
HALO = 11
STRIDE = 4
MOVERS = (EXT // STRIDE + 1) // 2
LAYERS = 2 * BAND + 3 * (BAND - 1)
PER = EXT // STRIDE

SIDE_ROW = 26

MIB = 1024 * 1024

SMEM = pl.BlockSpec(memory_space=pltpu.SMEM)
VMEM = pl.BlockSpec(memory_space=pltpu.VMEM)
HBM = pl.BlockSpec(memory_space=pltpu.HBM)


def lane_ids():
    return lax.broadcasted_iota(jnp.int32, (8, LANES), 1)


def row_ids():
    return lax.broadcasted_iota(jnp.int32, (8, LANES), 0)


def roll(value, shift):
    if isinstance(shift, int):
        shift = shift % LANES
        if shift == 0:
            return value
    return pltpu.roll(value, shift, 1)


def pair_sum(value):
    return roll(value, 1) + roll(value, -1)


def stencil_parts(centre, across, z_centre, z_across):
    both = across + z_centre
    part = 0.25 * z_across
    near = both + part
    return centre + 0.25 * (near + part), near


def layers(field):
    return 0 if field < 2 else 1


def layer_row(field, layer):
    return 4 * field + layer if field < 2 else 8 + 3 * (field - 2) + layer - 1


def bands_kernel(iterate, source, wave, x_out, z_out, corner_out, x_part, z_part, sems):
    fields = [iterate.at[0], iterate.at[1], source.at[0], source.at[1], wave]
    copies = [
        pltpu.make_async_copy(ref.at[pl.ds(CX - BAND, BAND)], x_part.at[f], sems.at[f])
        for f, ref in enumerate(fields)
    ]
    for f, ref in enumerate(fields):
        for piece in range(2):
            some = pl.ds(CX // 2 * piece, CX // 2)
            copies.append(
                pltpu.make_async_copy(
                    ref.at[some, pl.ds(CZ - 8, 8)], z_part.at[f, some], sems.at[5 + 2 * f + piece]
                )
            )
    for copy in copies:
        copy.start()
    for copy in copies:
        copy.wait()
    corner_out[...] = jnp.zeros_like(corner_out)
    for field in range(5):
        first = layers(field)
        depth = BAND - first
        for layer in range(first, BAND):
            row = layer_row(field, layer)
            x_out[row] = x_part[field, layer]
            corner_out[pl.ds(BAND * row, BAND), :] = x_part[field, layer, pl.ds(CZ - BAND, BAND), :]
        for x in range(CX):
            rows = pl.ds(LAYERS * x + layer_row(field, first), depth)
            z_out[rows, :] = z_part[field, x, pl.ds(8 - depth, depth), :]


def tile_of(fields, bands, corner_tiles, field, plane, tile, keep_x):
    if tile == 0:
        return corner_tiles[field, plane]
    rows = pl.ds(8 * (tile - 1), 8)
    if plane < BAND:
        if plane < layers(field):
            return jnp.zeros((8, LANES), jnp.float32)
        return bands[layer_row(field, plane), rows, :] * keep_x
    ref, index = fields[field]
    x = plane - BAND
    return ref[x, rows, :] if index is None else ref[index, x, rows, :]


def fill_low_tiles(low, z_band, corner, keep_x, keep_z, count=5):
    keep_both = keep_x * keep_z
    low[...] = jnp.zeros_like(low)
    for field in range(count):
        first = layers(field)
        depth = BAND - first
        for plane in range(EXT):
            to = pl.ds(8 - depth, depth)
            if plane >= BAND:
                rows = pl.ds(LAYERS * (plane - BAND) + layer_row(field, first), depth)
                low[field, plane, to, :] = z_band[rows, :] * keep_z
            elif plane >= first:
                rows = pl.ds(BAND * layer_row(field, plane) + first, depth)
                low[field, plane, to, :] = corner[rows, :] * keep_both


def halo_kernel(info, keep, iterate, source, wave, x_band, z_band, corner, out, low):
    half = info[0]
    keep_x = keep[0]
    fill_low_tiles(low, z_band, corner, keep_x, keep[1])
    fields = [(iterate, 0), (iterate, 1), (source, 0), (source, 1), (wave, None)]
    lanes = lane_ids()
    place = lanes % GROUP
    least = (GROUP - HALO) * (1 - half)
    wanted = (place >= least) & (place < least + HALO)
    masks = [wanted & (lanes // GROUP == j) for j in range(PER)]
    for field in range(5):
        for start in range(STRIDE):
            for tile in range(4):
                packed = jnp.zeros((8, LANES), jnp.float32)
                for j in range(PER):
                    value = tile_of(fields, x_band, low, field, STRIDE * j + start, tile, keep_x)
                    turned = pltpu.roll(value, GROUP * (j + 1 - half), 1)
                    packed = jnp.where(masks[j], turned, packed)
                out[field, start, pl.ds(8 * tile, 8), :] = packed


def coefficients(wave_sq, s_re, s_im, sigma):
    diag = 5.0 - wave_sq
    scale = (0.5 * OMEGA) / (diag * diag + sigma * sigma)
    er = diag * scale
    ei = -sigma * scale
    return er, ei, 2.0 * (er * s_re - ei * s_im), 2.0 * (er * s_im + ei * s_re)


def sigma_z(tile, flag):
    if tile == 0:
        return jnp.zeros((8, LANES), jnp.float32)
    z = (row_ids() + 8 * (tile - 1)).astype(jnp.float32)
    ramp = jnp.maximum(z - (CZ - PML) + 1.0, 0.0) / PML
    return SIGMA * ramp * ramp * flag


def weights_kernel(
    info, keep, iterate, source, wave, x_band, z_band, corner,
    e_re, e_im, f_re, f_im, movers, low,
):
    half = info[0]
    keep_x = keep[0]
    lane = lax.broadcasted_iota(jnp.int32, (16, 2 * LANES), 1)
    row = lax.broadcasted_iota(jnp.int32, (16, 2 * LANES), 0)
    ends = lane % LANES == (LANES - 1) * (1 - half)
    for m in range(MOVERS):
        start = GROUP * (2 * m + lane // LANES) + (GROUP - 1) * half
        for first in range(0, 2 * LANES, 16):
            hit = ends & ((row + first) % LANES == start)
            movers[m, pl.ds(first, 16), :] = hit.astype(jnp.float32).astype(jnp.bfloat16)
    fill_low_tiles(low, z_band, corner, keep_x, keep[1])
    fields = [(iterate, 0), (iterate, 1), (source, 0), (source, 1), (wave, None)]
    zeros = jnp.zeros((8, LANES), jnp.float32)
    kept_rows = row_ids() < 5
    for tile in range(4):
        along_z = sigma_z(tile, keep[3])
        at = pl.ds(8 * tile, 8)
        for plane in range(EXT):
            values = [tile_of(fields, x_band, low, f, plane, tile, keep_x) for f in range(5)]
            w_re, w_im, s_re, s_im, wave_sq = values
            if plane == 0:
                er, ei, fr, fi = zeros, zeros, OMEGA * w_re, OMEGA * w_im
            else:
                ramp = max(plane - BAND - (CX - PML) + 1.0, 0.0) / PML
                sigma = along_z + SIGMA * ramp * ramp * keep[2]
                er, ei, fr, fi = coefficients(wave_sq, s_re, s_im, sigma)
                if tile == 0:
                    er = jnp.where(kept_rows, 0.0, er)
                    ei = jnp.where(kept_rows, 0.0, ei)
                    fr = jnp.where(kept_rows, OMEGA * w_re, fr)
                    fi = jnp.where(kept_rows, OMEGA * w_im, fi)
            e_re[plane, at, :] = er
            e_im[plane, at, :] = ei
            f_re[plane, at, :] = fr
            f_im[plane, at, :] = fi


def relax_kernel(
    info, keep, iterate, x_band, z_band, corner, e_re, e_im, f_re, f_im, movers, halo,
    own, beside, x_a, x_b, z_first, z_last,
    low, w, w_next, h, h_next, he_re, he_im, hf_re, hf_im, hq, hr, hs, mq, mr, sides,
):
    half = info[0]
    active = info[1]
    odd = info[2]

    @pl.when(active == 0)
    def _():
        own[...] = iterate[...]
        beside[...] = halo[pl.ds(0, 2)]

    @pl.when(active == 1)
    def _():
        keep_x = keep[0]
        fill_low_tiles(low, z_band, corner, keep_x, keep[1], 2)
        fields = [(iterate, 0), (iterate, 1)]
        lanes = lane_ids()
        rows = row_ids()
        place = lanes % GROUP
        group = lanes // GROUP
        least = (GROUP - HALO) * half
        zeros = jnp.zeros((8, LANES), jnp.float32)
        for scratch in (w, w_next, h, h_next):
            scratch[...] = jnp.zeros_like(scratch)

        for tile in range(4):
            along_z = sigma_z(tile, keep[3])
            kept_rows = rows < 5
            at, inner = pl.ds(8 * tile, 8), pl.ds(8 + 8 * tile, 8)
            for plane in range(EXT):
                for part in range(2):
                    w[part, plane + 1, inner, :] = tile_of(
                        fields, x_band, low, part, plane, tile, keep_x
                    )
            for start in range(STRIDE):
                w_re, w_im, s_re, s_im, wave_sq = [halo[f, start, at, :] for f in range(5)]
                h[0, start, inner, :] = w_re
                h[1, start, inner, :] = w_im
                x = (STRIDE * group + start - BAND).astype(jnp.float32)
                ramp = jnp.maximum(x - (CX - PML) + 1.0, 0.0) / PML
                sigma = along_z + SIGMA * ramp * ramp * keep[2]
                er, ei, fr, fi = coefficients(wave_sq, s_re, s_im, sigma)
                kept = (place < least) | (place >= least + HALO) | (group == PER)
                if start == 0:
                    kept = kept | (group == 0)
                if tile == 0:
                    kept = kept | kept_rows
                he_re[start, at, :] = jnp.where(kept, 0.0, er)
                he_im[start, at, :] = jnp.where(kept, 0.0, ei)
                hf_re[start, at, :] = jnp.where(kept, OMEGA * w_re, fr)
                hf_im[start, at, :] = jnp.where(kept, OMEGA * w_im, fi)

        first_lane = lanes == 0
        last_lane = lanes == LANES - 1
        turns = [GROUP * (j + half) for j in range(PER)]
        taken = [
            lanes == lax.rem(turn + jnp.where(half == 0, LANES - 1, 0), LANES) for turn in turns
        ]

        def undamped(plane, tile):
            return plane < BAND + CX - PML and tile < 3

        def updated(w_re, w_im, t_re, t_im, er, ei, fr, fi):
            new_re = (1.0 - OMEGA) * w_re + fr
            new_im = (1.0 - OMEGA) * w_im + fi
            if ei is None:
                return new_re + er * t_re, new_im + er * t_im
            return new_re + (er * t_re - ei * t_im), new_im + (er * t_im + ei * t_re)

        def sweep(w, h, w_out, h_out):
            def centre_and_z(ref, part, plane, tile):
                base = 8 + 8 * tile
                return ref[part, plane, pl.ds(base, 8), :], (
                    ref[part, plane, pl.ds(base - 1, 8), :]
                    + ref[part, plane, pl.ds(base + 1, 8), :]
                )

            for tile in range(4):
                at = pl.ds(8 * tile, 8)
                for part in range(2):
                    both = [centre_and_z(h, part, s, tile) for s in range(STRIDE)]
                    below = [roll(value, GROUP) for value in both[-1]]
                    above = [roll(value, -GROUP) for value in both[0]]
                    both = [below] + both + [above]
                    for s in range(STRIDE):
                        q, near = stencil_parts(
                            both[s + 1][0], both[s][0] + both[s + 2][0],
                            both[s + 1][1], both[s][1] + both[s + 2][1],
                        )
                        hq[part, s, at, :] = q
                        hs[pl.ds(32 * (STRIDE * part + s) + 8 * tile, 8), :] = q
                        hr[part, s, at, :] = near

            value = hs[...]
            head = value.astype(jnp.bfloat16)
            tail = (value - head.astype(jnp.float32)).astype(jnp.bfloat16)
            both = jnp.concatenate([head, tail], 1)
            for m in range(MOVERS):
                moved = jnp.dot(both, movers[m], preferred_element_type=jnp.float32)
                sides[2 * m] = moved[:, :LANES]
                if 2 * m + 1 < PER:
                    sides[2 * m + 1] = moved[:, LANES:]

            for tile in range(4):
                at = pl.ds(8 * tile, 8)
                for part in range(2):
                    before, here = (zeros, zeros), centre_and_z(w, part, 1, tile)
                    for plane in range(EXT):
                        after = (zeros, zeros)
                        if plane + 1 < EXT:
                            after = centre_and_z(w, part, plane + 2, tile)
                        q, near = stencil_parts(
                            here[0], before[0] + after[0], here[1], before[1] + after[1]
                        )
                        mq[part, plane, at, :] = q
                        mr[part, plane, at, :] = near
                        before, here = here, after

            for tile in range(4):
                at = pl.ds(8 * tile, 8)
                base = 8 + 8 * tile
                joint = [[hq[part, s, at, :] for s in range(STRIDE)] for part in range(2)]
                for j in range(PER):
                    planes = range(STRIDE * j, STRIDE * (j + 1))
                    q = [[mq[part, plane, at, :] for part in range(2)] for plane in planes]
                    up = [[roll(value, -1) for value in pair] for pair in q]
                    down = [[roll(value, 1) for value in pair] for pair in q]
                    side = [
                        [
                            sides[j, pl.ds(32 * (STRIDE * part + s) + 8 * tile, 8), :]
                            for part in range(2)
                        ]
                        for s in range(STRIDE)
                    ]
                    turned = [[pltpu.roll(value, turns[j], 1) for value in pair] for pair in q]
                    for n, plane in enumerate(planes):
                        total = [
                            jnp.where(last_lane, side[n][part], up[n][part])
                            + jnp.where(first_lane, side[n][part], down[n][part])
                            + mr[part, plane, at, :]
                            for part in range(2)
                        ]
                        for part in range(2):
                            joint[part][n] = jnp.where(taken[j], turned[n][part], joint[part][n])
                        new_re, new_im = updated(
                            w[0, plane + 1, pl.ds(base, 8), :], w[1, plane + 1, pl.ds(base, 8), :],
                            total[0], total[1],
                            e_re[plane, at, :], None if undamped(plane, tile) else e_im[plane, at, :],
                            f_re[plane, at, :], f_im[plane, at, :],
                        )
                        w_out[0, plane + 1, pl.ds(base, 8), :] = new_re
                        w_out[1, plane + 1, pl.ds(base, 8), :] = new_im

                for part in range(2):
                    for s in range(STRIDE):
                        hq[part, s, at, :] = joint[part][s]

            for tile in range(4):
                at = pl.ds(8 * tile, 8)
                base = 8 + 8 * tile
                total = [
                    [pair_sum(hq[part, s, at, :]) + hr[part, s, at, :] for part in range(2)]
                    for s in range(STRIDE)
                ]
                for s in range(STRIDE):
                    new_re, new_im = updated(
                        h[0, s, pl.ds(base, 8), :], h[1, s, pl.ds(base, 8), :],
                        total[s][0], total[s][1],
                        he_re[s, at, :], he_im[s, at, :],
                        hf_re[s, at, :], hf_im[s, at, :],
                    )
                    h_out[0, s, pl.ds(base, 8), :] = new_re
                    h_out[1, s, pl.ds(base, 8), :] = new_im

        def two_sweeps(turn, carry):
            sweep(w, h, w_next, h_next)
            sweep(w_next, h_next, w, h)
            return carry

        lax.fori_loop(0, SWEEPS // 2, two_sweeps, 0)
        for part in range(2):
            for x in range(CX):
                own[part, x] = w[part, x + BAND + 1, pl.ds(16, CZ), :]
            for s in range(STRIDE):
                beside[part, s] = h[part, s, pl.ds(8, 32), :]

    for part in range(2):
        for face, side in ((x_a, 1 - odd), (x_b, odd)):
            face[part, 0] = own[part, (CX - 1) * side]
            face[part, 1] = beside[part, (STRIDE - 1) * side, pl.ds(8, CZ), :]
        for face, z in ((z_first, 0), (z_last, CZ - 1)):
            face[part, pl.ds(24, 8), :] = jnp.zeros((8, LANES), jnp.float32)
            for x in range(CX):
                face[part, pl.ds(x + 1, 1), :] = own[part, x, pl.ds(z, 1), :]
            for s in range(STRIDE):
                face[part, pl.ds(SIDE_ROW + s, 1), :] = beside[part, s, pl.ds(8 + z, 1), :]


def face_kernel(info, keep, z_first, z_last, x_a, x_b, a_out, b_out, first, last):
    odd_x = info[2] == 1
    odd_z = info[3] == 1
    group = lax.broadcasted_iota(jnp.int32, (1, LANES), 1) // GROUP
    for face, out, z in ((z_first, first, 0), (z_last, last, CZ - 1)):
        out[...] = face[...]
        for part in range(2):
            a, b = [[ref[part, n, pl.ds(z, 1), :] for n in range(2)] for ref in (x_a, x_b)]
            low = [jnp.where(odd_x, a[n], b[n]) * keep[0] for n in range(2)]
            high = [jnp.where(odd_x, b[n], a[n]) * keep[1] for n in range(2)]
            out[part, pl.ds(0, 1), :] = low[0]
            out[part, pl.ds(CX + 1, 1), :] = high[0]
            for s, value, to, turn in (
                (STRIDE - 1, low[1], 0, -6 * GROUP), (0, high[1], 7, 6 * GROUP)
            ):
                at = pl.ds(SIDE_ROW + s, 1)
                out[part, at, :] = jnp.where(group == to, roll(value, turn), face[part, at, :])
    a_out[...] = jnp.where(odd_z, first[...], last[...])
    b_out[...] = jnp.where(odd_z, last[...], first[...])


def residual_kernel(
    info, keep, field, source, wave, beside, x_a, x_b, z_a, z_b,
    out, total, box, sides, mq, mr, hs, z_low, z_high,
):
    half = info[0]
    odd_x = info[2] == 1
    odd_z = info[3] == 1
    z_low[...] = jnp.where(odd_z, z_a[...], z_b[...])
    z_high[...] = jnp.where(odd_z, z_b[...], z_a[...])

    def x_sides(part, n, rows):
        a, b = x_a[part, n, rows, :], x_b[part, n, rows, :]
        return jnp.where(odd_x, a, b) * keep[0], jnp.where(odd_x, b, a) * keep[1]

    lanes = lane_ids()
    group = lanes // GROUP
    zeros = jnp.zeros((8, LANES), jnp.float32)
    for part in range(2):
        low, high = x_sides(part, 0, pl.ds(0, CZ))
        box[part, 0, pl.ds(8, CZ), :] = low
        box[part, CX + 1, pl.ds(8, CZ), :] = high
        for x in range(CX):
            box[part, x + 1, pl.ds(8, CZ), :] = field[part, x]
        for x in range(CX + 2):
            box[part, x, pl.ds(7, 1), :] = z_low[part, pl.ds(x, 1), :] * keep[2]
            box[part, x, pl.ds(8 + CZ, 1), :] = z_high[part, pl.ds(x, 1), :] * keep[3]
        for s in range(STRIDE):
            row = pl.ds(SIDE_ROW + s, 1)
            sides[part, s, pl.ds(7, 1), :] = z_low[part, row, :] * keep[2]
            sides[part, s, pl.ds(8 + CZ, 1), :] = z_high[part, row, :] * keep[3]
            for tile in range(3):
                value = beside[part, s, pl.ds(8 + 8 * tile, 8), :]
                low, high = x_sides(part, 1, pl.ds(8 * tile, 8))
                if s == STRIDE - 1:
                    value = jnp.where(group == 0, roll(low, -6 * GROUP), value)
                if s == 0:
                    value = jnp.where(group == 7, roll(high, 6 * GROUP), value)
                sides[part, s, pl.ds(8 + 8 * tile, 8), :] = value

    def centre_and_z(ref, part, plane, tile):
        base = 8 + 8 * tile
        return ref[part, plane, pl.ds(base, 8), :], (
            ref[part, plane, pl.ds(base - 1, 8), :] + ref[part, plane, pl.ds(base + 1, 8), :]
        )

    joined = lanes % GROUP == (GROUP - 1) * half
    for part in range(2):
        for tile in range(3):
            at = pl.ds(8 * tile, 8)
            both = [centre_and_z(sides, part, s, tile) for s in range(STRIDE)]
            below = [roll(value, GROUP) for value in both[-1]]
            above = [roll(value, -GROUP) for value in both[0]]
            both = [below] + both + [above]
            for s in range(STRIDE):
                q, _ = stencil_parts(
                    both[s + 1][0], both[s][0] + both[s + 2][0],
                    both[s + 1][1], both[s][1] + both[s + 2][1],
                )
                hs[part, s, at, :] = jnp.where(joined, q, 0.0)

    for part in range(2):
        for tile in range(3):
            at = pl.ds(8 * tile, 8)
            before, here = centre_and_z(box, part, 0, tile), centre_and_z(box, part, 1, tile)
            for x in range(CX):
                after = centre_and_z(box, part, x + 2, tile)
                q, near = stencil_parts(
                    here[0], before[0] + after[0], here[1], before[1] + after[1]
                )
                mq[part, x, at, :] = q
                mr[part, x, at, :] = near
                before, here = here, after

    first_lane = lanes == 0
    last_lane = lanes == LANES - 1
    to_edge = jnp.where(half == 0, LANES - 1, 1)
    squares = [zeros] * 4
    for part in range(2):
        for tile in range(3):
            at = pl.ds(8 * tile, 8)
            for j in range(1, PER):
                turn = lax.rem(LANES - GROUP * (j + half) + to_edge, LANES)
                planes = range(STRIDE * (j - 1), STRIDE * j)
                q = [mq[part, x, at, :] for x in planes]
                up = [roll(value, -1) for value in q]
                down = [roll(value, 1) for value in q]
                side = [pltpu.roll(hs[part, s, at, :], turn, 1) for s in range(STRIDE)]
                for n, x in enumerate(planes):
                    y = jnp.where(last_lane, side[n], up[n]) + jnp.where(
                        first_lane, side[n], down[n]
                    )
                    gap = (
                        source[part, x, at, :]
                        - (5.0 - wave[x, at, :]) * field[part, x, at, :]
                        + 0.5 * (y + mr[part, x, at, :])
                    )
                    out[part, x, at, :] = gap
                    squares[n] = squares[n] + gap * gap
    total[...] = jnp.broadcast_to(jnp.sum(sum(squares[1:], squares[0])), total.shape)


def f32(*shape):
    return jax.ShapeDtypeStruct(shape, jnp.float32)


def ring(value, axis, by):
    size = lax.axis_size(axis)
    return lax.ppermute(value, axis, [(i, (i + by) % size) for i in range(size)])


def pairs(value, axis, first):
    size = lax.axis_size(axis)
    moves = []
    for i in range(first, size, 2):
        j = (i + 1) % size
        moves += [(i, j), (j, i)]
    return lax.ppermute(value, axis, moves)


def diagonal(value, by_x, by_z):
    size_x, size_z = lax.axis_size("gx"), lax.axis_size("gz")
    pairs = [
        (x * size_z + z, ((x + by_x) % size_x) * size_z + (z + by_z) % size_z)
        for x in range(size_x)
        for z in range(size_z)
    ]
    return lax.ppermute(value, ("gx", "gz"), pairs)


def swap(value):
    return lax.ppermute(value, "gy", [(0, 1), (1, 0)])


def on_device(source, iterate, wave_sq, front, pml_flags):
    size_x, size_z, size_y = lax.axis_size("gx"), lax.axis_size("gz"), lax.axis_size("gy")
    at_x, at_z, half = lax.axis_index("gx"), lax.axis_index("gz"), lax.axis_index("gy")
    active = (jnp.mod(at_x + at_z - front[0], size_z) == 0).astype(jnp.int32)
    info = jnp.stack([half, active, at_x % 2, at_z % 2]).astype(jnp.int32)
    flag_bits = pml_flags[0, 0]
    as_float = lambda test: test.astype(jnp.float32)
    band_keep = jnp.stack(
        [
            as_float(at_x > 0),
            as_float(at_z > 0),
            as_float(flag_bits % 2),
            as_float(flag_bits // 2 % 2),
        ]
    )
    box_keep = jnp.stack(
        [
            as_float(at_x > 0),
            as_float(at_x < size_x - 1),
            as_float(at_z > 0),
            as_float(at_z < size_z - 1),
        ]
    )

    def call(kernel, outs, ins, name, scratch=(), place=VMEM, sems=0):
        scalars = sum(value.ndim == 1 for value in ins)
        return pl.pallas_call(
            kernel,
            out_shape=outs,
            in_specs=[SMEM] * scalars + [place] * (len(ins) - scalars),
            out_specs=jax.tree.map(lambda _: VMEM, outs),
            scratch_shapes=[pltpu.VMEM(shape, jnp.float32) for shape in scratch]
            + [pltpu.SemaphoreType.DMA((sems,))] * (sems > 0),
            compiler_params=pltpu.CompilerParams(vmem_limit_bytes=20 * MIB),
            name=name,
        )(*ins)

    x_band, z_band, corner = call(
        bands_kernel,
        (f32(LAYERS, CZ, LANES), f32(LAYERS * CX, LANES), f32(72, LANES)),
        [pltpu.with_memory_space_constraint(v, pltpu.HBM) for v in (iterate, source, wave_sq)],
        "bands",
        [(5, BAND, CZ, LANES), (5, CX, 8, LANES)],
        place=HBM,
        sems=15,
    )
    corner = diagonal(corner, 1, 1)
    x_band = ring(x_band, "gx", 1)
    z_band = ring(z_band, "gz", 1)
    low_tiles = (5, EXT, 8, LANES)
    halo = call(
        halo_kernel,
        f32(5, STRIDE, 32, LANES),
        (info, band_keep, iterate, source, wave_sq, x_band, z_band, corner),
        "pack_halo",
        [low_tiles],
    )
    halo = swap(halo)
    planes, packs = (EXT, 32, LANES), (STRIDE, 32, LANES)
    own = (2, CX, CZ, LANES)
    in_vmem = pltpu.VMEM(own, jnp.float32)
    box_like, pack_like = (2, EXT + 2, 48, LANES), (2, STRIDE, 48, LANES)
    x_face, z_face = f32(2, 2, CZ, LANES), f32(2, 32, LANES)
    weights = call(
        weights_kernel,
        (f32(*planes),) * 4
        + (jax.ShapeDtypeStruct((MOVERS, 2 * LANES, 2 * LANES), jnp.bfloat16),),
        (info, band_keep, iterate, source, wave_sq, x_band, z_band, corner),
        "weights",
        [low_tiles],
    )
    new, beside, x_a, x_b, z_first, z_last = call(
        relax_kernel,
        (in_vmem, f32(2, STRIDE, 32, LANES), x_face, x_face, z_face, z_face),
        (info, band_keep, iterate, x_band, z_band, corner, *weights, halo),
        "relax",
        [(2,) + low_tiles[1:], box_like, box_like]
        + [pack_like] * 2
        + [packs] * 4
        + [(2,) + packs] * 2
        + [(2 * STRIDE * 32, LANES)]
        + [(2,) + planes] * 2
        + [(PER, 2 * STRIDE * 32, LANES)],
    )
    x_a, x_b = pairs(x_a, "gx", 0), pairs(x_b, "gx", 1)
    z_a, z_b = call(
        face_kernel,
        (z_face, z_face),
        (info, box_keep, z_first, z_last, x_a, x_b),
        "faces",
        [z_face.shape] * 2,
    )
    z_a, z_b = pairs(z_a, "gz", 0), pairs(z_b, "gz", 1)
    count = size_x * size_z * size_y
    residual, total = call(
        residual_kernel,
        (in_vmem, f32(count, LANES)),
        (info, box_keep, new, source, wave_sq, beside, x_a, x_b, z_a, z_b),
        "residual",
        [(2, CX + 2, 48, LANES), (2, STRIDE, 48, LANES), own, own, (2, STRIDE, CZ, LANES)]
        + [z_face.shape] * 2,
    )
    parts = lax.all_to_all(total, ("gx", "gz", "gy"), 0, 0, tiled=True)
    cells = 2 * CX * CZ * LANES * count
    norm = jnp.sqrt(jnp.sum(parts, axis=0)[:1] / cells)
    return new, residual, norm


def solution(mesh):
    in_specs = (
        P(None, "gx", "gz", "gy"),
        P(None, "gx", "gz", "gy"),
        P("gx", "gz", "gy"),
        P(),
        P("gx", "gz"),
    )
    out_specs = (P(None, "gx", "gz", "gy"), P(None, "gx", "gz", "gy"), P())
    return jax.shard_map(
        on_device, mesh=mesh, in_specs=in_specs, out_specs=out_specs, check_vma=False
    )
```

```python
import jax
import jax.numpy as jnp
from jax import lax
from jax.experimental import pallas as pl
from jax.experimental.pallas import tpu as pltpu
from jax.sharding import PartitionSpec as P

BAND = 4
PML = 8
SWEEPS = 10
OMEGA = 0.6
SIGMA = 6.0

CX = 24
CZ = 24
LANES = 128
EXT = CX + BAND
GROUP = 16
HALO = 11
OVER = GROUP - HALO
STRIDE = 4
MOVERS = (EXT // STRIDE + 1) // 2
LAYERS = 2 * BAND + 3 * (BAND - 1)
PER = EXT // STRIDE

HALO_ROW = 2 * CZ
SIDE_ROW = 26

MIB = 1024 * 1024

SMEM = pl.BlockSpec(memory_space=pltpu.SMEM)
VMEM = pl.BlockSpec(memory_space=pltpu.VMEM)
HBM = pl.BlockSpec(memory_space=pltpu.HBM)


def lane_ids():
    return lax.broadcasted_iota(jnp.int32, (8, LANES), 1)


def row_ids():
    return lax.broadcasted_iota(jnp.int32, (8, LANES), 0)


def roll(value, shift):
    if isinstance(shift, int):
        shift = shift % LANES
        if shift == 0:
            return value
    return pltpu.roll(value, shift, 1)


def pair_sum(value):
    return roll(value, 1) + roll(value, -1)


def stencil_parts(centre, across, z_centre, z_across):
    both = across + z_centre
    part = 0.25 * z_across
    near = both + part
    return centre + 0.25 * (near + part), near


def layers(field):
    return 0 if field < 2 else 1


def layer_row(field, layer):
    return 4 * field + layer if field < 2 else 8 + 3 * (field - 2) + layer - 1


def bands_kernel(iterate, source, wave, x_out, z_out, corner_out, x_part, z_part, sems):
    fields = [iterate.at[0], iterate.at[1], source.at[0], source.at[1], wave]
    copies = [
        pltpu.make_async_copy(ref.at[pl.ds(CX - BAND, BAND)], x_part.at[f], sems.at[f])
        for f, ref in enumerate(fields)
    ]
    for f, ref in enumerate(fields):
        for piece in range(2):
            some = pl.ds(CX // 2 * piece, CX // 2)
            copies.append(
                pltpu.make_async_copy(
                    ref.at[some, pl.ds(CZ - 8, 8)], z_part.at[f, some], sems.at[5 + 2 * f + piece]
                )
            )
    for copy in copies:
        copy.start()
    for copy in copies:
        copy.wait()
    corner_out[...] = jnp.zeros_like(corner_out)
    for field in range(5):
        first = layers(field)
        depth = BAND - first
        for layer in range(first, BAND):
            row = layer_row(field, layer)
            x_out[row] = x_part[field, layer]
            corner_out[pl.ds(BAND * row, BAND), :] = x_part[field, layer, pl.ds(CZ - BAND, BAND), :]
        for x in range(CX):
            rows = pl.ds(LAYERS * x + layer_row(field, first), depth)
            z_out[rows, :] = z_part[field, x, pl.ds(8 - depth, depth), :]


def tile_of(fields, bands, corner_tiles, field, plane, tile, keep_x):
    if tile == 0:
        return corner_tiles[field, plane]
    rows = pl.ds(8 * (tile - 1), 8)
    if plane < BAND:
        if plane < layers(field):
            return jnp.zeros((8, LANES), jnp.float32)
        return bands[layer_row(field, plane), rows, :] * keep_x
    ref, index = fields[field]
    x = plane - BAND
    return ref[x, rows, :] if index is None else ref[index, x, rows, :]


def fill_low_tiles(low, z_band, corner, keep_x, keep_z, count=5):
    keep_both = keep_x * keep_z
    low[...] = jnp.zeros_like(low)
    for field in range(count):
        first = layers(field)
        depth = BAND - first
        for plane in range(EXT):
            to = pl.ds(8 - depth, depth)
            if plane >= BAND:
                rows = pl.ds(LAYERS * (plane - BAND) + layer_row(field, first), depth)
                low[field, plane, to, :] = z_band[rows, :] * keep_z
            elif plane >= first:
                rows = pl.ds(BAND * layer_row(field, plane) + first, depth)
                low[field, plane, to, :] = corner[rows, :] * keep_both


def own_layout(half):
    return OVER + (HALO - OVER) * half, HALO * half, OVER


def other_layout(half):
    return HALO - (HALO - OVER) * half, OVER * half, HALO


def join_lane(half):
    return OVER + (GROUP - 1 - 2 * OVER) * half


def pack(packed, values, layout):
    turn, least, count = layout
    lanes = lane_ids()
    place = lanes % GROUP
    wanted = (place >= least) & (place < least + count)
    turned = [(j, pltpu.roll(v, lax.rem(GROUP * j + turn, LANES), 1)) for j, v in values]
    for j, value in turned:
        packed = jnp.where(wanted & (lanes // GROUP == j), value, packed)
    return packed


def inner_halo_kernel(info, iterate, source, wave, theirs, mine):
    half = info[0]
    fields = [(iterate, 0), (iterate, 1), (source, 0), (source, 1), (wave, None)]
    zeros = jnp.zeros((8, LANES), jnp.float32)
    for field in range(5):
        for start in range(STRIDE):
            for tile in range(1, 4):
                values = [
                    (j, tile_of(fields, None, None, field, STRIDE * j + start, tile, None))
                    for j in range(1, PER)
                ]
                at = pl.ds(8 * tile, 8)
                theirs[field, start, at, :] = pack(zeros, values, other_layout(half))
                mine[field, start, at, :] = pack(zeros, values, own_layout(half))


def pack_bands(inner, out, low, x_band, keep_x, layout):
    for field in range(5):
        for start in range(STRIDE):
            values = [(j, low[field, STRIDE * j + start]) for j in range(PER)]
            zeros = jnp.zeros((8, LANES), jnp.float32)
            out[field, start, pl.ds(0, 8), :] = pack(zeros, values, layout)
            for tile in range(1, 4):
                at = pl.ds(8 * tile, 8)
                packed = inner[field, start, at, :]
                if start >= layers(field):
                    value = x_band[layer_row(field, start), pl.ds(8 * (tile - 1), 8), :] * keep_x
                    packed = pack(packed, [(0, value)], layout)
                out[field, start, at, :] = packed


def halo_kernel(info, keep, inner, x_band, z_band, corner, out, low):
    fill_low_tiles(low, z_band, corner, keep[0], keep[1])
    pack_bands(inner, out, low, x_band, keep[0], other_layout(info[0]))


def coefficients(wave_sq, s_re, s_im, sigma):
    diag = 5.0 - wave_sq
    scale = (0.5 * OMEGA) / (diag * diag + sigma * sigma)
    er = diag * scale
    ei = -sigma * scale
    return er, ei, 2.0 * (er * s_re - ei * s_im), 2.0 * (er * s_im + ei * s_re)


def sigma_z(tile, flag):
    if tile == 0:
        return jnp.zeros((8, LANES), jnp.float32)
    z = (row_ids() + 8 * (tile - 1)).astype(jnp.float32)
    ramp = jnp.maximum(z - (CZ - PML) + 1.0, 0.0) / PML
    return SIGMA * ramp * ramp * flag


def weights_kernel(
    info, keep, iterate, source, wave, inner, x_band, z_band, corner,
    e_re, e_im, f_re, f_im, movers, mine, low,
):
    half = info[0]
    keep_x = keep[0]
    lane = lax.broadcasted_iota(jnp.int32, (16, 2 * LANES), 1)
    row = lax.broadcasted_iota(jnp.int32, (16, 2 * LANES), 0)
    ends = lane % LANES == (LANES - 1) * (1 - half)
    for m in range(MOVERS):
        start = GROUP * (2 * m + lane // LANES) + join_lane(half)
        for first in range(0, 2 * LANES, 16):
            hit = ends & ((row + first) % LANES == start)
            movers[m, pl.ds(first, 16), :] = hit.astype(jnp.float32).astype(jnp.bfloat16)
    fill_low_tiles(low, z_band, corner, keep_x, keep[1])
    pack_bands(inner, mine, low, x_band, keep_x, own_layout(half))
    fields = [(iterate, 0), (iterate, 1), (source, 0), (source, 1), (wave, None)]
    zeros = jnp.zeros((8, LANES), jnp.float32)
    kept_rows = row_ids() < 5
    for tile in range(4):
        along_z = sigma_z(tile, keep[3])
        at = pl.ds(8 * tile, 8)
        for plane in range(EXT):
            values = [tile_of(fields, x_band, low, f, plane, tile, keep_x) for f in range(5)]
            w_re, w_im, s_re, s_im, wave_sq = values
            if plane == 0:
                er, ei, fr, fi = zeros, zeros, OMEGA * w_re, OMEGA * w_im
            else:
                ramp = max(plane - BAND - (CX - PML) + 1.0, 0.0) / PML
                sigma = along_z + SIGMA * ramp * ramp * keep[2]
                er, ei, fr, fi = coefficients(wave_sq, s_re, s_im, sigma)
                if tile == 0:
                    er = jnp.where(kept_rows, 0.0, er)
                    ei = jnp.where(kept_rows, 0.0, ei)
                    fr = jnp.where(kept_rows, OMEGA * w_re, fr)
                    fi = jnp.where(kept_rows, OMEGA * w_im, fi)
            e_re[plane, at, :] = er
            e_im[plane, at, :] = ei
            f_re[plane, at, :] = fr
            f_im[plane, at, :] = fi


def relax_kernel(
    info, keep, iterate, x_band, z_band, corner, e_re, e_im, f_re, f_im, movers, mine, halo,
    own, beside, x_a, x_b, z_first, z_last,
    low, w, h, he_re, he_im, hf_re, hf_im, hq, hr, hs, mq, mr, sides,
):
    half = info[0]
    active = info[1]
    odd = info[2]

    @pl.when(active == 0)
    def _():
        own[...] = iterate[...]
        beside[...] = halo[pl.ds(0, 2)]

    @pl.when(active == 1)
    def _():
        keep_x = keep[0]
        fill_low_tiles(low, z_band, corner, keep_x, keep[1], 2)
        fields = [(iterate, 0), (iterate, 1)]
        lanes = lane_ids()
        rows = row_ids()
        place = lanes % GROUP
        group = lanes // GROUP
        turn, least, count = own_layout(half)
        repeated = (place >= least) & (place < least + count)
        zeros = jnp.zeros((8, LANES), jnp.float32)
        for scratch in (w, h):
            scratch[...] = jnp.zeros_like(scratch)

        for tile in range(4):
            along_z = sigma_z(tile, keep[3])
            kept_rows = rows < 5
            at, inner = pl.ds(8 * tile, 8), pl.ds(8 + 8 * tile, 8)
            for plane in range(EXT):
                for part in range(2):
                    value = tile_of(fields, x_band, low, part, plane, tile, keep_x)
                    w[part, plane + 1, inner, :] = value
            for start in range(STRIDE):
                w_re, w_im, s_re, s_im, wave_sq = [
                    jnp.where(repeated, mine[f, start, at, :], halo[f, start, at, :])
                    for f in range(5)
                ]
                h[0, start, inner, :] = w_re
                h[1, start, inner, :] = w_im
                x = (STRIDE * group + start - BAND).astype(jnp.float32)
                ramp = jnp.maximum(x - (CX - PML) + 1.0, 0.0) / PML
                sigma = along_z + SIGMA * ramp * ramp * keep[2]
                er, ei, fr, fi = coefficients(wave_sq, s_re, s_im, sigma)
                kept = group == PER
                if start == 0:
                    kept = kept | (group == 0)
                if tile == 0:
                    kept = kept | kept_rows
                he_re[start, at, :] = jnp.where(kept, 0.0, er)
                he_im[start, at, :] = jnp.where(kept, 0.0, ei)
                hf_re[start, at, :] = jnp.where(kept, OMEGA * w_re, fr)
                hf_im[start, at, :] = jnp.where(kept, OMEGA * w_im, fi)

        first_lane = lanes == 0
        last_lane = lanes == LANES - 1
        def undamped(plane, tile):
            return plane < BAND + CX - PML and tile < 3

        def updated(w_re, w_im, t_re, t_im, er, ei, fr, fi):
            new_re = (1.0 - OMEGA) * w_re + fr
            new_im = (1.0 - OMEGA) * w_im + fi
            if ei is None:
                return new_re + er * t_re, new_im + er * t_im
            return new_re + (er * t_re - ei * t_im), new_im + (er * t_im + ei * t_re)

        def sweep():
            first = 1
            def centre_and_z(ref, part, plane, tile):
                base = 8 + 8 * tile
                return ref[part, plane, pl.ds(base, 8), :], (
                    ref[part, plane, pl.ds(base - 1, 8), :]
                    + ref[part, plane, pl.ds(base + 1, 8), :]
                )

            for tile in range(4):
                at = pl.ds(8 * tile, 8)
                for part in range(2):
                    both = [centre_and_z(h, part, s, tile) for s in range(STRIDE)]
                    below = [roll(value, GROUP) for value in both[-1]]
                    above = [roll(value, -GROUP) for value in both[0]]
                    both = [below] + both + [above]
                    for s in range(STRIDE):
                        q, near = stencil_parts(
                            both[s + 1][0], both[s][0] + both[s + 2][0],
                            both[s + 1][1], both[s][1] + both[s + 2][1],
                        )
                        hq[part, s, at, :] = q
                        hs[pl.ds(32 * (STRIDE * part + s) + 8 * tile, 8), :] = q
                        hr[part, s, at, :] = near

            value = hs[...]
            head = value.astype(jnp.bfloat16)
            tail = (value - head.astype(jnp.float32)).astype(jnp.bfloat16)
            both = jnp.concatenate([head, tail], 1)
            for m in range(MOVERS):
                moved = jnp.dot(both, movers[m], preferred_element_type=jnp.float32)
                sides[2 * m] = moved[:, :LANES]
                if 2 * m + 1 < PER:
                    sides[2 * m + 1] = moved[:, LANES:]

            for tile in range(4):
                at = pl.ds(8 * tile, 8)
                for part in range(2):
                    before = centre_and_z(w, part, first, tile)
                    here = centre_and_z(w, part, first + 1, tile)
                    for plane in range(first, EXT):
                        after = (zeros, zeros)
                        if plane + 1 < EXT:
                            after = centre_and_z(w, part, plane + 2, tile)
                        q, near = stencil_parts(
                            here[0], before[0] + after[0], here[1], before[1] + after[1]
                        )
                        mq[part, plane, at, :] = q
                        mr[part, plane, at, :] = near
                        before, here = here, after

            for tile in range(4):
                at = pl.ds(8 * tile, 8)
                base = 8 + 8 * tile
                for j in range(PER):
                    planes = range(max(STRIDE * j, first), STRIDE * (j + 1))
                    q = [[mq[part, plane, at, :] for part in range(2)] for plane in planes]
                    up = [[roll(value, -1) for value in pair] for pair in q]
                    down = [[roll(value, 1) for value in pair] for pair in q]
                    side = [
                        [
                            sides[j, pl.ds(32 * (STRIDE * part + plane % STRIDE) + 8 * tile, 8), :]
                            for part in range(2)
                        ]
                        for plane in planes
                    ]
                    for n, plane in enumerate(planes):
                        total = [
                            jnp.where(last_lane, side[n][part], up[n][part])
                            + jnp.where(first_lane, side[n][part], down[n][part])
                            + mr[part, plane, at, :]
                            for part in range(2)
                        ]
                        new_re, new_im = updated(
                            w[0, plane + 1, pl.ds(base, 8), :], w[1, plane + 1, pl.ds(base, 8), :],
                            total[0], total[1],
                            e_re[plane, at, :], None if undamped(plane, tile) else e_im[plane, at, :],
                            f_re[plane, at, :], f_im[plane, at, :],
                        )
                        w[0, plane + 1, pl.ds(base, 8), :] = new_re
                        w[1, plane + 1, pl.ds(base, 8), :] = new_im

            for tile in range(4):
                at = pl.ds(8 * tile, 8)
                base = 8 + 8 * tile
                total = [
                    [pair_sum(hq[part, s, at, :]) + hr[part, s, at, :] for part in range(2)]
                    for s in range(STRIDE)
                ]
                for s in range(STRIDE):
                    new_re, new_im = updated(
                        h[0, s, pl.ds(base, 8), :], h[1, s, pl.ds(base, 8), :],
                        total[s][0], total[s][1],
                        he_re[s, at, :], he_im[s, at, :],
                        hf_re[s, at, :], hf_im[s, at, :],
                    )
                    h[0, s, pl.ds(base, 8), :] = new_re
                    h[1, s, pl.ds(base, 8), :] = new_im

        def renew():
            for tile in range(4):
                at = pl.ds(8 + 8 * tile, 8)
                for part in range(2):
                    for s in range(STRIDE):
                        values = [(j, w[part, STRIDE * j + s + 1, at, :]) for j in range(PER)]
                        h[part, s, at, :] = pack(h[part, s, at, :], values, own_layout(half))

        def one_sweep(turn, carry):
            sweep()

            @pl.when(turn == SWEEPS // 2 - 1)
            def _():
                renew()

            return carry

        lax.fori_loop(0, SWEEPS, one_sweep, 0)
        for part in range(2):
            for x in range(CX):
                own[part, x] = w[part, x + BAND + 1, pl.ds(16, CZ), :]
            for s in range(STRIDE):
                beside[part, s] = h[part, s, pl.ds(8, 32), :]

    place_in = lane_ids() // GROUP
    for face, side in ((x_a, 1 - odd), (x_b, odd)):
        turned = [
            pltpu.roll(
                beside[n // 3, (STRIDE - 1) * side, pl.ds(8 + 8 * (n % 3), 8), :],
                lax.rem(LANES + GROUP * (n - 1 - (PER - 2) * side), LANES),
                1,
            )
            for n in range(6)
        ]
        packed = turned[0]
        for n in range(1, 6):
            packed = jnp.where(place_in == n, turned[n], packed)
        face[pl.ds(HALO_ROW, 8), :] = packed

    for part in range(2):
        for face, side in ((x_a, 1 - odd), (x_b, odd)):
            face[pl.ds(CZ * part, CZ), :] = own[part, (CX - 1) * side]
        for face, z in ((z_first, 0), (z_last, CZ - 1)):
            face[part, pl.ds(24, 8), :] = jnp.zeros((8, LANES), jnp.float32)
            for x in range(CX):
                face[part, pl.ds(x + 1, 1), :] = own[part, x, pl.ds(z, 1), :]
            for s in range(STRIDE):
                face[part, pl.ds(SIDE_ROW + s, 1), :] = beside[part, s, pl.ds(8 + z, 1), :]


def face_kernel(info, keep, z_first, z_last, x_a, x_b, a_out, b_out, first, last):
    odd_x = info[2] == 1
    odd_z = info[3] == 1
    group = lax.broadcasted_iota(jnp.int32, (1, LANES), 1) // GROUP
    for face, out, z in ((z_first, first, 0), (z_last, last, CZ - 1)):
        out[...] = face[...]
        for part in range(2):
            rows = [pl.ds(CZ * part + z, 1), pl.ds(HALO_ROW + z % 8, 1)]
            a, b = [[ref[row, :] for row in rows] for ref in (x_a, x_b)]
            piece = 3 * part + z // 8
            low = [jnp.where(odd_x, a[n], b[n]) * keep[0] for n in range(2)]
            high = [jnp.where(odd_x, b[n], a[n]) * keep[1] for n in range(2)]
            out[part, pl.ds(0, 1), :] = low[0]
            out[part, pl.ds(CX + 1, 1), :] = high[0]
            for s, value, to, turn in (
                (STRIDE - 1, low[1], 0, -GROUP * piece), (0, high[1], 7, GROUP * (7 - piece))
            ):
                at = pl.ds(SIDE_ROW + s, 1)
                out[part, at, :] = jnp.where(group == to, roll(value, turn), face[part, at, :])
    a_out[...] = jnp.where(odd_z, first[...], last[...])
    b_out[...] = jnp.where(odd_z, last[...], first[...])


def residual_kernel(
    info, keep, field, source, wave, beside, x_a, x_b, z_a, z_b,
    out, total, box, sides, mq, mr, hs, z_low, z_high,
):
    half = info[0]
    odd_x = info[2] == 1
    odd_z = info[3] == 1
    z_low[...] = jnp.where(odd_z, z_a[...], z_b[...])
    z_high[...] = jnp.where(odd_z, z_b[...], z_a[...])

    def x_sides(rows):
        a, b = x_a[rows, :], x_b[rows, :]
        return jnp.where(odd_x, a, b) * keep[0], jnp.where(odd_x, b, a) * keep[1]

    lanes = lane_ids()
    group = lanes // GROUP
    zeros = jnp.zeros((8, LANES), jnp.float32)
    low_halo, high_halo = x_sides(pl.ds(HALO_ROW, 8))
    for part in range(2):
        low, high = x_sides(pl.ds(CZ * part, CZ))
        box[part, 0, pl.ds(8, CZ), :] = low
        box[part, CX + 1, pl.ds(8, CZ), :] = high
        for x in range(CX):
            box[part, x + 1, pl.ds(8, CZ), :] = field[part, x]
        for x in range(CX + 2):
            box[part, x, pl.ds(7, 1), :] = z_low[part, pl.ds(x, 1), :] * keep[2]
            box[part, x, pl.ds(8 + CZ, 1), :] = z_high[part, pl.ds(x, 1), :] * keep[3]
        for s in range(STRIDE):
            row = pl.ds(SIDE_ROW + s, 1)
            sides[part, s, pl.ds(7, 1), :] = z_low[part, row, :] * keep[2]
            sides[part, s, pl.ds(8 + CZ, 1), :] = z_high[part, row, :] * keep[3]
            for tile in range(3):
                value = beside[part, s, pl.ds(8 + 8 * tile, 8), :]
                piece = 3 * part + tile
                if s == STRIDE - 1:
                    value = jnp.where(group == 0, roll(low_halo, -GROUP * piece), value)
                if s == 0:
                    value = jnp.where(group == 7, roll(high_halo, GROUP * (7 - piece)), value)
                sides[part, s, pl.ds(8 + 8 * tile, 8), :] = value

    def centre_and_z(ref, part, plane, tile):
        base = 8 + 8 * tile
        return ref[part, plane, pl.ds(base, 8), :], (
            ref[part, plane, pl.ds(base - 1, 8), :] + ref[part, plane, pl.ds(base + 1, 8), :]
        )

    joined = lanes % GROUP == join_lane(half)
    for part in range(2):
        for tile in range(3):
            at = pl.ds(8 * tile, 8)
            both = [centre_and_z(sides, part, s, tile) for s in range(STRIDE)]
            below = [roll(value, GROUP) for value in both[-1]]
            above = [roll(value, -GROUP) for value in both[0]]
            both = [below] + both + [above]
            for s in range(STRIDE):
                q, _ = stencil_parts(
                    both[s + 1][0], both[s][0] + both[s + 2][0],
                    both[s + 1][1], both[s][1] + both[s + 2][1],
                )
                hs[part, s, at, :] = jnp.where(joined, q, 0.0)

    for part in range(2):
        for tile in range(3):
            at = pl.ds(8 * tile, 8)
            before, here = centre_and_z(box, part, 0, tile), centre_and_z(box, part, 1, tile)
            for x in range(CX):
                after = centre_and_z(box, part, x + 2, tile)
                q, near = stencil_parts(
                    here[0], before[0] + after[0], here[1], before[1] + after[1]
                )
                mq[part, x, at, :] = q
                mr[part, x, at, :] = near
                before, here = here, after

    first_lane = lanes == 0
    last_lane = lanes == LANES - 1
    to_edge = (LANES - 1) * (1 - half) - join_lane(half)
    squares = [zeros] * 4
    for part in range(2):
        for tile in range(3):
            at = pl.ds(8 * tile, 8)
            for j in range(1, PER):
                turn = lax.rem(2 * LANES - GROUP * j + to_edge, LANES)
                planes = range(STRIDE * (j - 1), STRIDE * j)
                q = [mq[part, x, at, :] for x in planes]
                up = [roll(value, -1) for value in q]
                down = [roll(value, 1) for value in q]
                side = [pltpu.roll(hs[part, s, at, :], turn, 1) for s in range(STRIDE)]
                for n, x in enumerate(planes):
                    y = jnp.where(last_lane, side[n], up[n]) + jnp.where(
                        first_lane, side[n], down[n]
                    )
                    gap = (
                        source[part, x, at, :]
                        - (5.0 - wave[x, at, :]) * field[part, x, at, :]
                        + 0.5 * (y + mr[part, x, at, :])
                    )
                    out[part, x, at, :] = gap
                    squares[n] = squares[n] + gap * gap
    total[...] = jnp.broadcast_to(jnp.sum(sum(squares[1:], squares[0])), total.shape)


def f32(*shape):
    return jax.ShapeDtypeStruct(shape, jnp.float32)


def ring(value, axis, by):
    size = lax.axis_size(axis)
    return lax.ppermute(value, axis, [(i, (i + by) % size) for i in range(size)])


def pairs(value, axis, first):
    size = lax.axis_size(axis)
    moves = []
    for i in range(first, size, 2):
        j = (i + 1) % size
        moves += [(i, j), (j, i)]
    return lax.ppermute(value, axis, moves)


def diagonal(value, by_x, by_z):
    size_x, size_z = lax.axis_size("gx"), lax.axis_size("gz")
    pairs = [
        (x * size_z + z, ((x + by_x) % size_x) * size_z + (z + by_z) % size_z)
        for x in range(size_x)
        for z in range(size_z)
    ]
    return lax.ppermute(value, ("gx", "gz"), pairs)


def swap(value):
    return lax.ppermute(value, "gy", [(0, 1), (1, 0)])


def on_device(source, iterate, wave_sq, front, pml_flags):
    size_x, size_z, size_y = lax.axis_size("gx"), lax.axis_size("gz"), lax.axis_size("gy")
    at_x, at_z, half = lax.axis_index("gx"), lax.axis_index("gz"), lax.axis_index("gy")
    active = (jnp.mod(at_x + at_z - front[0], size_z) == 0).astype(jnp.int32)
    info = jnp.stack([half, active, at_x % 2, at_z % 2]).astype(jnp.int32)
    flag_bits = pml_flags[0, 0]
    as_float = lambda test: test.astype(jnp.float32)
    band_keep = jnp.stack(
        [
            as_float(at_x > 0),
            as_float(at_z > 0),
            as_float(flag_bits % 2),
            as_float(flag_bits // 2 % 2),
        ]
    )
    box_keep = jnp.stack(
        [
            as_float(at_x > 0),
            as_float(at_x < size_x - 1),
            as_float(at_z > 0),
            as_float(at_z < size_z - 1),
        ]
    )

    def call(kernel, outs, ins, name, scratch=(), place=VMEM, sems=0):
        scalars = sum(value.ndim == 1 for value in ins)
        return pl.pallas_call(
            kernel,
            out_shape=outs,
            in_specs=[SMEM] * scalars + [place] * (len(ins) - scalars),
            out_specs=jax.tree.map(lambda _: VMEM, outs),
            scratch_shapes=[pltpu.VMEM(shape, jnp.float32) for shape in scratch]
            + [pltpu.SemaphoreType.DMA((sems,))] * (sems > 0),
            compiler_params=pltpu.CompilerParams(vmem_limit_bytes=20 * MIB),
            name=name,
        )(*ins)

    x_band, z_band, corner = call(
        bands_kernel,
        (f32(LAYERS, CZ, LANES), f32(LAYERS * CX, LANES), f32(72, LANES)),
        [pltpu.with_memory_space_constraint(v, pltpu.HBM) for v in (iterate, source, wave_sq)],
        "bands",
        [(5, BAND, CZ, LANES), (5, CX, 8, LANES)],
        place=HBM,
        sems=15,
    )
    corner = diagonal(corner, 1, 1)
    x_band = ring(x_band, "gx", 1)
    z_band = ring(z_band, "gz", 1)
    low_tiles = (5, EXT, 8, LANES)
    packed = f32(5, STRIDE, 32, LANES)
    theirs, mine = call(
        inner_halo_kernel, (packed, packed), (info, iterate, source, wave_sq), "pack_inner"
    )
    halo = call(
        halo_kernel,
        packed,
        (info, band_keep, theirs, x_band, z_band, corner),
        "pack_halo",
        [low_tiles],
    )
    halo = swap(halo)
    planes, packs = (EXT, 32, LANES), (STRIDE, 32, LANES)
    own = (2, CX, CZ, LANES)
    in_vmem = pltpu.VMEM(own, jnp.float32)
    box_like, pack_like = (2, EXT + 2, 48, LANES), (2, STRIDE, 48, LANES)
    x_face, z_face = f32(HALO_ROW + 8, LANES), f32(2, 32, LANES)
    weights = call(
        weights_kernel,
        (f32(*planes),) * 4
        + (jax.ShapeDtypeStruct((MOVERS, 2 * LANES, 2 * LANES), jnp.bfloat16), packed),
        (info, band_keep, iterate, source, wave_sq, mine, x_band, z_band, corner),
        "weights",
        [low_tiles],
    )
    new, beside, x_a, x_b, z_first, z_last = call(
        relax_kernel,
        (in_vmem, f32(2, STRIDE, 32, LANES), x_face, x_face, z_face, z_face),
        (info, band_keep, iterate, x_band, z_band, corner, *weights, halo),
        "relax",
        [(2,) + low_tiles[1:], box_like, pack_like]
        + [packs] * 4
        + [(2,) + packs] * 2
        + [(2 * STRIDE * 32, LANES)]
        + [(2,) + planes] * 2
        + [(PER, 2 * STRIDE * 32, LANES)],
    )
    x_a, x_b = pairs(x_a, "gx", 0), pairs(x_b, "gx", 1)
    z_a, z_b = call(
        face_kernel,
        (z_face, z_face),
        (info, box_keep, z_first, z_last, x_a, x_b),
        "faces",
        [z_face.shape] * 2,
    )
    z_a, z_b = pairs(z_a, "gz", 0), pairs(z_b, "gz", 1)
    count = size_x * size_z * size_y
    residual, total = call(
        residual_kernel,
        (in_vmem, pltpu.VMEM((count, LANES), jnp.float32)),
        (info, box_keep, new, source, wave_sq, beside, x_a, x_b, z_a, z_b),
        "residual",
        [(2, CX + 2, 48, LANES), (2, STRIDE, 48, LANES), own, own, (2, STRIDE, CZ, LANES)]
        + [z_face.shape] * 2,
    )
    parts = lax.all_to_all(total, ("gx", "gz", "gy"), 0, 0, tiled=True)
    cells = 2 * CX * CZ * LANES * count
    norm = jnp.sqrt(jnp.sum(parts, axis=0)[:1] / cells)
    return new, residual, norm


def solution(mesh):
    in_specs = (
        P(None, "gx", "gz", "gy"),
        P(None, "gx", "gz", "gy"),
        P("gx", "gz", "gy"),
        P(),
        P("gx", "gz"),
    )
    out_specs = (P(None, "gx", "gz", "gy"), P(None, "gx", "gz", "gy"), P())
    return jax.shard_map(
        on_device, mesh=mesh, in_specs=in_specs, out_specs=out_specs, check_vma=False
    )
```

```python
import jax
import jax.numpy as jnp
from jax import lax
from jax.experimental import pallas as pl
from jax.experimental.pallas import tpu as pltpu
from jax.sharding import PartitionSpec as P

BAND = 4
PML = 8
SWEEPS = 10
OMEGA = 0.6
SIGMA = 6.0

CX = 24
CZ = 24
LANES = 128
EXT = CX + BAND
GROUP = 16
HALO = 11
OVER = GROUP - HALO
STRIDE = 4
MOVERS = (EXT // STRIDE + 1) // 2
LAYERS = 2 * BAND + 3 * (BAND - 1)
PER = EXT // STRIDE

HALO_ROW = 2 * CZ
SIDE_ROW = 26

MIB = 1024 * 1024

SMEM = pl.BlockSpec(memory_space=pltpu.SMEM)
VMEM = pl.BlockSpec(memory_space=pltpu.VMEM)
HBM = pl.BlockSpec(memory_space=pltpu.HBM)


def lane_ids():
    return lax.broadcasted_iota(jnp.int32, (8, LANES), 1)


def row_ids():
    return lax.broadcasted_iota(jnp.int32, (8, LANES), 0)


def flags(info, first):
    return [info[first + n].astype(jnp.float32) for n in range(4)]


def roll(value, shift):
    if isinstance(shift, int):
        shift = shift % LANES
        if shift == 0:
            return value
    return pltpu.roll(value, shift, 1)


def pair_sum(value):
    return roll(value, 1) + roll(value, -1)


def stencil_parts(centre, across, z_centre, z_across):
    both = across + z_centre
    part = 0.25 * z_across
    near = both + part
    return centre + 0.25 * (near + part), near


def layers(field):
    return 0 if field < 2 else 1


def layer_row(field, layer):
    return 4 * field + layer if field < 2 else 8 + 3 * (field - 2) + layer - 1


def bands_kernel(iterate, source, wave, x_out, z_out, corner_out, x_part, z_part, sems):
    fields = [iterate.at[0], iterate.at[1], source.at[0], source.at[1], wave]
    copies = [
        pltpu.make_async_copy(ref.at[pl.ds(CX - BAND, BAND)], x_part.at[f], sems.at[f])
        for f, ref in enumerate(fields)
    ]
    for f, ref in enumerate(fields):
        for piece in range(2):
            some = pl.ds(CX // 2 * piece, CX // 2)
            copies.append(
                pltpu.make_async_copy(
                    ref.at[some, pl.ds(CZ - 8, 8)], z_part.at[f, some], sems.at[5 + 2 * f + piece]
                )
            )
    for copy in copies:
        copy.start()
    for copy in copies:
        copy.wait()
    corner_out[...] = jnp.zeros_like(corner_out)
    for field in range(5):
        first = layers(field)
        depth = BAND - first
        for layer in range(first, BAND):
            row = layer_row(field, layer)
            x_out[row] = x_part[field, layer]
            corner_out[pl.ds(BAND * row, BAND), :] = x_part[field, layer, pl.ds(CZ - BAND, BAND), :]
        for x in range(CX):
            rows = pl.ds(LAYERS * x + layer_row(field, first), depth)
            z_out[rows, :] = z_part[field, x, pl.ds(8 - depth, depth), :]


def tile_of(fields, bands, corner_tiles, field, plane, tile, keep_x):
    if tile == 0:
        return corner_tiles[field, plane]
    rows = pl.ds(8 * (tile - 1), 8)
    if plane < BAND:
        if plane < layers(field):
            return jnp.zeros((8, LANES), jnp.float32)
        return bands[layer_row(field, plane), rows, :] * keep_x
    ref, index = fields[field]
    x = plane - BAND
    return ref[x, rows, :] if index is None else ref[index, x, rows, :]


def fill_low_tiles(low, z_band, corner, keep_x, keep_z, count=5):
    keep_both = keep_x * keep_z
    low[...] = jnp.zeros_like(low)
    for field in range(count):
        first = layers(field)
        depth = BAND - first
        for plane in range(EXT):
            to = pl.ds(8 - depth, depth)
            if plane >= BAND:
                rows = pl.ds(LAYERS * (plane - BAND) + layer_row(field, first), depth)
                low[field, plane, to, :] = z_band[rows, :] * keep_z
            elif plane >= first:
                rows = pl.ds(BAND * layer_row(field, plane) + first, depth)
                low[field, plane, to, :] = corner[rows, :] * keep_both


def own_layout(half):
    return OVER + (HALO - OVER) * half, HALO * half, OVER


def other_layout(half):
    return HALO - (HALO - OVER) * half, OVER * half, HALO


def join_lane(half):
    return OVER + (GROUP - 1 - 2 * OVER) * half


def pack(packed, values, layout):
    turn, least, count = layout
    lanes = lane_ids()
    place = lanes % GROUP
    wanted = (place >= least) & (place < least + count)
    turned = [(j, pltpu.roll(v, lax.rem(GROUP * j + turn, LANES), 1)) for j, v in values]
    for j, value in turned:
        packed = jnp.where(wanted & (lanes // GROUP == j), value, packed)
    return packed


def inner_halo_kernel(info, iterate, source, wave, theirs, mine):
    half = info[0]
    fields = [(iterate, 0), (iterate, 1), (source, 0), (source, 1), (wave, None)]
    zeros = jnp.zeros((8, LANES), jnp.float32)
    for field in range(5):
        for start in range(STRIDE):
            for tile in range(1, 4):
                values = [
                    (j, tile_of(fields, None, None, field, STRIDE * j + start, tile, None))
                    for j in range(1, PER)
                ]
                at = pl.ds(8 * tile, 8)
                theirs[field, start, at, :] = pack(zeros, values, other_layout(half))
                mine[field, start, at, :] = pack(zeros, values, own_layout(half))


def pack_bands(inner, out, low, x_band, keep_x, layout):
    for field in range(5):
        for start in range(STRIDE):
            values = [(j, low[field, STRIDE * j + start]) for j in range(PER)]
            zeros = jnp.zeros((8, LANES), jnp.float32)
            out[field, start, pl.ds(0, 8), :] = pack(zeros, values, layout)
            for tile in range(1, 4):
                at = pl.ds(8 * tile, 8)
                packed = inner[field, start, at, :]
                if start >= layers(field):
                    value = x_band[layer_row(field, start), pl.ds(8 * (tile - 1), 8), :] * keep_x
                    packed = pack(packed, [(0, value)], layout)
                out[field, start, at, :] = packed


def halo_kernel(info, inner, x_band, z_band, corner, out, low):
    keep = flags(info, 4)
    fill_low_tiles(low, z_band, corner, keep[0], keep[1])
    pack_bands(inner, out, low, x_band, keep[0], other_layout(info[0]))


def coefficients(wave_sq, s_re, s_im, sigma):
    diag = 5.0 - wave_sq
    scale = (0.5 * OMEGA) / (diag * diag + sigma * sigma)
    er = diag * scale
    ei = -sigma * scale
    return er, ei, 2.0 * (er * s_re - ei * s_im), 2.0 * (er * s_im + ei * s_re)


def sigma_z(tile, flag):
    if tile == 0:
        return jnp.zeros((8, LANES), jnp.float32)
    z = (row_ids() + 8 * (tile - 1)).astype(jnp.float32)
    ramp = jnp.maximum(z - (CZ - PML) + 1.0, 0.0) / PML
    return SIGMA * ramp * ramp * flag


def weights_kernel(
    info, iterate, source, wave, inner, x_band, z_band, corner,
    e_re, e_im, f_re, f_im, movers, mine, low,
):
    keep = flags(info, 4)
    half = info[0]
    keep_x = keep[0]
    lane = lax.broadcasted_iota(jnp.int32, (16, 2 * LANES), 1)
    row = lax.broadcasted_iota(jnp.int32, (16, 2 * LANES), 0)
    ends = lane % LANES == (LANES - 1) * (1 - half)
    for m in range(MOVERS):
        start = GROUP * (2 * m + lane // LANES) + join_lane(half)
        for first in range(0, 2 * LANES, 16):
            hit = ends & ((row + first) % LANES == start)
            movers[m, pl.ds(first, 16), :] = hit.astype(jnp.float32).astype(jnp.bfloat16)
    fill_low_tiles(low, z_band, corner, keep_x, keep[1])
    pack_bands(inner, mine, low, x_band, keep_x, own_layout(half))
    fields = [(iterate, 0), (iterate, 1), (source, 0), (source, 1), (wave, None)]
    zeros = jnp.zeros((8, LANES), jnp.float32)
    kept_rows = row_ids() < 5
    for tile in range(4):
        along_z = sigma_z(tile, keep[3])
        at = pl.ds(8 * tile, 8)
        for plane in range(EXT):
            values = [tile_of(fields, x_band, low, f, plane, tile, keep_x) for f in range(5)]
            w_re, w_im, s_re, s_im, wave_sq = values
            if plane == 0:
                er, ei, fr, fi = zeros, zeros, OMEGA * w_re, OMEGA * w_im
            else:
                ramp = max(plane - BAND - (CX - PML) + 1.0, 0.0) / PML
                sigma = along_z + SIGMA * ramp * ramp * keep[2]
                er, ei, fr, fi = coefficients(wave_sq, s_re, s_im, sigma)
                if tile == 0:
                    er = jnp.where(kept_rows, 0.0, er)
                    ei = jnp.where(kept_rows, 0.0, ei)
                    fr = jnp.where(kept_rows, OMEGA * w_re, fr)
                    fi = jnp.where(kept_rows, OMEGA * w_im, fi)
            e_re[plane, at, :] = er
            e_im[plane, at, :] = ei
            f_re[plane, at, :] = fr
            f_im[plane, at, :] = fi


def relax_kernel(
    info, iterate, x_band, z_band, corner, e_re, e_im, f_re, f_im, movers, mine, halo,
    own, beside, x_a, x_b, z_first, z_last,
    low, w, h, he_re, he_im, hf_re, hf_im, hq, hr, hs, mq, mr, sides,
):
    keep = flags(info, 4)
    half = info[0]
    active = info[1]
    odd = info[2]

    @pl.when(active == 0)
    def _():
        own[...] = iterate[...]
        beside[...] = halo[pl.ds(0, 2)]

    @pl.when(active == 1)
    def _():
        keep_x = keep[0]
        fill_low_tiles(low, z_band, corner, keep_x, keep[1], 2)
        fields = [(iterate, 0), (iterate, 1)]
        lanes = lane_ids()
        rows = row_ids()
        place = lanes % GROUP
        group = lanes // GROUP
        turn, least, count = own_layout(half)
        repeated = (place >= least) & (place < least + count)
        zeros = jnp.zeros((8, LANES), jnp.float32)
        for scratch in (w, h):
            scratch[...] = jnp.zeros_like(scratch)

        for tile in range(4):
            along_z = sigma_z(tile, keep[3])
            kept_rows = rows < 5
            at, inner = pl.ds(8 * tile, 8), pl.ds(8 + 8 * tile, 8)
            for plane in range(EXT):
                for part in range(2):
                    value = tile_of(fields, x_band, low, part, plane, tile, keep_x)
                    w[part, plane + 1, inner, :] = value
            for start in range(STRIDE):
                w_re, w_im, s_re, s_im, wave_sq = [
                    jnp.where(repeated, mine[f, start, at, :], halo[f, start, at, :])
                    for f in range(5)
                ]
                h[0, start, inner, :] = w_re
                h[1, start, inner, :] = w_im
                x = (STRIDE * group + start - BAND).astype(jnp.float32)
                ramp = jnp.maximum(x - (CX - PML) + 1.0, 0.0) / PML
                sigma = along_z + SIGMA * ramp * ramp * keep[2]
                er, ei, fr, fi = coefficients(wave_sq, s_re, s_im, sigma)
                kept = group == PER
                if start == 0:
                    kept = kept | (group == 0)
                if tile == 0:
                    kept = kept | kept_rows
                he_re[start, at, :] = jnp.where(kept, 0.0, er)
                he_im[start, at, :] = jnp.where(kept, 0.0, ei)
                hf_re[start, at, :] = jnp.where(kept, OMEGA * w_re, fr)
                hf_im[start, at, :] = jnp.where(kept, OMEGA * w_im, fi)

        first_lane = lanes == 0
        last_lane = lanes == LANES - 1
        def undamped(plane, tile):
            return plane < BAND + CX - PML and tile < 3

        def updated(w_re, w_im, t_re, t_im, er, ei, fr, fi):
            new_re = (1.0 - OMEGA) * w_re + fr
            new_im = (1.0 - OMEGA) * w_im + fi
            if ei is None:
                return new_re + er * t_re, new_im + er * t_im
            return new_re + (er * t_re - ei * t_im), new_im + (er * t_im + ei * t_re)

        def sweep():
            first = 1
            def centre_and_z(ref, part, plane, tile):
                base = 8 + 8 * tile
                return ref[part, plane, pl.ds(base, 8), :], (
                    ref[part, plane, pl.ds(base - 1, 8), :]
                    + ref[part, plane, pl.ds(base + 1, 8), :]
                )

            for tile in range(4):
                at = pl.ds(8 * tile, 8)
                for part in range(2):
                    both = [centre_and_z(h, part, s, tile) for s in range(STRIDE)]
                    below = [roll(value, GROUP) for value in both[-1]]
                    above = [roll(value, -GROUP) for value in both[0]]
                    both = [below] + both + [above]
                    for s in range(STRIDE):
                        q, near = stencil_parts(
                            both[s + 1][0], both[s][0] + both[s + 2][0],
                            both[s + 1][1], both[s][1] + both[s + 2][1],
                        )
                        hq[part, s, at, :] = q
                        hs[pl.ds(32 * (STRIDE * part + s) + 8 * tile, 8), :] = q
                        hr[part, s, at, :] = near

            value = hs[...]
            head = value.astype(jnp.bfloat16)
            tail = (value - head.astype(jnp.float32)).astype(jnp.bfloat16)
            both = jnp.concatenate([head, tail], 1)
            for m in range(MOVERS):
                moved = jnp.dot(both, movers[m], preferred_element_type=jnp.float32)
                sides[2 * m] = moved[:, :LANES]
                if 2 * m + 1 < PER:
                    sides[2 * m + 1] = moved[:, LANES:]

            for tile in range(4):
                at = pl.ds(8 * tile, 8)
                for part in range(2):
                    before = centre_and_z(w, part, first, tile)
                    here = centre_and_z(w, part, first + 1, tile)
                    for plane in range(first, EXT):
                        after = (zeros, zeros)
                        if plane + 1 < EXT:
                            after = centre_and_z(w, part, plane + 2, tile)
                        q, near = stencil_parts(
                            here[0], before[0] + after[0], here[1], before[1] + after[1]
                        )
                        mq[part, plane, at, :] = q
                        mr[part, plane, at, :] = near
                        before, here = here, after

            for tile in range(4):
                at = pl.ds(8 * tile, 8)
                base = 8 + 8 * tile
                for j in range(PER):
                    planes = range(max(STRIDE * j, first), STRIDE * (j + 1))
                    q = [[mq[part, plane, at, :] for part in range(2)] for plane in planes]
                    up = [[roll(value, -1) for value in pair] for pair in q]
                    down = [[roll(value, 1) for value in pair] for pair in q]
                    side = [
                        [
                            sides[j, pl.ds(32 * (STRIDE * part + plane % STRIDE) + 8 * tile, 8), :]
                            for part in range(2)
                        ]
                        for plane in planes
                    ]
                    for n, plane in enumerate(planes):
                        total = [
                            jnp.where(last_lane, side[n][part], up[n][part])
                            + jnp.where(first_lane, side[n][part], down[n][part])
                            + mr[part, plane, at, :]
                            for part in range(2)
                        ]
                        new_re, new_im = updated(
                            w[0, plane + 1, pl.ds(base, 8), :], w[1, plane + 1, pl.ds(base, 8), :],
                            total[0], total[1],
                            e_re[plane, at, :], None if undamped(plane, tile) else e_im[plane, at, :],
                            f_re[plane, at, :], f_im[plane, at, :],
                        )
                        w[0, plane + 1, pl.ds(base, 8), :] = new_re
                        w[1, plane + 1, pl.ds(base, 8), :] = new_im

            for tile in range(4):
                at = pl.ds(8 * tile, 8)
                base = 8 + 8 * tile
                total = [
                    [pair_sum(hq[part, s, at, :]) + hr[part, s, at, :] for part in range(2)]
                    for s in range(STRIDE)
                ]
                for s in range(STRIDE):
                    new_re, new_im = updated(
                        h[0, s, pl.ds(base, 8), :], h[1, s, pl.ds(base, 8), :],
                        total[s][0], total[s][1],
                        he_re[s, at, :], he_im[s, at, :],
                        hf_re[s, at, :], hf_im[s, at, :],
                    )
                    h[0, s, pl.ds(base, 8), :] = new_re
                    h[1, s, pl.ds(base, 8), :] = new_im

        def renew():
            for tile in range(4):
                at = pl.ds(8 + 8 * tile, 8)
                for part in range(2):
                    for s in range(STRIDE):
                        values = [(j, w[part, STRIDE * j + s + 1, at, :]) for j in range(PER)]
                        h[part, s, at, :] = pack(h[part, s, at, :], values, own_layout(half))

        def one_sweep(turn, carry):
            sweep()

            @pl.when(turn == SWEEPS // 2 - 1)
            def _():
                renew()

            return carry

        lax.fori_loop(0, SWEEPS, one_sweep, 0)
        for part in range(2):
            for x in range(CX):
                own[part, x] = w[part, x + BAND + 1, pl.ds(16, CZ), :]
            for s in range(STRIDE):
                beside[part, s] = h[part, s, pl.ds(8, 32), :]

    place_in = lane_ids() // GROUP
    for face, side in ((x_a, 1 - odd), (x_b, odd)):
        turned = [
            pltpu.roll(
                beside[n // 3, (STRIDE - 1) * side, pl.ds(8 + 8 * (n % 3), 8), :],
                lax.rem(LANES + GROUP * (n - 1 - (PER - 2) * side), LANES),
                1,
            )
            for n in range(6)
        ]
        packed = turned[0]
        for n in range(1, 6):
            packed = jnp.where(place_in == n, turned[n], packed)
        face[pl.ds(HALO_ROW, 8), :] = packed

    for part in range(2):
        for face, side in ((x_a, 1 - odd), (x_b, odd)):
            face[pl.ds(CZ * part, CZ), :] = own[part, (CX - 1) * side]
        for face, z in ((z_first, 0), (z_last, CZ - 1)):
            face[part, pl.ds(24, 8), :] = jnp.zeros((8, LANES), jnp.float32)
            for x in range(CX):
                face[part, pl.ds(x + 1, 1), :] = own[part, x, pl.ds(z, 1), :]
            for s in range(STRIDE):
                face[part, pl.ds(SIDE_ROW + s, 1), :] = beside[part, s, pl.ds(8 + z, 1), :]


def face_kernel(info, z_first, z_last, x_a, x_b, a_out, b_out, first, last):
    keep = flags(info, 8)
    odd_x = info[2] == 1
    odd_z = info[3] == 1
    group = lax.broadcasted_iota(jnp.int32, (1, LANES), 1) // GROUP
    for face, out, z in ((z_first, first, 0), (z_last, last, CZ - 1)):
        out[...] = face[...]
        for part in range(2):
            rows = [pl.ds(CZ * part + z, 1), pl.ds(HALO_ROW + z % 8, 1)]
            a, b = [[ref[row, :] for row in rows] for ref in (x_a, x_b)]
            piece = 3 * part + z // 8
            low = [jnp.where(odd_x, a[n], b[n]) * keep[0] for n in range(2)]
            high = [jnp.where(odd_x, b[n], a[n]) * keep[1] for n in range(2)]
            out[part, pl.ds(0, 1), :] = low[0]
            out[part, pl.ds(CX + 1, 1), :] = high[0]
            for s, value, to, turn in (
                (STRIDE - 1, low[1], 0, -GROUP * piece), (0, high[1], 7, GROUP * (7 - piece))
            ):
                at = pl.ds(SIDE_ROW + s, 1)
                out[part, at, :] = jnp.where(group == to, roll(value, turn), face[part, at, :])
    a_out[...] = jnp.where(odd_z, first[...], last[...])
    b_out[...] = jnp.where(odd_z, last[...], first[...])


def residual_kernel(
    info, field, source, wave, beside, x_a, x_b, z_a, z_b,
    out, total, box, sides, mq, mr, hs, z_low, z_high,
):
    keep = flags(info, 8)
    half = info[0]
    odd_x = info[2] == 1
    odd_z = info[3] == 1
    z_low[...] = jnp.where(odd_z, z_a[...], z_b[...])
    z_high[...] = jnp.where(odd_z, z_b[...], z_a[...])

    def x_sides(rows):
        a, b = x_a[rows, :], x_b[rows, :]
        return jnp.where(odd_x, a, b) * keep[0], jnp.where(odd_x, b, a) * keep[1]

    lanes = lane_ids()
    group = lanes // GROUP
    zeros = jnp.zeros((8, LANES), jnp.float32)
    low_halo, high_halo = x_sides(pl.ds(HALO_ROW, 8))
    for part in range(2):
        low, high = x_sides(pl.ds(CZ * part, CZ))
        box[part, 0, pl.ds(8, CZ), :] = low
        box[part, CX + 1, pl.ds(8, CZ), :] = high
        for x in range(CX):
            box[part, x + 1, pl.ds(8, CZ), :] = field[part, x]
        for x in range(CX + 2):
            box[part, x, pl.ds(7, 1), :] = z_low[part, pl.ds(x, 1), :] * keep[2]
            box[part, x, pl.ds(8 + CZ, 1), :] = z_high[part, pl.ds(x, 1), :] * keep[3]
        for s in range(STRIDE):
            row = pl.ds(SIDE_ROW + s, 1)
            sides[part, s, pl.ds(7, 1), :] = z_low[part, row, :] * keep[2]
            sides[part, s, pl.ds(8 + CZ, 1), :] = z_high[part, row, :] * keep[3]
            for tile in range(3):
                value = beside[part, s, pl.ds(8 + 8 * tile, 8), :]
                piece = 3 * part + tile
                if s == STRIDE - 1:
                    value = jnp.where(group == 0, roll(low_halo, -GROUP * piece), value)
                if s == 0:
                    value = jnp.where(group == 7, roll(high_halo, GROUP * (7 - piece)), value)
                sides[part, s, pl.ds(8 + 8 * tile, 8), :] = value

    def centre_and_z(ref, part, plane, tile):
        base = 8 + 8 * tile
        return ref[part, plane, pl.ds(base, 8), :], (
            ref[part, plane, pl.ds(base - 1, 8), :] + ref[part, plane, pl.ds(base + 1, 8), :]
        )

    joined = lanes % GROUP == join_lane(half)
    for part in range(2):
        for tile in range(3):
            at = pl.ds(8 * tile, 8)
            both = [centre_and_z(sides, part, s, tile) for s in range(STRIDE)]
            below = [roll(value, GROUP) for value in both[-1]]
            above = [roll(value, -GROUP) for value in both[0]]
            both = [below] + both + [above]
            for s in range(STRIDE):
                q, _ = stencil_parts(
                    both[s + 1][0], both[s][0] + both[s + 2][0],
                    both[s + 1][1], both[s][1] + both[s + 2][1],
                )
                hs[part, s, at, :] = jnp.where(joined, q, 0.0)

    for part in range(2):
        for tile in range(3):
            at = pl.ds(8 * tile, 8)
            before, here = centre_and_z(box, part, 0, tile), centre_and_z(box, part, 1, tile)
            for x in range(CX):
                after = centre_and_z(box, part, x + 2, tile)
                q, near = stencil_parts(
                    here[0], before[0] + after[0], here[1], before[1] + after[1]
                )
                mq[part, x, at, :] = q
                mr[part, x, at, :] = near
                before, here = here, after

    first_lane = lanes == 0
    last_lane = lanes == LANES - 1
    to_edge = (LANES - 1) * (1 - half) - join_lane(half)
    squares = [zeros] * 4
    for part in range(2):
        for tile in range(3):
            at = pl.ds(8 * tile, 8)
            for j in range(1, PER):
                turn = lax.rem(2 * LANES - GROUP * j + to_edge, LANES)
                planes = range(STRIDE * (j - 1), STRIDE * j)
                q = [mq[part, x, at, :] for x in planes]
                up = [roll(value, -1) for value in q]
                down = [roll(value, 1) for value in q]
                side = [pltpu.roll(hs[part, s, at, :], turn, 1) for s in range(STRIDE)]
                for n, x in enumerate(planes):
                    y = jnp.where(last_lane, side[n], up[n]) + jnp.where(
                        first_lane, side[n], down[n]
                    )
                    gap = (
                        source[part, x, at, :]
                        - (5.0 - wave[x, at, :]) * field[part, x, at, :]
                        + 0.5 * (y + mr[part, x, at, :])
                    )
                    out[part, x, at, :] = gap
                    squares[n] = squares[n] + gap * gap
    total[...] = jnp.broadcast_to(jnp.sum(sum(squares[1:], squares[0])), total.shape)


def f32(*shape):
    return jax.ShapeDtypeStruct(shape, jnp.float32)


def ring(value, axis, by):
    size = lax.axis_size(axis)
    return lax.ppermute(value, axis, [(i, (i + by) % size) for i in range(size)])


def pairs(value, axis, first):
    size = lax.axis_size(axis)
    moves = []
    for i in range(first, size, 2):
        j = (i + 1) % size
        moves += [(i, j), (j, i)]
    return lax.ppermute(value, axis, moves)


def diagonal(value, by_x, by_z):
    size_x, size_z = lax.axis_size("gx"), lax.axis_size("gz")
    pairs = [
        (x * size_z + z, ((x + by_x) % size_x) * size_z + (z + by_z) % size_z)
        for x in range(size_x)
        for z in range(size_z)
    ]
    return lax.ppermute(value, ("gx", "gz"), pairs)


def swap(value):
    return lax.ppermute(value, "gy", [(0, 1), (1, 0)])


def on_device(source, iterate, wave_sq, front, pml_flags):
    size_x, size_z, size_y = lax.axis_size("gx"), lax.axis_size("gz"), lax.axis_size("gy")
    at_x, at_z, half = lax.axis_index("gx"), lax.axis_index("gz"), lax.axis_index("gy")
    active = (jnp.mod(at_x + at_z - front[0], size_z) == 0).astype(jnp.int32)
    flag_bits = pml_flags[0, 0]
    info = jnp.stack(
        [
            half, active, at_x % 2, at_z % 2,
            at_x > 0, at_z > 0, flag_bits % 2, flag_bits // 2 % 2,
            at_x > 0, at_x < size_x - 1, at_z > 0, at_z < size_z - 1,
        ]
    ).astype(jnp.int32)

    def call(kernel, outs, ins, name, scratch=(), place=VMEM, sems=0):
        scalars = sum(value.ndim == 1 for value in ins)
        return pl.pallas_call(
            kernel,
            out_shape=outs,
            in_specs=[SMEM] * scalars + [place] * (len(ins) - scalars),
            out_specs=jax.tree.map(lambda _: VMEM, outs),
            scratch_shapes=[pltpu.VMEM(shape, jnp.float32) for shape in scratch]
            + [pltpu.SemaphoreType.DMA((sems,))] * (sems > 0),
            compiler_params=pltpu.CompilerParams(vmem_limit_bytes=20 * MIB),
            name=name,
        )(*ins)

    x_band, z_band, corner = call(
        bands_kernel,
        (f32(LAYERS, CZ, LANES), f32(LAYERS * CX, LANES), f32(72, LANES)),
        [pltpu.with_memory_space_constraint(v, pltpu.HBM) for v in (iterate, source, wave_sq)],
        "bands",
        [(5, BAND, CZ, LANES), (5, CX, 8, LANES)],
        place=HBM,
        sems=15,
    )
    corner = diagonal(corner, 1, 1)
    x_band = ring(x_band, "gx", 1)
    z_band = ring(z_band, "gz", 1)
    low_tiles = (5, EXT, 8, LANES)
    packed = f32(5, STRIDE, 32, LANES)
    theirs, mine = call(
        inner_halo_kernel, (packed, packed), (info, iterate, source, wave_sq), "pack_inner"
    )
    halo = call(
        halo_kernel,
        packed,
        (info, theirs, x_band, z_band, corner),
        "pack_halo",
        [low_tiles],
    )
    halo = swap(halo)
    planes, packs = (EXT, 32, LANES), (STRIDE, 32, LANES)
    own = (2, CX, CZ, LANES)
    in_vmem = pltpu.VMEM(own, jnp.float32)
    box_like, pack_like = (2, EXT + 2, 48, LANES), (2, STRIDE, 48, LANES)
    x_face, z_face = f32(HALO_ROW + 8, LANES), f32(2, 32, LANES)
    weights = call(
        weights_kernel,
        (f32(*planes),) * 4
        + (jax.ShapeDtypeStruct((MOVERS, 2 * LANES, 2 * LANES), jnp.bfloat16), packed),
        (info, iterate, source, wave_sq, mine, x_band, z_band, corner),
        "weights",
        [low_tiles],
    )
    new, beside, x_a, x_b, z_first, z_last = call(
        relax_kernel,
        (in_vmem, f32(2, STRIDE, 32, LANES), x_face, x_face, z_face, z_face),
        (info, iterate, x_band, z_band, corner, *weights, halo),
        "relax",
        [(2,) + low_tiles[1:], box_like, pack_like]
        + [packs] * 4
        + [(2,) + packs] * 2
        + [(2 * STRIDE * 32, LANES)]
        + [(2,) + planes] * 2
        + [(PER, 2 * STRIDE * 32, LANES)],
    )
    x_a, x_b = pairs(x_a, "gx", 0), pairs(x_b, "gx", 1)
    z_a, z_b = call(
        face_kernel,
        (z_face, z_face),
        (info, z_first, z_last, x_a, x_b),
        "faces",
        [z_face.shape] * 2,
    )
    z_a, z_b = pairs(z_a, "gz", 0), pairs(z_b, "gz", 1)
    count = size_x * size_z * size_y
    residual, total = call(
        residual_kernel,
        (in_vmem, pltpu.VMEM((count, LANES), jnp.float32)),
        (info, new, source, wave_sq, beside, x_a, x_b, z_a, z_b),
        "residual",
        [(2, CX + 2, 48, LANES), (2, STRIDE, 48, LANES), own, own, (2, STRIDE, CZ, LANES)]
        + [z_face.shape] * 2,
    )
    parts = lax.all_to_all(total, ("gx", "gz", "gy"), 0, 0, tiled=True)
    cells = 2 * CX * CZ * LANES * count
    norm = jnp.sqrt(jnp.sum(parts, axis=0)[:1] / cells)
    return new, residual, norm


def solution(mesh):
    in_specs = (
        P(None, "gx", "gz", "gy"),
        P(None, "gx", "gz", "gy"),
        P("gx", "gz", "gy"),
        P(),
        P("gx", "gz"),
    )
    out_specs = (P(None, "gx", "gz", "gy"), P(None, "gx", "gz", "gy"), P())
    return jax.shard_map(
        on_device, mesh=mesh, in_specs=in_specs, out_specs=out_specs, check_vma=False
    )
```

```python
import jax
import jax.numpy as jnp
from jax import lax
from jax.experimental import pallas as pl
from jax.experimental.pallas import tpu as pltpu
from jax.sharding import PartitionSpec as P

BAND = 4
PML = 8
SWEEPS = 10
OMEGA = 0.6
SIGMA = 6.0

CX = 24
CZ = 24
LANES = 128
EXT = CX + BAND
GROUP = 16
HALO = 11
OVER = GROUP - HALO
STRIDE = 4
MOVERS = (EXT // STRIDE + 1) // 2
LAYERS = 2 * BAND + 3 * (BAND - 1)
PER = EXT // STRIDE

HALO_ROW = 2 * CZ
SIDE_ROW = 26

MIB = 1024 * 1024

SMEM = pl.BlockSpec(memory_space=pltpu.SMEM)
VMEM = pl.BlockSpec(memory_space=pltpu.VMEM)
HBM = pl.BlockSpec(memory_space=pltpu.HBM)


def lane_ids():
    return lax.broadcasted_iota(jnp.int32, (8, LANES), 1)


def row_ids():
    return lax.broadcasted_iota(jnp.int32, (8, LANES), 0)


def flags(info, first):
    return [info[first + n].astype(jnp.float32) for n in range(4)]


def roll(value, shift):
    if isinstance(shift, int):
        shift = shift % LANES
        if shift == 0:
            return value
    return pltpu.roll(value, shift, 1)


def pair_sum(value):
    return roll(value, 1) + roll(value, -1)


def stencil_parts(centre, across, z_centre, z_across):
    both = across + z_centre
    part = 0.25 * z_across
    near = both + part
    return centre + 0.25 * (near + part), near


def layers(field):
    return 0 if field < 2 else 1


def layer_row(field, layer):
    return 4 * field + layer if field < 2 else 8 + 3 * (field - 2) + layer - 1


def bands_kernel(iterate, source, wave, x_out, z_out, corner_out, x_part, z_part, sems):
    fields = [iterate.at[0], iterate.at[1], source.at[0], source.at[1], wave]
    copies = [
        pltpu.make_async_copy(ref.at[pl.ds(CX - BAND, BAND)], x_part.at[f], sems.at[f])
        for f, ref in enumerate(fields)
    ]
    for f, ref in enumerate(fields):
        for piece in range(2):
            some = pl.ds(CX // 2 * piece, CX // 2)
            copies.append(
                pltpu.make_async_copy(
                    ref.at[some, pl.ds(CZ - 8, 8)], z_part.at[f, some], sems.at[5 + 2 * f + piece]
                )
            )
    for copy in copies:
        copy.start()
    for copy in copies:
        copy.wait()
    corner_out[...] = jnp.zeros_like(corner_out)
    for field in range(5):
        first = layers(field)
        depth = BAND - first
        for layer in range(first, BAND):
            row = layer_row(field, layer)
            x_out[row] = x_part[field, layer]
            corner_out[pl.ds(BAND * row, BAND), :] = x_part[field, layer, pl.ds(CZ - BAND, BAND), :]
        for x in range(CX):
            rows = pl.ds(LAYERS * x + layer_row(field, first), depth)
            z_out[rows, :] = z_part[field, x, pl.ds(8 - depth, depth), :]


def tile_of(fields, bands, corner_tiles, field, plane, tile, keep_x):
    if tile == 0:
        return corner_tiles[field, plane]
    rows = pl.ds(8 * (tile - 1), 8)
    if plane < BAND:
        if plane < layers(field):
            return jnp.zeros((8, LANES), jnp.float32)
        return bands[layer_row(field, plane), rows, :] * keep_x
    ref, index = fields[field]
    x = plane - BAND
    return ref[x, rows, :] if index is None else ref[index, x, rows, :]


def fill_low_tiles(low, z_band, corner, keep_x, keep_z, count=5):
    keep_both = keep_x * keep_z
    low[...] = jnp.zeros_like(low)
    for field in range(count):
        first = layers(field)
        depth = BAND - first
        for plane in range(EXT):
            to = pl.ds(8 - depth, depth)
            if plane >= BAND:
                rows = pl.ds(LAYERS * (plane - BAND) + layer_row(field, first), depth)
                low[field, plane, to, :] = z_band[rows, :] * keep_z
            elif plane >= first:
                rows = pl.ds(BAND * layer_row(field, plane) + first, depth)
                low[field, plane, to, :] = corner[rows, :] * keep_both


def own_layout(half):
    return OVER + (HALO - OVER) * half, HALO * half, OVER


def other_layout(half):
    return HALO - (HALO - OVER) * half, OVER * half, HALO


def join_lane(half):
    return OVER + (GROUP - 1 - 2 * OVER) * half


def pack(packed, values, layout):
    turn, least, count = layout
    lanes = lane_ids()
    place = lanes % GROUP
    wanted = (place >= least) & (place < least + count)
    turned = [(j, pltpu.roll(v, lax.rem(GROUP * j + turn, LANES), 1)) for j, v in values]
    for j, value in turned:
        packed = jnp.where(wanted & (lanes // GROUP == j), value, packed)
    return packed


def inner_halo_kernel(info, iterate, source, wave, theirs, mine, movers):
    half = info[0]
    lane = lax.broadcasted_iota(jnp.int32, (16, 2 * LANES), 1)
    row = lax.broadcasted_iota(jnp.int32, (16, 2 * LANES), 0)
    ends = lane % LANES == (LANES - 1) * (1 - half)
    for m in range(MOVERS):
        start = GROUP * (2 * m + lane // LANES) + join_lane(half)
        for first in range(0, 2 * LANES, 16):
            hit = ends & ((row + first) % LANES == start)
            movers[m, pl.ds(first, 16), :] = hit.astype(jnp.float32).astype(jnp.bfloat16)
    fields = [(iterate, 0), (iterate, 1), (source, 0), (source, 1), (wave, None)]
    zeros = jnp.zeros((8, LANES), jnp.float32)
    for field in range(5):
        for start in range(STRIDE):
            for tile in range(1, 4):
                values = [
                    (j, tile_of(fields, None, None, field, STRIDE * j + start, tile, None))
                    for j in range(1, PER)
                ]
                at = pl.ds(8 * tile, 8)
                theirs[field, start, at, :] = pack(zeros, values, other_layout(half))
                mine[field, start, at, :] = pack(zeros, values, own_layout(half))


def pack_bands(inner, out, low, x_band, keep_x, layout):
    for field in range(5):
        for start in range(STRIDE):
            values = [(j, low[field, STRIDE * j + start]) for j in range(PER)]
            zeros = jnp.zeros((8, LANES), jnp.float32)
            out[field, start, pl.ds(0, 8), :] = pack(zeros, values, layout)
            for tile in range(1, 4):
                at = pl.ds(8 * tile, 8)
                packed = inner[field, start, at, :]
                if start >= layers(field):
                    value = x_band[layer_row(field, start), pl.ds(8 * (tile - 1), 8), :] * keep_x
                    packed = pack(packed, [(0, value)], layout)
                out[field, start, at, :] = packed


def halo_kernel(info, inner, x_band, z_band, corner, out, low):
    keep = flags(info, 4)
    fill_low_tiles(low, z_band, corner, keep[0], keep[1])
    pack_bands(inner, out, low, x_band, keep[0], other_layout(info[0]))


def coefficients(wave_sq, s_re, s_im, sigma):
    diag = 5.0 - wave_sq
    scale = (0.5 * OMEGA) / (diag * diag + sigma * sigma)
    er = diag * scale
    ei = -sigma * scale
    return er, ei, 2.0 * (er * s_re - ei * s_im), 2.0 * (er * s_im + ei * s_re)


def sigma_z(tile, flag):
    if tile == 0:
        return jnp.zeros((8, LANES), jnp.float32)
    z = (row_ids() + 8 * (tile - 1)).astype(jnp.float32)
    ramp = jnp.maximum(z - (CZ - PML) + 1.0, 0.0) / PML
    return SIGMA * ramp * ramp * flag


def weights_kernel(
    info, iterate, source, wave, inner, x_band, z_band, corner,
    e_re, e_im, f_re, f_im, mine, low,
):
    keep = flags(info, 4)
    half = info[0]
    keep_x = keep[0]
    fill_low_tiles(low, z_band, corner, keep_x, keep[1])
    pack_bands(inner, mine, low, x_band, keep_x, own_layout(half))
    fields = [(iterate, 0), (iterate, 1), (source, 0), (source, 1), (wave, None)]
    zeros = jnp.zeros((8, LANES), jnp.float32)
    kept_rows = row_ids() < 5
    for tile in range(4):
        along_z = sigma_z(tile, keep[3])
        at = pl.ds(8 * tile, 8)
        for plane in range(EXT):
            values = [tile_of(fields, x_band, low, f, plane, tile, keep_x) for f in range(5)]
            w_re, w_im, s_re, s_im, wave_sq = values
            if plane == 0:
                er, ei, fr, fi = zeros, zeros, OMEGA * w_re, OMEGA * w_im
            else:
                ramp = max(plane - BAND - (CX - PML) + 1.0, 0.0) / PML
                sigma = along_z + SIGMA * ramp * ramp * keep[2]
                er, ei, fr, fi = coefficients(wave_sq, s_re, s_im, sigma)
                if tile == 0:
                    er = jnp.where(kept_rows, 0.0, er)
                    ei = jnp.where(kept_rows, 0.0, ei)
                    fr = jnp.where(kept_rows, OMEGA * w_re, fr)
                    fi = jnp.where(kept_rows, OMEGA * w_im, fi)
            e_re[plane, at, :] = er
            e_im[plane, at, :] = ei
            f_re[plane, at, :] = fr
            f_im[plane, at, :] = fi


def relax_kernel(
    info, iterate, x_band, z_band, corner, e_re, e_im, f_re, f_im, movers, mine, halo,
    own, beside, x_a, x_b, z_first, z_last,
    low, w, h, he_re, he_im, hf_re, hf_im, hq, hr, hs, mq, mr, sides,
):
    keep = flags(info, 4)
    half = info[0]
    active = info[1]
    odd = info[2]

    @pl.when(active == 0)
    def _():
        own[...] = iterate[...]
        beside[...] = halo[pl.ds(0, 2)]

    @pl.when(active == 1)
    def _():
        keep_x = keep[0]
        fill_low_tiles(low, z_band, corner, keep_x, keep[1], 2)
        fields = [(iterate, 0), (iterate, 1)]
        lanes = lane_ids()
        rows = row_ids()
        place = lanes % GROUP
        group = lanes // GROUP
        turn, least, count = own_layout(half)
        repeated = (place >= least) & (place < least + count)
        zeros = jnp.zeros((8, LANES), jnp.float32)
        for scratch in (w, h):
            scratch[...] = jnp.zeros_like(scratch)

        for tile in range(4):
            along_z = sigma_z(tile, keep[3])
            kept_rows = rows < 5
            at, inner = pl.ds(8 * tile, 8), pl.ds(8 + 8 * tile, 8)
            for plane in range(EXT):
                for part in range(2):
                    value = tile_of(fields, x_band, low, part, plane, tile, keep_x)
                    w[part, plane + 1, inner, :] = value
            for start in range(STRIDE):
                w_re, w_im, s_re, s_im, wave_sq = [
                    jnp.where(repeated, mine[f, start, at, :], halo[f, start, at, :])
                    for f in range(5)
                ]
                h[0, start, inner, :] = w_re
                h[1, start, inner, :] = w_im
                x = (STRIDE * group + start - BAND).astype(jnp.float32)
                ramp = jnp.maximum(x - (CX - PML) + 1.0, 0.0) / PML
                sigma = along_z + SIGMA * ramp * ramp * keep[2]
                er, ei, fr, fi = coefficients(wave_sq, s_re, s_im, sigma)
                kept = group == PER
                if start == 0:
                    kept = kept | (group == 0)
                if tile == 0:
                    kept = kept | kept_rows
                he_re[start, at, :] = jnp.where(kept, 0.0, er)
                he_im[start, at, :] = jnp.where(kept, 0.0, ei)
                hf_re[start, at, :] = jnp.where(kept, OMEGA * w_re, fr)
                hf_im[start, at, :] = jnp.where(kept, OMEGA * w_im, fi)

        first_lane = lanes == 0
        last_lane = lanes == LANES - 1
        def undamped(plane, tile):
            return plane < BAND + CX - PML and tile < 3

        def updated(w_re, w_im, t_re, t_im, er, ei, fr, fi):
            new_re = (1.0 - OMEGA) * w_re + fr
            new_im = (1.0 - OMEGA) * w_im + fi
            if ei is None:
                return new_re + er * t_re, new_im + er * t_im
            return new_re + (er * t_re - ei * t_im), new_im + (er * t_im + ei * t_re)

        def sweep():
            first = 1
            def centre_and_z(ref, part, plane, tile):
                base = 8 + 8 * tile
                return ref[part, plane, pl.ds(base, 8), :], (
                    ref[part, plane, pl.ds(base - 1, 8), :]
                    + ref[part, plane, pl.ds(base + 1, 8), :]
                )

            for tile in range(4):
                at = pl.ds(8 * tile, 8)
                for part in range(2):
                    both = [centre_and_z(h, part, s, tile) for s in range(STRIDE)]
                    below = [roll(value, GROUP) for value in both[-1]]
                    above = [roll(value, -GROUP) for value in both[0]]
                    both = [below] + both + [above]
                    for s in range(STRIDE):
                        q, near = stencil_parts(
                            both[s + 1][0], both[s][0] + both[s + 2][0],
                            both[s + 1][1], both[s][1] + both[s + 2][1],
                        )
                        hq[part, s, at, :] = q
                        hs[pl.ds(32 * (STRIDE * part + s) + 8 * tile, 8), :] = q
                        hr[part, s, at, :] = near

            value = hs[...]
            head = value.astype(jnp.bfloat16)
            tail = (value - head.astype(jnp.float32)).astype(jnp.bfloat16)
            both = jnp.concatenate([head, tail], 1)
            for m in range(MOVERS):
                moved = jnp.dot(both, movers[m], preferred_element_type=jnp.float32)
                sides[2 * m] = moved[:, :LANES]
                if 2 * m + 1 < PER:
                    sides[2 * m + 1] = moved[:, LANES:]

            for tile in range(4):
                at = pl.ds(8 * tile, 8)
                for part in range(2):
                    before = centre_and_z(w, part, first, tile)
                    here = centre_and_z(w, part, first + 1, tile)
                    for plane in range(first, EXT):
                        after = (zeros, zeros)
                        if plane + 1 < EXT:
                            after = centre_and_z(w, part, plane + 2, tile)
                        q, near = stencil_parts(
                            here[0], before[0] + after[0], here[1], before[1] + after[1]
                        )
                        mq[part, plane, at, :] = q
                        mr[part, plane, at, :] = near
                        before, here = here, after

            for tile in range(4):
                at = pl.ds(8 * tile, 8)
                base = 8 + 8 * tile
                for j in range(PER):
                    planes = range(max(STRIDE * j, first), STRIDE * (j + 1))
                    q = [[mq[part, plane, at, :] for part in range(2)] for plane in planes]
                    up = [[roll(value, -1) for value in pair] for pair in q]
                    down = [[roll(value, 1) for value in pair] for pair in q]
                    side = [
                        [
                            sides[j, pl.ds(32 * (STRIDE * part + plane % STRIDE) + 8 * tile, 8), :]
                            for part in range(2)
                        ]
                        for plane in planes
                    ]
                    for n, plane in enumerate(planes):
                        total = [
                            jnp.where(last_lane, side[n][part], up[n][part])
                            + jnp.where(first_lane, side[n][part], down[n][part])
                            + mr[part, plane, at, :]
                            for part in range(2)
                        ]
                        new_re, new_im = updated(
                            w[0, plane + 1, pl.ds(base, 8), :], w[1, plane + 1, pl.ds(base, 8), :],
                            total[0], total[1],
                            e_re[plane, at, :], None if undamped(plane, tile) else e_im[plane, at, :],
                            f_re[plane, at, :], f_im[plane, at, :],
                        )
                        w[0, plane + 1, pl.ds(base, 8), :] = new_re
                        w[1, plane + 1, pl.ds(base, 8), :] = new_im

            for tile in range(4):
                at = pl.ds(8 * tile, 8)
                base = 8 + 8 * tile
                total = [
                    [pair_sum(hq[part, s, at, :]) + hr[part, s, at, :] for part in range(2)]
                    for s in range(STRIDE)
                ]
                for s in range(STRIDE):
                    new_re, new_im = updated(
                        h[0, s, pl.ds(base, 8), :], h[1, s, pl.ds(base, 8), :],
                        total[s][0], total[s][1],
                        he_re[s, at, :], he_im[s, at, :],
                        hf_re[s, at, :], hf_im[s, at, :],
                    )
                    h[0, s, pl.ds(base, 8), :] = new_re
                    h[1, s, pl.ds(base, 8), :] = new_im

        def renew():
            for tile in range(4):
                at = pl.ds(8 + 8 * tile, 8)
                for part in range(2):
                    for s in range(STRIDE):
                        values = [(j, w[part, STRIDE * j + s + 1, at, :]) for j in range(PER)]
                        h[part, s, at, :] = pack(h[part, s, at, :], values, own_layout(half))

        def one_sweep(turn, carry):
            sweep()

            @pl.when(turn == SWEEPS // 2 - 1)
            def _():
                renew()

            return carry

        lax.fori_loop(0, SWEEPS, one_sweep, 0)
        for part in range(2):
            for x in range(CX):
                own[part, x] = w[part, x + BAND + 1, pl.ds(16, CZ), :]
            for s in range(STRIDE):
                beside[part, s] = h[part, s, pl.ds(8, 32), :]

    place_in = lane_ids() // GROUP
    for face, side in ((x_a, 1 - odd), (x_b, odd)):
        turned = [
            pltpu.roll(
                beside[n // 3, (STRIDE - 1) * side, pl.ds(8 + 8 * (n % 3), 8), :],
                lax.rem(LANES + GROUP * (n - 1 - (PER - 2) * side), LANES),
                1,
            )
            for n in range(6)
        ]
        packed = turned[0]
        for n in range(1, 6):
            packed = jnp.where(place_in == n, turned[n], packed)
        face[pl.ds(HALO_ROW, 8), :] = packed

    for part in range(2):
        for face, side in ((x_a, 1 - odd), (x_b, odd)):
            face[pl.ds(CZ * part, CZ), :] = own[part, (CX - 1) * side]
        for face, z in ((z_first, 0), (z_last, CZ - 1)):
            face[part, pl.ds(24, 8), :] = jnp.zeros((8, LANES), jnp.float32)
            for x in range(CX):
                face[part, pl.ds(x + 1, 1), :] = own[part, x, pl.ds(z, 1), :]
            for s in range(STRIDE):
                face[part, pl.ds(SIDE_ROW + s, 1), :] = beside[part, s, pl.ds(8 + z, 1), :]


def face_kernel(info, z_first, z_last, x_a, x_b, a_out, b_out, first, last):
    keep = flags(info, 8)
    odd_x = info[2] == 1
    odd_z = info[3] == 1
    group = lax.broadcasted_iota(jnp.int32, (1, LANES), 1) // GROUP
    for face, out, z in ((z_first, first, 0), (z_last, last, CZ - 1)):
        out[...] = face[...]
        for part in range(2):
            rows = [pl.ds(CZ * part + z, 1), pl.ds(HALO_ROW + z % 8, 1)]
            a, b = [[ref[row, :] for row in rows] for ref in (x_a, x_b)]
            piece = 3 * part + z // 8
            low = [jnp.where(odd_x, a[n], b[n]) * keep[0] for n in range(2)]
            high = [jnp.where(odd_x, b[n], a[n]) * keep[1] for n in range(2)]
            out[part, pl.ds(0, 1), :] = low[0]
            out[part, pl.ds(CX + 1, 1), :] = high[0]
            for s, value, to, turn in (
                (STRIDE - 1, low[1], 0, -GROUP * piece), (0, high[1], 7, GROUP * (7 - piece))
            ):
                at = pl.ds(SIDE_ROW + s, 1)
                out[part, at, :] = jnp.where(group == to, roll(value, turn), face[part, at, :])
    a_out[...] = jnp.where(odd_z, first[...], last[...])
    b_out[...] = jnp.where(odd_z, last[...], first[...])


def residual_kernel(
    info, field, source, wave, beside, x_a, x_b, z_a, z_b,
    out, total, box, sides, mq, mr, hs, z_low, z_high,
):
    keep = flags(info, 8)
    half = info[0]
    odd_x = info[2] == 1
    odd_z = info[3] == 1
    z_low[...] = jnp.where(odd_z, z_a[...], z_b[...])
    z_high[...] = jnp.where(odd_z, z_b[...], z_a[...])

    def x_sides(rows):
        a, b = x_a[rows, :], x_b[rows, :]
        return jnp.where(odd_x, a, b) * keep[0], jnp.where(odd_x, b, a) * keep[1]

    lanes = lane_ids()
    group = lanes // GROUP
    zeros = jnp.zeros((8, LANES), jnp.float32)
    low_halo, high_halo = x_sides(pl.ds(HALO_ROW, 8))
    for part in range(2):
        low, high = x_sides(pl.ds(CZ * part, CZ))
        box[part, 0, pl.ds(8, CZ), :] = low
        box[part, CX + 1, pl.ds(8, CZ), :] = high
        for x in range(CX):
            box[part, x + 1, pl.ds(8, CZ), :] = field[part, x]
        for x in range(CX + 2):
            box[part, x, pl.ds(7, 1), :] = z_low[part, pl.ds(x, 1), :] * keep[2]
            box[part, x, pl.ds(8 + CZ, 1), :] = z_high[part, pl.ds(x, 1), :] * keep[3]
        for s in range(STRIDE):
            row = pl.ds(SIDE_ROW + s, 1)
            sides[part, s, pl.ds(7, 1), :] = z_low[part, row, :] * keep[2]
            sides[part, s, pl.ds(8 + CZ, 1), :] = z_high[part, row, :] * keep[3]
            for tile in range(3):
                value = beside[part, s, pl.ds(8 + 8 * tile, 8), :]
                piece = 3 * part + tile
                if s == STRIDE - 1:
                    value = jnp.where(group == 0, roll(low_halo, -GROUP * piece), value)
                if s == 0:
                    value = jnp.where(group == 7, roll(high_halo, GROUP * (7 - piece)), value)
                sides[part, s, pl.ds(8 + 8 * tile, 8), :] = value

    def centre_and_z(ref, part, plane, tile):
        base = 8 + 8 * tile
        return ref[part, plane, pl.ds(base, 8), :], (
            ref[part, plane, pl.ds(base - 1, 8), :] + ref[part, plane, pl.ds(base + 1, 8), :]
        )

    joined = lanes % GROUP == join_lane(half)
    for part in range(2):
        for tile in range(3):
            at = pl.ds(8 * tile, 8)
            both = [centre_and_z(sides, part, s, tile) for s in range(STRIDE)]
            below = [roll(value, GROUP) for value in both[-1]]
            above = [roll(value, -GROUP) for value in both[0]]
            both = [below] + both + [above]
            for s in range(STRIDE):
                q, _ = stencil_parts(
                    both[s + 1][0], both[s][0] + both[s + 2][0],
                    both[s + 1][1], both[s][1] + both[s + 2][1],
                )
                hs[part, s, at, :] = jnp.where(joined, q, 0.0)

    for part in range(2):
        for tile in range(3):
            at = pl.ds(8 * tile, 8)
            before, here = centre_and_z(box, part, 0, tile), centre_and_z(box, part, 1, tile)
            for x in range(CX):
                after = centre_and_z(box, part, x + 2, tile)
                q, near = stencil_parts(
                    here[0], before[0] + after[0], here[1], before[1] + after[1]
                )
                mq[part, x, at, :] = q
                mr[part, x, at, :] = near
                before, here = here, after

    first_lane = lanes == 0
    last_lane = lanes == LANES - 1
    to_edge = (LANES - 1) * (1 - half) - join_lane(half)
    squares = [zeros] * 4
    for part in range(2):
        for tile in range(3):
            at = pl.ds(8 * tile, 8)
            for j in range(1, PER):
                turn = lax.rem(2 * LANES - GROUP * j + to_edge, LANES)
                planes = range(STRIDE * (j - 1), STRIDE * j)
                q = [mq[part, x, at, :] for x in planes]
                up = [roll(value, -1) for value in q]
                down = [roll(value, 1) for value in q]
                side = [pltpu.roll(hs[part, s, at, :], turn, 1) for s in range(STRIDE)]
                for n, x in enumerate(planes):
                    y = jnp.where(last_lane, side[n], up[n]) + jnp.where(
                        first_lane, side[n], down[n]
                    )
                    gap = (
                        source[part, x, at, :]
                        - (5.0 - wave[x, at, :]) * field[part, x, at, :]
                        + 0.5 * (y + mr[part, x, at, :])
                    )
                    out[part, x, at, :] = gap
                    squares[n] = squares[n] + gap * gap
    total[...] = jnp.broadcast_to(jnp.sum(sum(squares[1:], squares[0])), total.shape)


def f32(*shape):
    return jax.ShapeDtypeStruct(shape, jnp.float32)


def ring(value, axis, by):
    size = lax.axis_size(axis)
    return lax.ppermute(value, axis, [(i, (i + by) % size) for i in range(size)])


def pairs(value, axis, first):
    size = lax.axis_size(axis)
    moves = []
    for i in range(first, size, 2):
        j = (i + 1) % size
        moves += [(i, j), (j, i)]
    return lax.ppermute(value, axis, moves)


def diagonal(value, by_x, by_z):
    size_x, size_z = lax.axis_size("gx"), lax.axis_size("gz")
    pairs = [
        (x * size_z + z, ((x + by_x) % size_x) * size_z + (z + by_z) % size_z)
        for x in range(size_x)
        for z in range(size_z)
    ]
    return lax.ppermute(value, ("gx", "gz"), pairs)


def swap(value):
    return lax.ppermute(value, "gy", [(0, 1), (1, 0)])


def on_device(source, iterate, wave_sq, front, pml_flags):
    size_x, size_z, size_y = lax.axis_size("gx"), lax.axis_size("gz"), lax.axis_size("gy")
    at_x, at_z, half = lax.axis_index("gx"), lax.axis_index("gz"), lax.axis_index("gy")
    active = (jnp.mod(at_x + at_z - front[0], size_z) == 0).astype(jnp.int32)
    flag_bits = pml_flags[0, 0]
    info = jnp.stack(
        [
            half, active, at_x % 2, at_z % 2,
            at_x > 0, at_z > 0, flag_bits % 2, flag_bits // 2 % 2,
            at_x > 0, at_x < size_x - 1, at_z > 0, at_z < size_z - 1,
        ]
    ).astype(jnp.int32)

    def call(kernel, outs, ins, name, scratch=(), place=VMEM, sems=0):
        scalars = sum(value.ndim == 1 for value in ins)
        return pl.pallas_call(
            kernel,
            out_shape=outs,
            in_specs=[SMEM] * scalars + [place] * (len(ins) - scalars),
            out_specs=jax.tree.map(lambda _: VMEM, outs),
            scratch_shapes=[pltpu.VMEM(shape, jnp.float32) for shape in scratch]
            + [pltpu.SemaphoreType.DMA((sems,))] * (sems > 0),
            compiler_params=pltpu.CompilerParams(vmem_limit_bytes=20 * MIB),
            name=name,
        )(*ins)

    x_band, z_band, corner = call(
        bands_kernel,
        (f32(LAYERS, CZ, LANES), f32(LAYERS * CX, LANES), f32(72, LANES)),
        [pltpu.with_memory_space_constraint(v, pltpu.HBM) for v in (iterate, source, wave_sq)],
        "bands",
        [(5, BAND, CZ, LANES), (5, CX, 8, LANES)],
        place=HBM,
        sems=15,
    )
    corner = diagonal(corner, 1, 1)
    x_band = ring(x_band, "gx", 1)
    z_band = ring(z_band, "gz", 1)
    low_tiles = (5, EXT, 8, LANES)
    packed = f32(5, STRIDE, 32, LANES)
    moves = jax.ShapeDtypeStruct((MOVERS, 2 * LANES, 2 * LANES), jnp.bfloat16)
    theirs, mine, movers = call(
        inner_halo_kernel, (packed, packed, moves), (info, iterate, source, wave_sq), "pack_inner"
    )
    halo = call(
        halo_kernel,
        packed,
        (info, theirs, x_band, z_band, corner),
        "pack_halo",
        [low_tiles],
    )
    halo = swap(halo)
    planes, packs = (EXT, 32, LANES), (STRIDE, 32, LANES)
    own = (2, CX, CZ, LANES)
    in_vmem = pltpu.VMEM(own, jnp.float32)
    box_like, pack_like = (2, EXT + 2, 48, LANES), (2, STRIDE, 48, LANES)
    x_face, z_face = f32(HALO_ROW + 8, LANES), f32(2, 32, LANES)
    *weights, mine = call(
        weights_kernel,
        (f32(*planes),) * 4 + (packed,),
        (info, iterate, source, wave_sq, mine, x_band, z_band, corner),
        "weights",
        [low_tiles],
    )
    new, beside, x_a, x_b, z_first, z_last = call(
        relax_kernel,
        (in_vmem, f32(2, STRIDE, 32, LANES), x_face, x_face, z_face, z_face),
        (info, iterate, x_band, z_band, corner, *weights, movers, mine, halo),
        "relax",
        [(2,) + low_tiles[1:], box_like, pack_like]
        + [packs] * 4
        + [(2,) + packs] * 2
        + [(2 * STRIDE * 32, LANES)]
        + [(2,) + planes] * 2
        + [(PER, 2 * STRIDE * 32, LANES)],
    )
    x_a, x_b = pairs(x_a, "gx", 0), pairs(x_b, "gx", 1)
    z_a, z_b = call(
        face_kernel,
        (z_face, z_face),
        (info, z_first, z_last, x_a, x_b),
        "faces",
        [z_face.shape] * 2,
    )
    z_a, z_b = pairs(z_a, "gz", 0), pairs(z_b, "gz", 1)
    count = size_x * size_z * size_y
    residual, total = call(
        residual_kernel,
        (in_vmem, pltpu.VMEM((count, LANES), jnp.float32)),
        (info, new, source, wave_sq, beside, x_a, x_b, z_a, z_b),
        "residual",
        [(2, CX + 2, 48, LANES), (2, STRIDE, 48, LANES), own, own, (2, STRIDE, CZ, LANES)]
        + [z_face.shape] * 2,
    )
    parts = lax.all_to_all(total, ("gx", "gz", "gy"), 0, 0, tiled=True)
    cells = 2 * CX * CZ * LANES * count
    norm = jnp.sqrt(jnp.sum(parts, axis=0)[:1] / cells)
    return new, residual, norm


def solution(mesh):
    in_specs = (
        P(None, "gx", "gz", "gy"),
        P(None, "gx", "gz", "gy"),
        P("gx", "gz", "gy"),
        P(),
        P("gx", "gz"),
    )
    out_specs = (P(None, "gx", "gz", "gy"), P(None, "gx", "gz", "gy"), P())
    return jax.shard_map(
        on_device, mesh=mesh, in_specs=in_specs, out_specs=out_specs, check_vma=False
    )
```

```python
import jax
import jax.numpy as jnp
from jax import lax
from jax.experimental import pallas as pl
from jax.experimental.pallas import tpu as pltpu
from jax.sharding import PartitionSpec as P

BAND = 4
PML = 8
SWEEPS = 10
OMEGA = 0.6
SIGMA = 6.0

CX = 24
CZ = 24
LANES = 128
EXT = CX + BAND
GROUP = 16
HALO = 11
OVER = GROUP - HALO
STRIDE = 4
MOVERS = (EXT // STRIDE + 1) // 2
LAYERS = 2 * BAND + 3 * (BAND - 1)
PER = EXT // STRIDE

HALO_ROW = 2 * CZ
SIDE_ROW = 26

MIB = 1024 * 1024

SMEM = pl.BlockSpec(memory_space=pltpu.SMEM)
VMEM = pl.BlockSpec(memory_space=pltpu.VMEM)
HBM = pl.BlockSpec(memory_space=pltpu.HBM)


def lane_ids():
    return lax.broadcasted_iota(jnp.int32, (8, LANES), 1)


def row_ids():
    return lax.broadcasted_iota(jnp.int32, (8, LANES), 0)


def flags(info, first):
    return [info[first + n].astype(jnp.float32) for n in range(4)]


def roll(value, shift):
    if isinstance(shift, int):
        shift = shift % LANES
        if shift == 0:
            return value
    return pltpu.roll(value, shift, 1)


def pair_sum(value):
    return roll(value, 1) + roll(value, -1)


def stencil_parts(centre, across, z_centre, z_across):
    both = across + z_centre
    part = 0.25 * z_across
    near = both + part
    return centre + 0.25 * (near + part), near


def layers(field):
    return 0 if field < 2 else 1


def layer_row(field, layer):
    return 4 * field + layer if field < 2 else 8 + 3 * (field - 2) + layer - 1


def bands_kernel(iterate, source, wave, x_out, z_out, corner_out, x_part, z_part, sems):
    fields = [iterate.at[0], iterate.at[1], source.at[0], source.at[1], wave]
    copies = [
        pltpu.make_async_copy(ref.at[pl.ds(CX - BAND, BAND)], x_part.at[f], sems.at[f])
        for f, ref in enumerate(fields)
    ]
    for f, ref in enumerate(fields):
        for piece in range(2):
            some = pl.ds(CX // 2 * piece, CX // 2)
            copies.append(
                pltpu.make_async_copy(
                    ref.at[some, pl.ds(CZ - 8, 8)], z_part.at[f, some], sems.at[5 + 2 * f + piece]
                )
            )
    for copy in copies:
        copy.start()
    for copy in copies:
        copy.wait()
    corner_out[...] = jnp.zeros_like(corner_out)
    for field in range(5):
        first = layers(field)
        depth = BAND - first
        for layer in range(first, BAND):
            row = layer_row(field, layer)
            x_out[row] = x_part[field, layer]
            corner_out[pl.ds(BAND * row, BAND), :] = x_part[field, layer, pl.ds(CZ - BAND, BAND), :]
        for x in range(CX):
            rows = pl.ds(LAYERS * x + layer_row(field, first), depth)
            z_out[rows, :] = z_part[field, x, pl.ds(8 - depth, depth), :]


def tile_of(fields, bands, corner_tiles, field, plane, tile, keep_x):
    if tile == 0:
        return corner_tiles[field, plane]
    rows = pl.ds(8 * (tile - 1), 8)
    if plane < BAND:
        if plane < layers(field):
            return jnp.zeros((8, LANES), jnp.float32)
        return bands[layer_row(field, plane), rows, :] * keep_x
    ref, index = fields[field]
    x = plane - BAND
    return ref[x, rows, :] if index is None else ref[index, x, rows, :]


def fill_low_tiles(low, z_band, corner, keep_x, keep_z, count=5):
    keep_both = keep_x * keep_z
    low[...] = jnp.zeros_like(low)
    for field in range(count):
        first = layers(field)
        depth = BAND - first
        for plane in range(EXT):
            to = pl.ds(8 - depth, depth)
            if plane >= BAND:
                rows = pl.ds(LAYERS * (plane - BAND) + layer_row(field, first), depth)
                low[field, plane, to, :] = z_band[rows, :] * keep_z
            elif plane >= first:
                rows = pl.ds(BAND * layer_row(field, plane) + first, depth)
                low[field, plane, to, :] = corner[rows, :] * keep_both


def own_layout(half):
    return OVER + (HALO - OVER) * half, HALO * half, OVER


def other_layout(half):
    return HALO - (HALO - OVER) * half, OVER * half, HALO


def join_lane(half):
    return OVER + (GROUP - 1 - 2 * OVER) * half


def pack(packed, values, layout):
    turn, least, count = layout
    lanes = lane_ids()
    place = lanes % GROUP
    wanted = (place >= least) & (place < least + count)
    turned = [(j, pltpu.roll(v, lax.rem(GROUP * j + turn, LANES), 1)) for j, v in values]
    for j, value in turned:
        packed = jnp.where(wanted & (lanes // GROUP == j), value, packed)
    return packed


def inner_halo_kernel(info, iterate, source, wave, theirs, mine, movers):
    half = info[0]
    lane = lax.broadcasted_iota(jnp.int32, (16, 2 * LANES), 1)
    row = lax.broadcasted_iota(jnp.int32, (16, 2 * LANES), 0)
    ends = lane % LANES == (LANES - 1) * (1 - half)
    for m in range(MOVERS):
        start = GROUP * (2 * m + lane // LANES) + join_lane(half)
        for first in range(0, 2 * LANES, 16):
            hit = ends & ((row + first) % LANES == start)
            movers[m, pl.ds(first, 16), :] = hit.astype(jnp.float32).astype(jnp.bfloat16)
    fields = [(iterate, 0), (iterate, 1), (source, 0), (source, 1), (wave, None)]
    zeros = jnp.zeros((8, LANES), jnp.float32)
    for field in range(5):
        for start in range(STRIDE):
            for tile in range(1, 4):
                values = [
                    (j, tile_of(fields, None, None, field, STRIDE * j + start, tile, None))
                    for j in range(1, PER)
                ]
                at = pl.ds(8 * tile, 8)
                theirs[field, start, at, :] = pack(zeros, values, other_layout(half))
                mine[field, start, at, :] = pack(zeros, values, own_layout(half))


def pack_bands(inner, out, low, x_band, keep_x, layout):
    for field in range(5):
        for start in range(STRIDE):
            values = [(j, low[field, STRIDE * j + start]) for j in range(PER)]
            zeros = jnp.zeros((8, LANES), jnp.float32)
            out[field, start, pl.ds(0, 8), :] = pack(zeros, values, layout)
            for tile in range(1, 4):
                at = pl.ds(8 * tile, 8)
                packed = inner[field, start, at, :]
                if start >= layers(field):
                    value = x_band[layer_row(field, start), pl.ds(8 * (tile - 1), 8), :] * keep_x
                    packed = pack(packed, [(0, value)], layout)
                out[field, start, at, :] = packed


def halo_kernel(info, inner, x_band, z_band, corner, out, low):
    keep = flags(info, 4)
    fill_low_tiles(low, z_band, corner, keep[0], keep[1])
    pack_bands(inner, out, low, x_band, keep[0], other_layout(info[0]))


def coefficients(wave_sq, s_re, s_im, sigma):
    diag = 5.0 - wave_sq
    scale = (0.5 * OMEGA) / (diag * diag + sigma * sigma)
    er = diag * scale
    ei = -sigma * scale
    return er, ei, 2.0 * (er * s_re - ei * s_im), 2.0 * (er * s_im + ei * s_re)


def sigma_z(tile, flag):
    if tile == 0:
        return jnp.zeros((8, LANES), jnp.float32)
    z = (row_ids() + 8 * (tile - 1)).astype(jnp.float32)
    ramp = jnp.maximum(z - (CZ - PML) + 1.0, 0.0) / PML
    return SIGMA * ramp * ramp * flag


def weights_kernel(
    info, iterate, source, wave, inner, x_band, z_band, corner,
    e_re, e_im, f_re, f_im, mine, low,
):
    keep = flags(info, 4)
    half = info[0]
    keep_x = keep[0]
    fill_low_tiles(low, z_band, corner, keep_x, keep[1])
    pack_bands(inner, mine, low, x_band, keep_x, own_layout(half))
    fields = [(iterate, 0), (iterate, 1), (source, 0), (source, 1), (wave, None)]
    zeros = jnp.zeros((8, LANES), jnp.float32)
    kept_rows = row_ids() < 5
    for tile in range(4):
        along_z = sigma_z(tile, keep[3])
        at = pl.ds(8 * tile, 8)
        for plane in range(EXT):
            values = [tile_of(fields, x_band, low, f, plane, tile, keep_x) for f in range(5)]
            w_re, w_im, s_re, s_im, wave_sq = values
            if plane == 0:
                er, ei, fr, fi = zeros, zeros, OMEGA * w_re, OMEGA * w_im
            else:
                ramp = max(plane - BAND - (CX - PML) + 1.0, 0.0) / PML
                sigma = along_z + SIGMA * ramp * ramp * keep[2]
                er, ei, fr, fi = coefficients(wave_sq, s_re, s_im, sigma)
                if tile == 0:
                    er = jnp.where(kept_rows, 0.0, er)
                    ei = jnp.where(kept_rows, 0.0, ei)
                    fr = jnp.where(kept_rows, OMEGA * w_re, fr)
                    fi = jnp.where(kept_rows, OMEGA * w_im, fi)
            e_re[plane, at, :] = er
            e_im[plane, at, :] = ei
            f_re[plane, at, :] = fr
            f_im[plane, at, :] = fi


def relax_kernel(
    info, iterate, x_band, z_band, corner, e_re, e_im, f_re, f_im, movers, mine, halo,
    own, beside, x_a, x_b, z_first, z_last,
    low, w, h, he_re, he_im, hf_re, hf_im, hq, hr, hs, mq, mr, sides,
):
    keep = flags(info, 4)
    half = info[0]
    active = info[1]
    odd = info[2]

    @pl.when(active == 0)
    def _():
        own[...] = iterate[...]
        beside[...] = halo[pl.ds(0, 2)]

    @pl.when(active == 1)
    def _():
        keep_x = keep[0]
        fill_low_tiles(low, z_band, corner, keep_x, keep[1], 2)
        fields = [(iterate, 0), (iterate, 1)]
        lanes = lane_ids()
        rows = row_ids()
        place = lanes % GROUP
        group = lanes // GROUP
        turn, least, count = own_layout(half)
        repeated = (place >= least) & (place < least + count)
        zeros = jnp.zeros((8, LANES), jnp.float32)
        for scratch in (w, h):
            scratch[...] = jnp.zeros_like(scratch)

        for tile in range(4):
            along_z = sigma_z(tile, keep[3])
            kept_rows = rows < 5
            at, inner = pl.ds(8 * tile, 8), pl.ds(8 + 8 * tile, 8)
            for plane in range(EXT):
                for part in range(2):
                    value = tile_of(fields, x_band, low, part, plane, tile, keep_x)
                    w[part, plane + 1, inner, :] = value
            for start in range(STRIDE):
                w_re, w_im, s_re, s_im, wave_sq = [
                    jnp.where(repeated, mine[f, start, at, :], halo[f, start, at, :])
                    for f in range(5)
                ]
                h[0, start, inner, :] = w_re
                h[1, start, inner, :] = w_im
                x = (STRIDE * group + start - BAND).astype(jnp.float32)
                ramp = jnp.maximum(x - (CX - PML) + 1.0, 0.0) / PML
                sigma = along_z + SIGMA * ramp * ramp * keep[2]
                er, ei, fr, fi = coefficients(wave_sq, s_re, s_im, sigma)
                kept = group == PER
                if start == 0:
                    kept = kept | (group == 0)
                if tile == 0:
                    kept = kept | kept_rows
                he_re[start, at, :] = jnp.where(kept, 0.0, er)
                he_im[start, at, :] = jnp.where(kept, 0.0, ei)
                hf_re[start, at, :] = jnp.where(kept, OMEGA * w_re, fr)
                hf_im[start, at, :] = jnp.where(kept, OMEGA * w_im, fi)

        first_lane = lanes == 0
        last_lane = lanes == LANES - 1
        def undamped(plane, tile):
            return plane < BAND + CX - PML and tile < 3

        def updated(w_re, w_im, t_re, t_im, er, ei, fr, fi):
            new_re = (1.0 - OMEGA) * w_re + fr
            new_im = (1.0 - OMEGA) * w_im + fi
            if ei is None:
                return new_re + er * t_re, new_im + er * t_im
            return new_re + (er * t_re - ei * t_im), new_im + (er * t_im + ei * t_re)

        def sweep():
            first = 1
            def centre_and_z(ref, part, plane, tile):
                base = 8 + 8 * tile
                return ref[part, plane, pl.ds(base, 8), :], (
                    ref[part, plane, pl.ds(base - 1, 8), :]
                    + ref[part, plane, pl.ds(base + 1, 8), :]
                )

            for tile in range(4):
                at = pl.ds(8 * tile, 8)
                for part in range(2):
                    both = [centre_and_z(h, part, s, tile) for s in range(STRIDE)]
                    below = [roll(value, GROUP) for value in both[-1]]
                    above = [roll(value, -GROUP) for value in both[0]]
                    both = [below] + both + [above]
                    for s in range(STRIDE):
                        q, near = stencil_parts(
                            both[s + 1][0], both[s][0] + both[s + 2][0],
                            both[s + 1][1], both[s][1] + both[s + 2][1],
                        )
                        hq[part, s, at, :] = q
                        hs[pl.ds(32 * (STRIDE * part + s) + 8 * tile, 8), :] = q
                        hr[part, s, at, :] = near

            value = hs[...]
            head = value.astype(jnp.bfloat16)
            tail = (value - head.astype(jnp.float32)).astype(jnp.bfloat16)
            both = jnp.concatenate([head, tail], 1)
            for m in range(MOVERS):
                moved = jnp.dot(both, movers[m], preferred_element_type=jnp.float32)
                sides[2 * m] = moved[:, :LANES]
                if 2 * m + 1 < PER:
                    sides[2 * m + 1] = moved[:, LANES:]

            for tile in range(4):
                at = pl.ds(8 * tile, 8)
                for part in range(2):
                    before = centre_and_z(w, part, first, tile)
                    here = centre_and_z(w, part, first + 1, tile)
                    for plane in range(first, EXT):
                        after = (zeros, zeros)
                        if plane + 1 < EXT:
                            after = centre_and_z(w, part, plane + 2, tile)
                        q, near = stencil_parts(
                            here[0], before[0] + after[0], here[1], before[1] + after[1]
                        )
                        mq[part, plane, at, :] = q
                        mr[part, plane, at, :] = near
                        before, here = here, after

            for tile in range(4):
                at = pl.ds(8 * tile, 8)
                base = 8 + 8 * tile
                for j in range(PER):
                    planes = range(max(STRIDE * j, first), STRIDE * (j + 1))
                    q = [[mq[part, plane, at, :] for part in range(2)] for plane in planes]
                    up = [[roll(value, -1) for value in pair] for pair in q]
                    down = [[roll(value, 1) for value in pair] for pair in q]
                    side = [
                        [
                            sides[j, pl.ds(32 * (STRIDE * part + plane % STRIDE) + 8 * tile, 8), :]
                            for part in range(2)
                        ]
                        for plane in planes
                    ]
                    for n, plane in enumerate(planes):
                        total = [
                            jnp.where(last_lane, side[n][part], up[n][part])
                            + jnp.where(first_lane, side[n][part], down[n][part])
                            + mr[part, plane, at, :]
                            for part in range(2)
                        ]
                        new_re, new_im = updated(
                            w[0, plane + 1, pl.ds(base, 8), :], w[1, plane + 1, pl.ds(base, 8), :],
                            total[0], total[1],
                            e_re[plane, at, :], None if undamped(plane, tile) else e_im[plane, at, :],
                            f_re[plane, at, :], f_im[plane, at, :],
                        )
                        w[0, plane + 1, pl.ds(base, 8), :] = new_re
                        w[1, plane + 1, pl.ds(base, 8), :] = new_im

            for tile in range(4):
                at = pl.ds(8 * tile, 8)
                base = 8 + 8 * tile
                total = [
                    [pair_sum(hq[part, s, at, :]) + hr[part, s, at, :] for part in range(2)]
                    for s in range(STRIDE)
                ]
                for s in range(STRIDE):
                    new_re, new_im = updated(
                        h[0, s, pl.ds(base, 8), :], h[1, s, pl.ds(base, 8), :],
                        total[s][0], total[s][1],
                        he_re[s, at, :], he_im[s, at, :],
                        hf_re[s, at, :], hf_im[s, at, :],
                    )
                    h[0, s, pl.ds(base, 8), :] = new_re
                    h[1, s, pl.ds(base, 8), :] = new_im

        def renew():
            for tile in range(4):
                at = pl.ds(8 + 8 * tile, 8)
                for part in range(2):
                    for s in range(STRIDE):
                        values = [(j, w[part, STRIDE * j + s + 1, at, :]) for j in range(PER)]
                        h[part, s, at, :] = pack(h[part, s, at, :], values, own_layout(half))

        def one_sweep(turn, carry):
            sweep()

            @pl.when(turn == SWEEPS // 2 - 1)
            def _():
                renew()

            return carry

        lax.fori_loop(0, SWEEPS, one_sweep, 0)
        for part in range(2):
            for x in range(CX):
                own[part, x] = w[part, x + BAND + 1, pl.ds(16, CZ), :]
            for s in range(STRIDE):
                beside[part, s] = h[part, s, pl.ds(8, 32), :]

    place_in = lane_ids() // GROUP
    for face, side in ((x_a, 1 - odd), (x_b, odd)):
        turned = [
            pltpu.roll(
                beside[n // 3, (STRIDE - 1) * side, pl.ds(8 + 8 * (n % 3), 8), :],
                lax.rem(LANES + GROUP * (n - 1 - (PER - 2) * side), LANES),
                1,
            )
            for n in range(6)
        ]
        packed = turned[0]
        for n in range(1, 6):
            packed = jnp.where(place_in == n, turned[n], packed)
        face[pl.ds(HALO_ROW, 8), :] = packed

    for part in range(2):
        for face, side in ((x_a, 1 - odd), (x_b, odd)):
            face[pl.ds(CZ * part, CZ), :] = own[part, (CX - 1) * side]
        for face, z in ((z_first, 0), (z_last, CZ - 1)):
            face[part, pl.ds(24, 8), :] = jnp.zeros((8, LANES), jnp.float32)
            for x in range(CX):
                face[part, pl.ds(x + 1, 1), :] = own[part, x, pl.ds(z, 1), :]
            for s in range(STRIDE):
                face[part, pl.ds(SIDE_ROW + s, 1), :] = beside[part, s, pl.ds(8 + z, 1), :]


def face_kernel(info, z_first, z_last, x_a, x_b, a_out, b_out, first, last):
    keep = flags(info, 8)
    odd_x = info[2] == 1
    odd_z = info[3] == 1
    group = lax.broadcasted_iota(jnp.int32, (1, LANES), 1) // GROUP
    for face, out, z in ((z_first, first, 0), (z_last, last, CZ - 1)):
        out[...] = face[...]
        for part in range(2):
            rows = [pl.ds(CZ * part + z, 1), pl.ds(HALO_ROW + z % 8, 1)]
            a, b = [[ref[row, :] for row in rows] for ref in (x_a, x_b)]
            piece = 3 * part + z // 8
            low = [jnp.where(odd_x, a[n], b[n]) * keep[0] for n in range(2)]
            high = [jnp.where(odd_x, b[n], a[n]) * keep[1] for n in range(2)]
            out[part, pl.ds(0, 1), :] = low[0]
            out[part, pl.ds(CX + 1, 1), :] = high[0]
            for s, value, to, turn in (
                (STRIDE - 1, low[1], 0, -GROUP * piece), (0, high[1], 7, GROUP * (7 - piece))
            ):
                at = pl.ds(SIDE_ROW + s, 1)
                out[part, at, :] = jnp.where(group == to, roll(value, turn), face[part, at, :])
    a_out[...] = jnp.where(odd_z, first[...], last[...])
    b_out[...] = jnp.where(odd_z, last[...], first[...])


def residual_kernel(
    info, field, source, wave, beside, movers, x_a, x_b, z_a, z_b,
    out, total, box, sides, mq, mr, hs, moved_to, z_low, z_high,
):
    keep = flags(info, 8)
    odd_x = info[2] == 1
    odd_z = info[3] == 1
    z_low[...] = jnp.where(odd_z, z_a[...], z_b[...])
    z_high[...] = jnp.where(odd_z, z_b[...], z_a[...])

    def x_sides(rows):
        a, b = x_a[rows, :], x_b[rows, :]
        return jnp.where(odd_x, a, b) * keep[0], jnp.where(odd_x, b, a) * keep[1]

    lanes = lane_ids()
    group = lanes // GROUP
    zeros = jnp.zeros((8, LANES), jnp.float32)
    low_halo, high_halo = x_sides(pl.ds(HALO_ROW, 8))
    for part in range(2):
        low, high = x_sides(pl.ds(CZ * part, CZ))
        box[part, 0, pl.ds(8, CZ), :] = low
        box[part, CX + 1, pl.ds(8, CZ), :] = high
        for x in range(CX):
            box[part, x + 1, pl.ds(8, CZ), :] = field[part, x]
        for x in range(CX + 2):
            box[part, x, pl.ds(7, 1), :] = z_low[part, pl.ds(x, 1), :] * keep[2]
            box[part, x, pl.ds(8 + CZ, 1), :] = z_high[part, pl.ds(x, 1), :] * keep[3]
        for s in range(STRIDE):
            row = pl.ds(SIDE_ROW + s, 1)
            sides[part, s, pl.ds(7, 1), :] = z_low[part, row, :] * keep[2]
            sides[part, s, pl.ds(8 + CZ, 1), :] = z_high[part, row, :] * keep[3]
            for tile in range(3):
                value = beside[part, s, pl.ds(8 + 8 * tile, 8), :]
                piece = 3 * part + tile
                if s == STRIDE - 1:
                    value = jnp.where(group == 0, roll(low_halo, -GROUP * piece), value)
                if s == 0:
                    value = jnp.where(group == 7, roll(high_halo, GROUP * (7 - piece)), value)
                sides[part, s, pl.ds(8 + 8 * tile, 8), :] = value

    def centre_and_z(ref, part, plane, tile):
        base = 8 + 8 * tile
        return ref[part, plane, pl.ds(base, 8), :], (
            ref[part, plane, pl.ds(base - 1, 8), :] + ref[part, plane, pl.ds(base + 1, 8), :]
        )

    for part in range(2):
        for tile in range(3):
            at = pl.ds(8 * tile, 8)
            both = [centre_and_z(sides, part, s, tile) for s in range(STRIDE)]
            below = [roll(value, GROUP) for value in both[-1]]
            above = [roll(value, -GROUP) for value in both[0]]
            both = [below] + both + [above]
            for s in range(STRIDE):
                q, _ = stencil_parts(
                    both[s + 1][0], both[s][0] + both[s + 2][0],
                    both[s + 1][1], both[s][1] + both[s + 2][1],
                )
                hs[pl.ds(CZ * (STRIDE * part + s) + 8 * tile, 8), :] = q

    value = hs[...]
    head = value.astype(jnp.bfloat16)
    tail = (value - head.astype(jnp.float32)).astype(jnp.bfloat16)
    both = jnp.concatenate([head, tail], 1)
    for m in range(MOVERS):
        moved = jnp.dot(both, movers[m], preferred_element_type=jnp.float32)
        moved_to[2 * m] = moved[:, :LANES]
        if 2 * m + 1 < PER:
            moved_to[2 * m + 1] = moved[:, LANES:]

    for part in range(2):
        for tile in range(3):
            at = pl.ds(8 * tile, 8)
            before, here = centre_and_z(box, part, 0, tile), centre_and_z(box, part, 1, tile)
            for x in range(CX):
                after = centre_and_z(box, part, x + 2, tile)
                q, near = stencil_parts(
                    here[0], before[0] + after[0], here[1], before[1] + after[1]
                )
                mq[part, x, at, :] = q
                mr[part, x, at, :] = near
                before, here = here, after

    first_lane = lanes == 0
    last_lane = lanes == LANES - 1
    squares = [zeros] * 4
    for part in range(2):
        for tile in range(3):
            at = pl.ds(8 * tile, 8)
            for j in range(1, PER):
                planes = range(STRIDE * (j - 1), STRIDE * j)
                q = [mq[part, x, at, :] for x in planes]
                up = [roll(value, -1) for value in q]
                down = [roll(value, 1) for value in q]
                side = [
                    moved_to[j, pl.ds(CZ * (STRIDE * part + s) + 8 * tile, 8), :]
                    for s in range(STRIDE)
                ]
                for n, x in enumerate(planes):
                    y = jnp.where(last_lane, side[n], up[n]) + jnp.where(
                        first_lane, side[n], down[n]
                    )
                    gap = (
                        source[part, x, at, :]
                        - (5.0 - wave[x, at, :]) * field[part, x, at, :]
                        + 0.5 * (y + mr[part, x, at, :])
                    )
                    out[part, x, at, :] = gap
                    squares[n] = squares[n] + gap * gap
    total[...] = jnp.broadcast_to(jnp.sum(sum(squares[1:], squares[0])), total.shape)


def f32(*shape):
    return jax.ShapeDtypeStruct(shape, jnp.float32)


def ring(value, axis, by):
    size = lax.axis_size(axis)
    return lax.ppermute(value, axis, [(i, (i + by) % size) for i in range(size)])


def pairs(value, axis, first):
    size = lax.axis_size(axis)
    moves = []
    for i in range(first, size, 2):
        j = (i + 1) % size
        moves += [(i, j), (j, i)]
    return lax.ppermute(value, axis, moves)


def diagonal(value, by_x, by_z):
    size_x, size_z = lax.axis_size("gx"), lax.axis_size("gz")
    pairs = [
        (x * size_z + z, ((x + by_x) % size_x) * size_z + (z + by_z) % size_z)
        for x in range(size_x)
        for z in range(size_z)
    ]
    return lax.ppermute(value, ("gx", "gz"), pairs)


def swap(value):
    return lax.ppermute(value, "gy", [(0, 1), (1, 0)])


def on_device(source, iterate, wave_sq, front, pml_flags):
    size_x, size_z, size_y = lax.axis_size("gx"), lax.axis_size("gz"), lax.axis_size("gy")
    at_x, at_z, half = lax.axis_index("gx"), lax.axis_index("gz"), lax.axis_index("gy")
    active = (jnp.mod(at_x + at_z - front[0], size_z) == 0).astype(jnp.int32)
    flag_bits = pml_flags[0, 0]
    info = jnp.stack(
        [
            half, active, at_x % 2, at_z % 2,
            at_x > 0, at_z > 0, flag_bits % 2, flag_bits // 2 % 2,
            at_x > 0, at_x < size_x - 1, at_z > 0, at_z < size_z - 1,
        ]
    ).astype(jnp.int32)

    def call(kernel, outs, ins, name, scratch=(), place=VMEM, sems=0):
        scalars = sum(value.ndim == 1 for value in ins)
        return pl.pallas_call(
            kernel,
            out_shape=outs,
            in_specs=[SMEM] * scalars + [place] * (len(ins) - scalars),
            out_specs=jax.tree.map(lambda _: VMEM, outs),
            scratch_shapes=[pltpu.VMEM(shape, jnp.float32) for shape in scratch]
            + [pltpu.SemaphoreType.DMA((sems,))] * (sems > 0),
            compiler_params=pltpu.CompilerParams(vmem_limit_bytes=20 * MIB),
            name=name,
        )(*ins)

    x_band, z_band, corner = call(
        bands_kernel,
        (f32(LAYERS, CZ, LANES), f32(LAYERS * CX, LANES), f32(72, LANES)),
        [pltpu.with_memory_space_constraint(v, pltpu.HBM) for v in (iterate, source, wave_sq)],
        "bands",
        [(5, BAND, CZ, LANES), (5, CX, 8, LANES)],
        place=HBM,
        sems=15,
    )
    corner = diagonal(corner, 1, 1)
    x_band = ring(x_band, "gx", 1)
    z_band = ring(z_band, "gz", 1)
    low_tiles = (5, EXT, 8, LANES)
    packed = f32(5, STRIDE, 32, LANES)
    moves = jax.ShapeDtypeStruct((MOVERS, 2 * LANES, 2 * LANES), jnp.bfloat16)
    theirs, mine, movers = call(
        inner_halo_kernel, (packed, packed, moves), (info, iterate, source, wave_sq), "pack_inner"
    )
    halo = call(
        halo_kernel,
        packed,
        (info, theirs, x_band, z_band, corner),
        "pack_halo",
        [low_tiles],
    )
    halo = swap(halo)
    planes, packs = (EXT, 32, LANES), (STRIDE, 32, LANES)
    own = (2, CX, CZ, LANES)
    in_vmem = pltpu.VMEM(own, jnp.float32)
    box_like, pack_like = (2, EXT + 2, 48, LANES), (2, STRIDE, 48, LANES)
    x_face, z_face = f32(HALO_ROW + 8, LANES), f32(2, 32, LANES)
    *weights, mine = call(
        weights_kernel,
        (f32(*planes),) * 4 + (packed,),
        (info, iterate, source, wave_sq, mine, x_band, z_band, corner),
        "weights",
        [low_tiles],
    )
    new, beside, x_a, x_b, z_first, z_last = call(
        relax_kernel,
        (in_vmem, f32(2, STRIDE, 32, LANES), x_face, x_face, z_face, z_face),
        (info, iterate, x_band, z_band, corner, *weights, movers, mine, halo),
        "relax",
        [(2,) + low_tiles[1:], box_like, pack_like]
        + [packs] * 4
        + [(2,) + packs] * 2
        + [(2 * STRIDE * 32, LANES)]
        + [(2,) + planes] * 2
        + [(PER, 2 * STRIDE * 32, LANES)],
    )
    x_a, x_b = pairs(x_a, "gx", 0), pairs(x_b, "gx", 1)
    z_a, z_b = call(
        face_kernel,
        (z_face, z_face),
        (info, z_first, z_last, x_a, x_b),
        "faces",
        [z_face.shape] * 2,
    )
    z_a, z_b = pairs(z_a, "gz", 0), pairs(z_b, "gz", 1)
    count = size_x * size_z * size_y
    residual, total = call(
        residual_kernel,
        (in_vmem, pltpu.VMEM((count, LANES), jnp.float32)),
        (info, new, source, wave_sq, beside, movers, x_a, x_b, z_a, z_b),
        "residual",
        [(2, CX + 2, 48, LANES), (2, STRIDE, 48, LANES), own, own]
        + [(2 * STRIDE * CZ, LANES), (PER, 2 * STRIDE * CZ, LANES)]
        + [z_face.shape] * 2,
    )
    parts = lax.all_to_all(total, ("gx", "gz", "gy"), 0, 0, tiled=True)
    cells = 2 * CX * CZ * LANES * count
    norm = jnp.sqrt(jnp.sum(parts, axis=0)[:1] / cells)
    return new, residual, norm


def solution(mesh):
    in_specs = (
        P(None, "gx", "gz", "gy"),
        P(None, "gx", "gz", "gy"),
        P("gx", "gz", "gy"),
        P(),
        P("gx", "gz"),
    )
    out_specs = (P(None, "gx", "gz", "gy"), P(None, "gx", "gz", "gy"), P())
    return jax.shard_map(
        on_device, mesh=mesh, in_specs=in_specs, out_specs=out_specs, check_vma=False
    )
```
